32 devices in a mesh: groups: 2 (over y), wide: 4 (over z), planes: 2 (over x), rep: 2 (over core).
Axes of the slice: x: 2, y: 2, z: 4, core: 2. Of those that a mesh axis runs over, the one named last changes fastest.
Arguments:
- movie_frames: bfloat16 [4, 128, 256, 128], P('planes', ('groups', 'wide'), 'rep'), parts along dimension 1, may hold values from -6 to 6
- pixel_mask: int32 [256, 128], P('rep'), may hold values 0 or 1
- tile_owner: int32 [256, 1], P('rep'), may hold values from 0 to 3; in each aligned block of 128 rows (0 to 127, 128 to 255, ...) at most 48 rows name the same one
- support: int32 [256, 128], P('rep'), may hold values from 0 to 511
- templates: bfloat16 [512, 4, 128], P(None, 'planes'), may hold values from -0.25 to 0.25
- row_taps: float32 [25], replicated, may hold values from -1.25 to 1.25
- col_taps: float32 [25], replicated, may hold values from -1.25 to 1.25
- lag_gains: float32 [4, 3, 65], P('wide'), may hold values from -0.4375 to 0.4375
- dilations: int32 [4, 3], P('wide'), may hold values from 1 to 8
Outputs:
- traces: bfloat16 [128, 128, 256], P('planes', ('groups', 'wide'), 'rep'), parts along dimension 1
- back_projected: bfloat16 [4, 128, 256, 128], P('planes', ('groups', 'wide'), 'rep'), parts along dimension 1
The draws below stay inside these ranges and needn't reach their ends.
There are 2 independent parts, one for each index of `groups`. The reference program is written for one: setup_inputs(seed, part) draws one part's arguments, and reference() takes and returns one part's arrays. A program takes and returns all parts, laid end to end along the dimension named above; an argument that names none is the same for every part. Nothing has to cross between parts.
Inputs may be any that keep to these rules, and one draw needn't show every extreme that they name: Strip h belongs to region class tile_owner[h,0]; the 128 rows of one device name each class at most 48 times.
All inputs are finite; a program needn't handle non-finite values. No bound on the sum of `pixel_mask` on one device may be relied on, other than what follows from the above.
Results may differ from the reference program's by a relative error of at most 0.015.
Values may be sent and summed in bfloat16 or wider, within the bound.
No kernel may reach another device: no remote copies, remote signals or barrier semaphores. Data moves between devices by JAX's collectives and lax.ppermute only.
A program may use at most 64 MiB of HBM per device.

```python
import math
import jax
import jax.numpy as jnp
import numpy as np
from jax import lax

H = 256
W = 128
FP = 128
NCOMP = 512
TAPS_S = 25
TAPS_T = 65
BANDS = 3
DMAX = 8
PLANES = 4
FRAMES = 64
HH = 128
CLUSTERS = 4
CAP = 48
N_REP = 2


def place_ends(entries, stream_key, least, high):
    longest = entries.shape.index(max(entries.shape))
    spots = []
    for shift in (0, 1):
        where = [jax.random.randint(jax.random.fold_in(stream_key, axis), (), 0, length) for axis, length in enumerate(entries.shape)]
        where[longest] = (where[longest] + shift) % entries.shape[longest]
        spots.append(tuple(where))
    return entries.at[spots[0]].set(least).at[spots[1]].set(high)


def level_of(key, shape, shards, smallest, top_value):
    def one(position, shards_of):
        draws = jax.random.uniform(jax.random.fold_in(jax.random.fold_in(key, 6), position), (shards_of,), jnp.float32, smallest / len(shards), top_value / len(shards))
        return jnp.repeat(jnp.exp(draws), shape[position] // shards_of).reshape((-1,) + (1,) * (len(shape) - position - 1))

    factor_of = one(*shards[0])
    for cut in shards[1:]:
        factor_of = factor_of * one(*cut)
    return factor_of


def deal_out(stream_key, own, number, rows, count, top, most, slope):
    sequence = jax.random.permutation(stream_key, count)
    packed, ordinary = load_shares(count, rows * top, most, slope, True), load_shares(count, rows * top, most, slope, False)
    places = jnp.arange(count)

    def named(tallies, offset_by):
        used = int((tallies > 0).sum())
        fixed = max(1, used // 4)
        passed = fixed + (places - fixed + offset_by * (used - fixed)) % max(1, count - fixed)
        return jnp.zeros((count,), jnp.int32).at[sequence[jnp.where(places < fixed, places, passed)]].set(jnp.asarray(tallies, jnp.int32))

    tallies = jnp.where(number % 4 == 0, named(packed, number // 4), named(ordinary, number - number // 4 - 1))
    mixed = jax.random.permutation(jax.random.fold_in(own, 3), count)
    donor, taker = mixed[0:count // 2 * 2:2], mixed[1:count // 2 * 2:2]
    room = jnp.minimum(tallies[donor] - 1, most - tallies[taker]) // 2
    room = jnp.where((donor == sequence[0]) | (taker == sequence[0]) | (tallies[taker] == 0), 0, jnp.maximum(room, 0))
    passed = jax.random.randint(jax.random.fold_in(own, 4), (count // 2,), 0, 1 << 20) % (room + 1)
    tallies = tallies.at[donor].add(-passed).at[taker].add(passed)
    items = jnp.searchsorted(jnp.cumsum(tallies), jnp.arange(rows * top), side="right").astype(jnp.int32)
    grid = items.reshape(top, rows).T
    grid = grid[jax.random.permutation(jax.random.fold_in(own, 1), rows)]
    offset_by = jax.random.randint(jax.random.fold_in(own, 2), (rows, 1), 0, top)
    return jnp.take_along_axis(grid, (jnp.arange(top)[None, :] + offset_by) % top, axis=1)


def load_shares(number_of, total, most, lean, full):
    weights = [(1 << 20) // math.isqrt(grade ** lean) + 1 for grade in range(1, number_of + 1)]
    largest = most if full else min(most, max(-(-total // number_of), total * weights[0] // sum(weights)))
    least = 1 if total - largest >= number_of - 1 else 0
    holding, spare = [largest] + [least] * (number_of - 1), total - largest - least * (number_of - 1)
    while spare > 0:
        free = [i for i in range(1, number_of) if holding[i] < largest] or [i for i in range(1, number_of) if holding[i] < most]
        pool, remaining = sum([weights[i] for i in free]), spare
        for i in free:
            addition = min(most - holding[i], max(1, remaining * weights[i] // pool), spare)
            holding[i] = holding[i] + addition
            spare = spare - addition
    return np.array(holding)


def normal_values(rng, extent, scale, reach, shards=(), held_as=jnp.bfloat16):
    values = scale * jax.random.normal(rng, extent, jnp.float32)
    if shards:
        values = values * level_of(rng, extent, shards, -0.22, 0.18)
    return jnp.clip(values, -reach, reach).astype(held_as)


def setup_inputs(seed: int = 0, part: int = 0) -> dict:
    key_list = jax.random.split(jax.random.key(seed), 10)
    own_keys = jax.random.split(jax.random.fold_in(key_list[9], part), 10)
    movie_frames = normal_values(own_keys[0], (PLANES, FRAMES, H, W), 1.0, 6.0, ((0, 2), (1, 4), (2, 2)))
    pixel_mask = place_ends((jax.random.randint(key_list[1], (H, W), 0, 4) < 3).astype(jnp.int32), jax.random.fold_in(key_list[1], 1), 0, 1)
    tile_owner_keys = jax.random.split(jax.random.fold_in(key_list[2], 1), H // HH)
    tile_owner_turns = jax.random.permutation(jax.random.fold_in(key_list[2], 3), H // HH)
    tile_owner = jax.vmap(lambda own, number: deal_out(jax.random.fold_in(key_list[2], 2), own, number, HH, CLUSTERS, 1, CAP, 2))(tile_owner_keys, tile_owner_turns).reshape((H, 1))
    support = place_ends(jax.random.randint(key_list[3], (H, FP), 0, NCOMP), jax.random.fold_in(key_list[3], 1), 0, NCOMP - 1).astype(jnp.int32)
    templates = normal_values(key_list[4], (NCOMP, PLANES, W), (PLANES * W) ** -0.5, 0.25, ((1, 2),))
    row_taps = normal_values(key_list[5], (TAPS_S,), TAPS_S ** -0.5, 1.25, (), jnp.float32)
    col_taps = normal_values(key_list[6], (TAPS_S,), TAPS_S ** -0.5, 1.25, (), jnp.float32)
    lag_gains = normal_values(key_list[7], (CLUSTERS, BANDS, TAPS_T), (BANDS * TAPS_T) ** -0.5, 0.4375, ((0, 4),), jnp.float32)
    dilations = place_ends(jax.random.randint(key_list[8], (CLUSTERS, BANDS), 1, DMAX + 1), jax.random.fold_in(key_list[8], 1), 1, DMAX).astype(jnp.int32)
    return {"movie_frames": movie_frames, "pixel_mask": pixel_mask, "tile_owner": tile_owner, "support": support, "templates": templates, "row_taps": row_taps, "col_taps": col_taps, "lag_gains": lag_gains, "dilations": dilations}


def band_matrix(tap_values, rows_in, rows_out, sign, offset):
    inner_idx = jnp.arange(rows_in, dtype=jnp.int32)[:, None]
    outer_idx = jnp.arange(rows_out, dtype=jnp.int32)[None, :]
    where_tap = sign * (inner_idx - outer_idx) + offset
    tap_index = jnp.arange(tap_values.shape[0], dtype=jnp.int32)
    picked_taps = where_tap[:, :, None] == tap_index[None, None, :]
    weights = jnp.where(picked_taps, tap_values[None, None, :], jnp.zeros((), tap_values.dtype))
    return jnp.sum(weights, axis=2).astype(jnp.bfloat16)


def lag_matrix(cluster_gains, cluster_lags, frame_count):
    tap_count = cluster_gains.shape[1]
    half_taps = (tap_count - 1) // 2
    lag_values = jnp.arange(2 * frame_count - 1, dtype=jnp.int32) - (frame_count - 1)
    tap_offsets = jnp.arange(tap_count, dtype=jnp.int32) - half_taps
    lag_hits = lag_values[None, :, None] == cluster_lags[:, None, None] * tap_offsets[None, None, :]
    spread = jnp.where(lag_hits, cluster_gains[:, None, :], jnp.zeros((), cluster_gains.dtype))
    kernel = jnp.sum(spread, axis=(0, 2))
    flipped = jnp.concatenate([kernel[::-1], jnp.zeros((1,), kernel.dtype)])
    tiled = jnp.broadcast_to(flipped, (frame_count, 2 * frame_count)).reshape(-1)
    tiled = tiled[: frame_count * (2 * frame_count - 1)].reshape(frame_count, 2 * frame_count - 1)
    return tiled[:, frame_count - 1:].astype(jnp.bfloat16)


def slot_table(owners, cluster_count, capacity):
    row_count = owners.shape[0]
    owner_marks = (owners[:, None] == jnp.arange(cluster_count, dtype=jnp.int32)[None, :]).astype(jnp.int32)
    before = jnp.cumsum(owner_marks, axis=0) - owner_marks
    slot_ranks = jnp.sum(before * owner_marks, axis=1)
    slot_of = owners * capacity + slot_ranks
    places = jnp.arange(cluster_count * capacity, dtype=jnp.int32)
    chosen = (slot_of[None, :] == places[:, None]).astype(jnp.int32)
    sources = jnp.sum(chosen * jnp.arange(row_count, dtype=jnp.int32)[None, :], axis=1)
    return slot_of, sources


def reference(movie_frames, pixel_mask, tile_owner, support, templates, row_taps, col_taps, lag_gains, dilations):
    plane_count, frame_count, row_count, col_count = movie_frames.shape
    half_rows = row_count // N_REP
    rim_width = (row_taps.shape[0] - 1) // 2
    col_fwd = band_matrix(col_taps, col_count, col_count, 1, rim_width)
    row_fwd = band_matrix(row_taps, row_count, row_count, 1, rim_width)
    col_adj = band_matrix(col_taps, col_count, col_count, -1, rim_width)
    row_adj = band_matrix(row_taps, row_count, row_count, -1, rim_width)
    mask_value = pixel_mask.astype(jnp.float32)

    def forward_plane(plane_frames):
        smooth = jnp.dot(plane_frames, col_fwd, preferred_element_type=jnp.float32).astype(jnp.bfloat16)
        along = jnp.einsum('thw,hg->tgw', smooth.astype(jnp.float32), row_fwd.astype(jnp.float32), precision=lax.Precision.HIGHEST)
        return (along * mask_value[None]).astype(jnp.bfloat16)

    filtered = lax.map(forward_plane, movie_frames)

    owner_halves = tile_owner[:, 0].reshape(N_REP, half_rows)
    slot_parts = []
    source_parts = []
    for half_index in range(N_REP):
        slot_of, sources = slot_table(owner_halves[half_index], CLUSTERS, CAP)
        slot_parts.append(slot_of)
        source_parts.append(sources + half_index * half_rows)
    picked_all = jnp.stack(source_parts).reshape(N_REP, CLUSTERS, CAP)
    picked_all = jnp.transpose(picked_all, (1, 0, 2)).reshape(CLUSTERS, N_REP * CAP).astype(jnp.int32)

    def per_cluster(inputs):
        cluster_gains, cluster_lags, picked = inputs
        lag_table = lag_matrix(cluster_gains, cluster_lags, frame_count)
        columns = jnp.take(filtered, picked, axis=2)
        mixed_cols = jnp.einsum('pscw,st->ptcw', columns.astype(jnp.float32), lag_table.astype(jnp.float32), precision=lax.Precision.HIGHEST).astype(jnp.bfloat16)
        shapes = jnp.take(templates, jnp.take(support, picked, axis=0), axis=0)
        scores = jnp.einsum('cjpw,ptcw->cjt', shapes.astype(jnp.float32), mixed_cols.astype(jnp.float32), precision=lax.Precision.HIGHEST)
        return jnp.maximum(scores, 0.0).astype(jnp.bfloat16)

    cluster_traces = lax.map(per_cluster, (lag_gains, dilations, picked_all))
    foot_count = cluster_traces.shape[2]
    flat_parts = []
    for half_index in range(N_REP):
        owners_here = owner_halves[half_index]
        slot_ranks = slot_parts[half_index] - owners_here * CAP
        flat_parts.append(owners_here * (N_REP * CAP) + half_index * CAP + slot_ranks)
    flat_index = jnp.concatenate(flat_parts).astype(jnp.int32)
    flat_traces = cluster_traces.reshape(CLUSTERS * N_REP * CAP, foot_count, frame_count)
    tile_traces = jnp.take(flat_traces, flat_index, axis=0)

    tile_shapes = jnp.take(templates, support, axis=0)
    plane_shapes = jnp.transpose(tile_shapes, (2, 0, 1, 3))
    trace_value = tile_traces.astype(jnp.float32)

    def backward_plane(inputs):
        plane_filtered, shape_plane = inputs
        model_part = jnp.einsum('hjw,hjt->thw', shape_plane.astype(jnp.float32), trace_value, precision=lax.Precision.HIGHEST)
        residual = (plane_filtered.astype(jnp.float32) - mask_value[None] * model_part).astype(jnp.bfloat16)
        back_rows = jnp.einsum('thw,hg->tgw', residual.astype(jnp.float32), row_adj.astype(jnp.float32), precision=lax.Precision.HIGHEST).astype(jnp.bfloat16)
        return jnp.dot(back_rows, col_adj, preferred_element_type=jnp.float32).astype(jnp.bfloat16)

    back_projected = lax.map(backward_plane, (filtered, plane_shapes))
    traces = jnp.transpose(tile_traces, (1, 2, 0))
    return traces, back_projected
```

```python
import functools

import jax
import jax.numpy as jnp
from jax import lax
from jax.experimental import pallas as pl
from jax.experimental.pallas import tpu as pltpu
from jax.sharding import PartitionSpec as P

BLOCK = 16
LANES = 128
F32 = jnp.float32
BF16 = jnp.bfloat16


def halo_pair(cells, axis, dim, width):
    count = lax.axis_size(axis)
    extent = cells.shape[dim]
    if count == 2:
        start = jnp.where(lax.axis_index(axis) == 0, extent - width, 0)
        edge = lax.dynamic_slice_in_dim(cells, start, width, axis=dim)
        other = lax.ppermute(edge, axis, [(0, 1), (1, 0)])
        return other, other
    head = lax.slice_in_dim(cells, 0, width, axis=dim)
    tail = lax.slice_in_dim(cells, extent - width, extent, axis=dim)
    above = lax.ppermute(tail, axis, [(i, i + 1) for i in range(count - 1)])
    below = lax.ppermute(head, axis, [(i + 1, i) for i in range(count - 1)])
    return above, below


def iota(shape, dim):
    return lax.broadcasted_iota(jnp.int32, shape, dim)


def column_band(lane_taps, rim):
    shape = (LANES, LANES)
    rolled = pltpu.roll(jnp.broadcast_to(lane_taps, shape), 0, 1, stride=1, stride_axis=0)
    gap = iota(shape, 1) - iota(shape, 0)
    return jnp.where(jnp.abs(gap) <= rim, rolled, 0.0).astype(BF16)


def row_band(lane_taps):
    rolled = pltpu.roll(
        jnp.broadcast_to(lane_taps, (BLOCK, LANES)), 0, 1, stride=1, stride_axis=0
    )
    return rolled[:, : 3 * BLOCK].astype(BF16)


def expand_forward(band, frames):
    out_rows, depth, span = BLOCK * frames, 3 * BLOCK * frames, 3 * BLOCK
    left = (iota((out_rows, BLOCK), 0) // frames == iota((out_rows, BLOCK), 1)).astype(BF16)
    right = (lax.rem(iota((span, depth), 1), span) == iota((span, depth), 0)).astype(BF16)
    wide_rows = jnp.dot(left, band, preferred_element_type=F32).astype(BF16)
    spread = jnp.dot(wide_rows, right, preferred_element_type=F32)
    start = iota((out_rows, depth), 1) - span * lax.rem(iota((out_rows, depth), 0), frames)
    return jnp.where((start >= 0) & (start < span), spread, 0.0).astype(BF16)


def expand_adjoint(band, frames):
    out_rows, depth, span = BLOCK * frames, 3 * BLOCK * frames, 3 * BLOCK
    left = (lax.rem(iota((out_rows, BLOCK), 0), BLOCK) == iota((out_rows, BLOCK), 1)).astype(BF16)
    right = (iota((span, depth), 1) // frames == iota((span, depth), 0)).astype(BF16)
    wide_rows = jnp.dot(left, band, preferred_element_type=F32).astype(BF16)
    spread = jnp.dot(wide_rows, right, preferred_element_type=F32)
    same = lax.rem(iota((out_rows, depth), 1), frames) == iota((out_rows, depth), 0) // BLOCK
    return jnp.where(same, spread, 0.0).astype(BF16)


def per_frame(rows, frames, copies):
    tall = jnp.broadcast_to(rows[:, None, :], (BLOCK, frames, LANES)).reshape(BLOCK * frames, LANES)
    return tall if copies == 1 else jnp.concatenate([tall] * copies, axis=1)


def forward_kernel(
    rim, ends_ref, movie_ref, above_ref, below_ref, col_ref, row_ref, mask_ref, support_ref,
    templates_ref, filtered_ref, projected_ref, smooth_ref,
):
    planes, frames, rows, _ = movie_ref.shape
    col_fwd = column_band(col_ref[...], rim)
    row_fwd = expand_forward(row_band(row_ref[...]), frames)
    for p in range(planes):
        lanes = slice(p * LANES, (p + 1) * LANES)

        @pl.loop(0, frames)
        def _(f):
            smooth_ref[f, BLOCK : BLOCK + rows, lanes] = jnp.dot(
                movie_ref[p, f], col_fwd, preferred_element_type=F32
            ).astype(BF16)

        for ref, spot, flag in ((above_ref, 0, 0), (below_ref, BLOCK + rows, 1)):
            edge = jnp.dot(
                ref[p].reshape(frames * BLOCK, LANES), col_fwd, preferred_element_type=F32
            )
            edge = jnp.where(ends_ref[flag] > 0, edge, 0.0).astype(BF16)
            smooth_ref[:, spot : spot + BLOCK, lanes] = edge.reshape(frames, BLOCK, LANES)

    tiles = templates_ref.shape[0] // LANES

    @pl.loop(0, rows // BLOCK)
    def _(b):
        top = pl.multiple_of(b * BLOCK, BLOCK)
        near = smooth_ref[:, pl.ds(top, 3 * BLOCK), :].reshape(
            frames * 3 * BLOCK, planes * LANES
        )
        along = jnp.dot(row_fwd, near, preferred_element_type=F32)
        mask = per_frame(mask_ref[pl.ds(top, BLOCK), :].astype(F32), frames, planes)
        filtered = (along * mask).astype(BF16)
        out_rows = pl.ds(pl.multiple_of(top * frames, BLOCK * frames), BLOCK * frames)
        filtered_ref[out_rows, :] = filtered
        dense = lax.dot_general(
            filtered, templates_ref[...], (((1,), (1,)), ((), ())), preferred_element_type=F32
        )
        picked = per_frame(support_ref[pl.ds(top, BLOCK), :], frames, 1)
        lane, tile = picked & (LANES - 1), picked // LANES
        chosen = jnp.zeros(picked.shape, F32)
        for t in range(tiles):
            found = jnp.take_along_axis(
                dense[:, t * LANES : (t + 1) * LANES], lane, axis=1, mode="promise_in_bounds"
            )
            chosen = jnp.where(tile == t, found, chosen)
        projected_ref[out_rows, :] = chosen.astype(BF16)


def mix_kernel(lag_ref, parts_ref, out_ref):
    planes, wide, rows, frames, lanes = parts_ref.shape

    @pl.loop(0, rows)
    def _(h):
        lag = lag_ref[h]
        total = None
        for p in range(planes):
            cells = parts_ref[p, :, h].reshape(wide * frames, lanes)
            term = jnp.dot(lag, cells, preferred_element_type=F32)
            total = term if total is None else total + term
        traces = jnp.maximum(total, 0.0).astype(BF16).reshape(wide, frames, lanes)
        for p in range(planes):
            out_ref[p, :, h] = traces


def shapes_kernel(support_ref, templates_ref, shapes_ref):
    pairs = shapes_ref.shape[0]
    count = templates_ref.shape[1]
    for i in range(pairs):
        both = jnp.concatenate(
            [support_ref[2 * i : 2 * i + 1, :], support_ref[2 * i + 1 : 2 * i + 2, :]], axis=1
        )
        hits = iota((count, 2 * LANES), 0) == jnp.broadcast_to(both, (count, 2 * LANES))
        shapes_ref[i] = jnp.dot(
            templates_ref[...], hits.astype(BF16), preferred_element_type=F32
        ).astype(BF16)


def residual_kernel(traces_ref, shapes_ref, filtered_ref, mask_ref, out_ref):
    rows, frames, lanes = traces_ref.shape
    copies = filtered_ref.shape[1] // LANES
    mask = mask_ref[...].astype(F32)
    for h in range(rows):
        shape = shapes_ref[h // 2, :, (h % 2) * lanes : (h % 2 + 1) * lanes]
        model = lax.dot_general(
            traces_ref[h], shape, (((1,), (1,)), ((), ())), preferred_element_type=F32
        )
        row = jnp.concatenate([mask[h : h + 1, :]] * copies, axis=1)
        spot = slice(h * frames, (h + 1) * frames)
        out_ref[spot, :] = (filtered_ref[spot, :].astype(F32) - row * model).astype(BF16)


def backward_kernel(
    rim, ends_ref, resid_ref, above_ref, below_ref, col_ref, row_ref, out_ref, padded_ref
):
    planes, frames, rows, _ = out_ref.shape
    edge = BLOCK * frames
    col_adj = column_band(col_ref[...], rim)
    row_adj = expand_adjoint(row_band(row_ref[...]), frames)
    padded_ref[:edge, :] = jnp.where(ends_ref[0] > 0, above_ref[...], jnp.zeros_like(above_ref))
    padded_ref[edge : edge + rows * frames, :] = resid_ref[...]
    padded_ref[edge + rows * frames :, :] = jnp.where(
        ends_ref[1] > 0, below_ref[...], jnp.zeros_like(below_ref)
    )

    @pl.loop(0, rows // BLOCK)
    def _(b):
        near = padded_ref[pl.ds(pl.multiple_of(b * edge, edge), 3 * edge), :]
        back = jnp.dot(row_adj, near, preferred_element_type=F32).astype(BF16)
        top = pl.multiple_of(b * BLOCK, BLOCK)
        for p in range(planes):
            full = jnp.dot(
                back[:, p * LANES : (p + 1) * LANES], col_adj, preferred_element_type=F32
            ).astype(BF16)
            out_ref[p, :, pl.ds(top, BLOCK), :] = full.reshape(frames, BLOCK, LANES)


def vmem(count):
    return [pl.BlockSpec(memory_space=pltpu.VMEM)] * count


def params():
    return pltpu.CompilerParams(vmem_limit_bytes=48 * 1024 * 1024)


def lag_kernel_values(gains, lags, frame_count):
    taps = gains.shape[1]
    lag_values = jnp.arange(2 * frame_count - 1, dtype=jnp.int32) - (frame_count - 1)
    offsets = jnp.arange(taps, dtype=jnp.int32) - (taps - 1) // 2
    hits = lag_values[None, :, None] == lags[:, None, None] * offsets[None, None, :]
    spread = jnp.where(hits, gains[:, None, :], jnp.zeros((), gains.dtype))
    return jnp.sum(spread, axis=(0, 2)).astype(BF16)


def lag_tables(kernels, frame_count):
    rows = kernels.shape[0]
    ext = jnp.pad(kernels, ((0, 0), (0, 1)))
    flat = jnp.broadcast_to(ext[:, None, :], (rows, frame_count, 2 * frame_count))
    flat = flat.reshape(rows, -1)[:, : frame_count * (2 * frame_count - 1)]
    return flat.reshape(rows, frame_count, 2 * frame_count - 1)[:, :, frame_count - 1 :]


def on_device(
    movie_frames, pixel_mask, tile_owner, support, templates, row_taps, col_taps, lag_gains, dilations
):
    planes, frames, rows, cols = movie_frames.shape
    wide, plane_count = lax.axis_size("wide"), lax.axis_size("planes")
    rim = (row_taps.shape[0] - 1) // 2
    total_frames = frames * wide
    share = rows // (wide * plane_count)
    rep, rep_count = lax.axis_index("rep"), lax.axis_size("rep")
    ends = jnp.stack([rep > 0, rep < rep_count - 1]).astype(jnp.int32)
    smem = pl.BlockSpec(memory_space=pltpu.SMEM)

    def around(taps):
        row = jnp.zeros((1, LANES), F32)
        row = lax.dynamic_update_slice(row, taps[None, rim:], (0, 0))
        return lax.dynamic_update_slice(row, taps[None, :rim], (0, LANES - rim))

    def placed(taps):
        spot = BLOCK - rim
        return jnp.pad(taps[None, :], ((0, 0), (spot, LANES - spot - taps.shape[0])))

    above, below = halo_pair(movie_frames, "rep", 2, BLOCK)
    kernel_row = lag_kernel_values(lag_gains[0], dilations[0], total_frames)
    kernels = lax.all_gather(kernel_row, "wide", axis=0)
    flat_templates = templates.reshape(templates.shape[0], planes * cols)

    filtered, projected = pl.pallas_call(
        functools.partial(forward_kernel, rim),
        out_shape=(
            jax.ShapeDtypeStruct((rows * frames, planes * cols), BF16),
            jax.ShapeDtypeStruct((rows * frames, support.shape[1]), BF16),
        ),
        in_specs=[smem] + vmem(8),
        out_specs=tuple(vmem(2)),
        scratch_shapes=[pltpu.VMEM((frames, rows + 2 * BLOCK, planes * cols), BF16)],
        compiler_params=params(),
        cost_estimate=pl.CostEstimate(flops=1700000000, bytes_accessed=4000000, transcendentals=0),
        name="forward",
    )(
        ends, movie_frames, above, below, around(col_taps[::-1]), placed(row_taps), pixel_mask, support,
        flat_templates,
    )
    parts = lax.all_to_all(
        projected.reshape(rows, frames, -1), ("planes", "wide"), split_axis=0, concat_axis=0, tiled=True
    )
    parts = parts.reshape(plane_count, wide, share, frames, -1)

    late_support, late_templates, _ = lax.optimization_barrier((support, flat_templates, projected))
    pairs = rows // 2
    steps = 8
    shapes = pl.pallas_call(
        shapes_kernel,
        grid=(steps,),
        out_shape=jax.ShapeDtypeStruct((pairs, planes * cols, 2 * LANES), BF16),
        in_specs=[
            pl.BlockSpec((rows // steps, LANES), lambda i: (i, 0)),
            pl.BlockSpec((planes * cols, templates.shape[0]), lambda i: (0, 0)),
        ],
        out_specs=pl.BlockSpec((pairs // steps, planes * cols, 2 * LANES), lambda i: (i, 0, 0)),
        compiler_params=params(),
        cost_estimate=pl.CostEstimate(flops=4300000000, bytes_accessed=9000000, transcendentals=0),
        name="shapes",
    )(late_support, late_templates.T)

    here = lax.axis_index("planes") * wide + lax.axis_index("wide")
    owners = lax.dynamic_slice_in_dim(tile_owner[:, 0], here * share, share, 0)
    tables = lag_tables(jnp.take(kernels, owners, axis=0), total_frames)
    traces = pl.pallas_call(
        mix_kernel,
        out_shape=jax.ShapeDtypeStruct(parts.shape, BF16),
        in_specs=vmem(2),
        out_specs=vmem(1)[0],
        compiler_params=params(),
        cost_estimate=pl.CostEstimate(flops=40000000, bytes_accessed=1200000, transcendentals=0),
        name="mix",
    )(tables, parts)
    traces = lax.all_to_all(
        traces.reshape(rows, frames, -1), ("planes", "wide"), split_axis=0, concat_axis=0, tiled=True
    )

    step_rows = BLOCK
    residual = pl.pallas_call(
        residual_kernel,
        grid=(rows // step_rows,),
        out_shape=jax.ShapeDtypeStruct((rows * frames, planes * cols), BF16),
        in_specs=[
            pl.BlockSpec((step_rows, frames, LANES), lambda i: (i, 0, 0)),
            pl.BlockSpec((step_rows // 2, planes * cols, 2 * LANES), lambda i: (i, 0, 0)),
            pl.BlockSpec((step_rows * frames, planes * cols), lambda i: (i, 0)),
            pl.BlockSpec((step_rows, cols), lambda i: (i, 0)),
        ],
        out_specs=pl.BlockSpec((step_rows * frames, planes * cols), lambda i: (i, 0)),
        compiler_params=params(),
        cost_estimate=pl.CostEstimate(flops=140000000, bytes_accessed=10000000, transcendentals=0),
        name="residual",
    )(traces, shapes, filtered, pixel_mask)

    above_back, below_back = halo_pair(residual, "rep", 0, BLOCK * frames)
    foot_share = support.shape[1] // plane_count
    mine = lax.dynamic_slice_in_dim(traces, lax.axis_index("planes") * foot_share, foot_share, 2)
    trace_out = jnp.transpose(mine, (2, 1, 0))
    back_projected = pl.pallas_call(
        functools.partial(backward_kernel, rim),
        out_shape=jax.ShapeDtypeStruct(movie_frames.shape, BF16),
        in_specs=[smem] + vmem(5),
        out_specs=vmem(1)[0],
        scratch_shapes=[pltpu.VMEM(((rows + 2 * BLOCK) * frames, planes * cols), BF16)],
        compiler_params=params(),
        cost_estimate=pl.CostEstimate(flops=1000000000, bytes_accessed=3000000, transcendentals=0),
        name="backward",
    )(ends, residual, above_back, below_back, around(col_taps), placed(row_taps[::-1]))
    return trace_out, back_projected


def solution(mesh):
    return jax.shard_map(
        on_device,
        mesh=mesh,
        in_specs=(
            P("planes", ("groups", "wide"), "rep", None),
            P("rep", None),
            P("rep", None),
            P("rep", None),
            P(None, "planes", None),
            P(),
            P(),
            P("wide", None, None),
            P("wide", None),
        ),
        out_specs=(
            P("planes", ("groups", "wide"), "rep"),
            P("planes", ("groups", "wide"), "rep", None),
        ),
        check_vma=False,
    )
```

```python
import functools

import jax
import jax.numpy as jnp
from jax import lax
from jax.experimental import pallas as pl
from jax.experimental.pallas import tpu as pltpu
from jax.sharding import PartitionSpec as P

BLOCK = 16
LANES = 128
F32 = jnp.float32
BF16 = jnp.bfloat16
REP, PLANE, WIDE = 0, 1, 2


def exchange(cells, axis, flip):
    count = lax.axis_size(axis)
    return lax.ppermute(cells, axis, [(i, i ^ flip) for i in range(count)])


def iota(shape, dim):
    return lax.broadcasted_iota(jnp.int32, shape, dim)


def tap_row(taps_ref, place):
    lane = iota((8, LANES), 1)
    row = jnp.zeros((8, LANES), F32)
    for k in range(taps_ref.shape[0]):
        row = jnp.where(lane == place(k) % LANES, taps_ref[k], row)
    return row[:1]


def toeplitz(row, count, shift=0):
    return pltpu.roll(
        jnp.broadcast_to(row, (count, row.shape[1])), shift, 1, stride=1, stride_axis=0
    )


def column_band(taps_ref, rim, sign):
    rolled = toeplitz(tap_row(taps_ref, lambda k: sign * (k - rim)), LANES)
    gap = iota((LANES, LANES), 1) - iota((LANES, LANES), 0)
    return jnp.where(jnp.abs(gap) <= rim, rolled, 0.0).astype(BF16)


def row_band_forward(taps_ref, rim, frames):
    out_rows, depth, span = BLOCK * frames, 3 * BLOCK * frames, 3 * BLOCK
    band = toeplitz(tap_row(taps_ref, lambda k: k + BLOCK - rim), BLOCK)[:, :span].astype(BF16)
    left = (iota((out_rows, BLOCK), 0) // frames == iota((out_rows, BLOCK), 1)).astype(BF16)
    right = (lax.rem(iota((span, depth), 1), span) == iota((span, depth), 0)).astype(BF16)
    tall = jnp.dot(left, band, preferred_element_type=F32).astype(BF16)
    spread = jnp.dot(tall, right, preferred_element_type=F32)
    start = iota((out_rows, depth), 1) - span * lax.rem(iota((out_rows, depth), 0), frames)
    return jnp.where((start >= 0) & (start < span), spread, 0.0).astype(BF16)


def row_band_adjoint(taps_ref, rim, frames):
    out_rows, depth, span = BLOCK * frames, 3 * BLOCK * frames, 3 * BLOCK
    band = toeplitz(tap_row(taps_ref, lambda k: BLOCK + rim - k), BLOCK)[:, :span].astype(BF16)
    left = (lax.rem(iota((out_rows, BLOCK), 0), BLOCK) == iota((out_rows, BLOCK), 1)).astype(BF16)
    right = (iota((span, depth), 1) // frames == iota((span, depth), 0)).astype(BF16)
    tall = jnp.dot(left, band, preferred_element_type=F32).astype(BF16)
    spread = jnp.dot(tall, right, preferred_element_type=F32)
    same = lax.rem(iota((out_rows, depth), 1), frames) == iota((out_rows, depth), 0) // BLOCK
    return jnp.where(same, spread, 0.0).astype(BF16)


def per_frame(rows, frames, copies):
    tall = jnp.broadcast_to(rows[:, None, :], (BLOCK, frames, LANES)).reshape(BLOCK * frames, LANES)
    return tall if copies == 1 else jnp.concatenate([tall] * copies, axis=1)


def smooth_kernel(rim, frames, col_ref, row_ref, movie_ref, smooth_ref, col_fwd_ref, row_fwd_ref):
    @pl.when((pl.program_id(0) == 0) & (pl.program_id(1) == 0))
    def _():
        col_fwd_ref[...] = column_band(col_ref, rim, -1)
        row_fwd_ref[...] = row_band_forward(row_ref, rim, frames)

    _, some, rows, _ = movie_ref.shape
    full = jnp.dot(
        movie_ref[0].reshape(some * rows, LANES), col_fwd_ref[...], preferred_element_type=F32
    )
    smooth_ref[:, BLOCK : BLOCK + rows, :] = full.astype(BF16).reshape(some, rows, LANES)


def forward_kernel(
    flip, fill, place_ref, smooth_in_ref, edge_ref, col_fwd_ref, row_fwd_ref, code_ref,
    templates_ref, smooth_ref, filtered_ref, projected_ref,
):
    frames, padded_rows, width = smooth_ref.shape
    planes, rows = width // LANES, padded_rows - 2 * BLOCK
    if fill:
        for p in range(planes):
            edge = jnp.dot(
                edge_ref[p].reshape(frames * BLOCK, LANES), col_fwd_ref[...],
                preferred_element_type=F32,
            ).reshape(frames, BLOCK, LANES)
            lanes = slice(p * LANES, (p + 1) * LANES)
            above = jnp.where(place_ref[REP] > 0, edge, 0.0).astype(BF16)
            below = jnp.where(place_ref[REP] > 0, 0.0, edge).astype(BF16)
            smooth_ref[:, :BLOCK, lanes] = above
            smooth_ref[:, BLOCK + rows :, lanes] = below
    here = filtered_ref.shape[0] // frames
    first = (place_ref[PLANE] ^ flip) * here
    tiles = templates_ref.shape[1] // LANES
    for b in range(here // BLOCK):
        top = pl.multiple_of(first + b * BLOCK, BLOCK)
        near = smooth_ref[:, pl.ds(top, 3 * BLOCK), :].reshape(frames * 3 * BLOCK, width)
        along = jnp.dot(row_fwd_ref[...], near, preferred_element_type=F32)
        code = code_ref[pl.ds(top, BLOCK), :]
        mask = per_frame((code & 1).astype(F32), frames, planes)
        filtered = (along * mask).astype(BF16)
        spot = slice(b * BLOCK * frames, (b + 1) * BLOCK * frames)
        filtered_ref[spot, :] = filtered
        dense = jnp.dot(filtered, templates_ref[...], preferred_element_type=F32)
        picked = per_frame(code >> 1, frames, 1)
        lane, tile = picked & (LANES - 1), picked // LANES
        chosen = jnp.zeros(picked.shape, F32)
        for t in range(tiles):
            found = jnp.take_along_axis(
                dense[:, t * LANES : (t + 1) * LANES], lane, axis=1, mode="promise_in_bounds"
            )
            chosen = jnp.where(tile == t, found, chosen)
        projected_ref[spot, :] = chosen.astype(BF16)


def split_kernel(count, place_ref, lag_ref, *refs):
    parts, outs = refs[:count], refs[count:]
    rows = parts[0].shape[0] // len(outs)
    for k, out_ref in enumerate(outs):
        start = pl.multiple_of((place_ref[WIDE] ^ k) * rows, rows)
        total = parts[0][pl.ds(start, rows), :].astype(F32)
        for part in parts[1:]:
            total = total + part[pl.ds(start, rows), :].astype(F32)
        out_ref[:rows, :] = total.astype(BF16)
        out_ref[rows:, :] = lag_ref[...]


def mix_kernel(wide, place_ref, owner_ref, *refs):
    blocks, outs = refs[:wide], refs[wide : 2 * wide]
    cells_ref, kernels_ref, traces_ref, tables_ref = refs[2 * wide :]
    _, share, frames, lanes = cells_ref.shape
    total = wide * frames
    here = place_ref[WIDE]
    for k, block in enumerate(blocks):
        cells_ref[here ^ k] = block[: share * frames, :].reshape(share, frames, lanes)
        kernels_ref[here ^ k] = block[share * frames :, :].astype(F32)

    def table(values):
        row = jnp.concatenate([values[i : i + 1, :] for i in range(2 * total // LANES)], axis=1)
        return toeplitz(row, total, total + 1)[:, :total].astype(BF16)

    if wide <= share:
        for d in range(wide):
            tables_ref[d] = table(kernels_ref[d])
    first = (place_ref[PLANE] * wide + here) * share
    for h in range(share):
        owner = owner_ref[first + h]
        lag = tables_ref[owner] if wide <= share else table(kernels_ref[owner])
        mixed = jnp.dot(lag, cells_ref[:, h].reshape(total, lanes), preferred_element_type=F32)
        traces_ref[:, h] = jnp.maximum(mixed, 0.0).astype(BF16).reshape(wide, frames, lanes)
    for k, out_ref in enumerate(outs):
        out_ref[...] = traces_ref[here ^ k]


def shapes_kernel(
    rim, frames, col_ref, row_ref, code_ref, templates_ref, shapes_ref, col_adj_ref, row_adj_ref
):
    @pl.when(pl.program_id(0) == 0)
    def _():
        col_adj_ref[...] = column_band(col_ref, rim, 1)
        row_adj_ref[...] = row_band_adjoint(row_ref, rim, frames)

    count = templates_ref.shape[1]
    support = code_ref[...] >> 1
    for i in range(0, shapes_ref.shape[0], 2):
        both = jnp.concatenate([support[i : i + 1, :], support[i + 1 : i + 2, :]], axis=1)
        hits = iota((count, 2 * LANES), 0) == jnp.broadcast_to(both, (count, 2 * LANES))
        pair = jnp.dot(
            templates_ref[...], hits.astype(BF16), preferred_element_type=F32
        ).astype(BF16)
        shapes_ref[i] = pair[:, :LANES]
        shapes_ref[i + 1] = pair[:, LANES:]


def residual_kernel(
    flip, place_ref, traces_ref, shapes_ref, filtered_ref, code_ref, out_ref, edge_ref, ordered_ref
):
    wide, share, frames, lanes = traces_ref.shape
    copies = filtered_ref.shape[1] // LANES
    base = (place_ref[PLANE] ^ flip) * wide * share
    for k in range(wide):
        block = place_ref[WIDE] ^ k
        for h in range(share):
            row = block * share + h
            model = lax.dot_general(
                traces_ref[k, h], shapes_ref[base + row], (((1,), (1,)), ((), ())),
                preferred_element_type=F32,
            )
            mask = (code_ref[pl.ds(base + row, 1), :] & 1).astype(F32)
            spot = pl.ds(pl.multiple_of(row * frames, frames), frames)
            out_ref[spot, :] = (
                filtered_ref[spot, :].astype(F32) - jnp.concatenate([mask] * copies, axis=1) * model
            ).astype(BF16)
        ordered_ref[pl.ds(block * share, share)] = traces_ref[k]
    edge = edge_ref.shape[0]
    start = jnp.where(place_ref[REP] > 0, 0, out_ref.shape[0] - edge)
    edge_ref[...] = out_ref[pl.ds(pl.multiple_of(start, edge), edge), :]


def backward_kernel(count, place_ref, edge_ref, col_adj_ref, row_adj_ref, *refs):
    parts, (out_ref, padded_ref) = refs[:count], refs[count:]
    planes, frames, rows, _ = out_ref.shape
    edge, size = BLOCK * frames, parts[0].shape[0]
    zero = jnp.zeros_like(edge_ref)
    padded_ref[:edge, :] = jnp.where(place_ref[REP] > 0, edge_ref[...], zero)
    padded_ref[edge + rows * frames :, :] = jnp.where(place_ref[REP] > 0, zero, edge_ref[...])
    for flip, part in enumerate(parts):
        spot = pl.multiple_of(edge + (place_ref[PLANE] ^ flip) * size, edge)
        padded_ref[pl.ds(spot, size), :] = part[...]
    for b in range(rows // BLOCK):
        near = padded_ref[b * edge : (b + 3) * edge, :]
        back = jnp.dot(row_adj_ref[...], near, preferred_element_type=F32).astype(BF16)
        for p in range(planes):
            full = jnp.dot(
                back[:, p * LANES : (p + 1) * LANES], col_adj_ref[...], preferred_element_type=F32
            ).astype(BF16)
            out_ref[p, :, b * BLOCK : (b + 1) * BLOCK, :] = full.reshape(frames, BLOCK, LANES)


VMEM = pl.BlockSpec(memory_space=pltpu.VMEM)
SMEM = pl.BlockSpec(memory_space=pltpu.SMEM)


def shaped(shape):
    return jax.ShapeDtypeStruct(shape, BF16)


def call(kernel, name, outs, smem, vmem, flops, moved, scratch=(), aliases=None):
    return pl.pallas_call(
        kernel,
        out_shape=tuple(shaped(s) for s in outs),
        in_specs=[SMEM] * smem + [VMEM] * vmem,
        out_specs=(VMEM,) * len(outs),
        scratch_shapes=scratch,
        input_output_aliases=aliases or {},
        compiler_params=pltpu.CompilerParams(vmem_limit_bytes=32 * 1024 * 1024),
        cost_estimate=pl.CostEstimate(flops=flops, bytes_accessed=moved, transcendentals=0),
        name=name,
    )


def lag_kernel_values(gains, lags, frame_count):
    taps = gains.shape[1]
    lag_values = jnp.arange(2 * frame_count, dtype=jnp.int32) - (frame_count - 1)
    offsets = jnp.arange(taps, dtype=jnp.int32) - (taps - 1) // 2
    hits = lag_values[None, :, None] == lags[:, None, None] * offsets[None, None, :]
    spread = jnp.where(hits, gains[:, None, :], jnp.zeros((), gains.dtype))
    return jnp.sum(spread, axis=(0, 2)).astype(BF16)


def on_device(
    movie_frames, pixel_mask, tile_owner, support, templates, row_taps, col_taps, lag_gains, dilations
):
    planes, frames, rows, cols = movie_frames.shape
    wide, plane_count = lax.axis_size("wide"), lax.axis_size("planes")
    rim = (row_taps.shape[0] - 1) // 2
    total_frames, width = frames * wide, planes * cols
    here = rows // plane_count
    share = here // wide
    edge = BLOCK * frames
    rep, plane, spot = lax.axis_index("rep"), lax.axis_index("planes"), lax.axis_index("wide")
    place = jnp.stack([rep, plane, spot]).astype(jnp.int32)
    mib = 1 << 20

    start = jnp.where(rep == 0, rows - BLOCK, 0)
    rim_rows = exchange(lax.dynamic_slice_in_dim(movie_frames, start, BLOCK, axis=2), "rep", 1)
    code = support * 2 + pixel_mask
    tall_templates = jnp.transpose(templates, (1, 2, 0)).reshape(width, -1)
    kernel_row = lag_kernel_values(lag_gains[0], dilations[0], total_frames)
    lag_rows = -(-2 * total_frames // (LANES * BLOCK)) * BLOCK
    kernel_row = jnp.pad(kernel_row, (0, lag_rows * LANES - 2 * total_frames)).reshape(lag_rows, LANES)

    half = frames // 2
    depth = 3 * BLOCK * frames
    smooth, col_fwd, row_fwd = pl.pallas_call(
        functools.partial(smooth_kernel, rim, frames),
        grid=(2, planes),
        out_shape=(
            shaped((frames, rows + 2 * BLOCK, width)), shaped((cols, cols)), shaped((edge, depth))
        ),
        in_specs=[SMEM, SMEM, pl.BlockSpec((1, half, rows, cols), lambda i, p: (p, i, 0, 0))],
        out_specs=(
            pl.BlockSpec((half, rows + 2 * BLOCK, cols), lambda i, p: (i, 0, p)),
            pl.BlockSpec((cols, cols), lambda i, p: (0, 0)),
            pl.BlockSpec((edge, depth), lambda i, p: (0, 0)),
        ),
        compiler_params=pltpu.CompilerParams(vmem_limit_bytes=32 * 1024 * 1024),
        cost_estimate=pl.CostEstimate(flops=200000000, bytes_accessed=3 * mib, transcendentals=0),
        name="smooth",
    )(col_taps, row_taps, movie_frames)

    filtered, projected = [None] * plane_count, [None] * plane_count
    for turn in range(plane_count):
        flip = (turn + 1) % plane_count
        smooth, filtered[flip], mine = call(
            functools.partial(forward_kernel, flip, turn == 0), "forward",
            [smooth.shape, (here * frames, width), (here * frames, support.shape[1])],
            1, 6, 800000000, 3 * mib, aliases={1: 0},
        )(place, smooth, rim_rows, col_fwd, row_fwd, code, tall_templates)
        projected[flip] = exchange(mine, "planes", flip) if flip else mine

    block_rows = share * frames + lag_rows
    blocks = call(
        functools.partial(split_kernel, plane_count), "split", [(block_rows, LANES)] * wide,
        1, 1 + plane_count, 1000000, mib,
    )(place, kernel_row, *projected)
    blocks = [exchange(block, "wide", k) if k else block for k, block in enumerate(blocks)]

    late_code, late_templates, _ = lax.optimization_barrier((code, tall_templates, blocks[0]))
    steps = 8
    shapes, col_adj, row_adj = pl.pallas_call(
        functools.partial(shapes_kernel, rim, frames),
        grid=(steps,),
        out_shape=(shaped((rows, width, LANES)), shaped((cols, cols)), shaped((edge, depth))),
        in_specs=[
            SMEM,
            SMEM,
            pl.BlockSpec((rows // steps, LANES), lambda i: (i, 0)),
            pl.BlockSpec((width, templates.shape[0]), lambda i: (0, 0)),
        ],
        out_specs=(
            pl.BlockSpec((rows // steps, width, LANES), lambda i: (i, 0, 0)),
            pl.BlockSpec((cols, cols), lambda i: (0, 0)),
            pl.BlockSpec((edge, depth), lambda i: (0, 0)),
        ),
        compiler_params=pltpu.CompilerParams(vmem_limit_bytes=32 * 1024 * 1024),
        cost_estimate=pl.CostEstimate(flops=4300000000, bytes_accessed=9 * mib, transcendentals=0),
        name="shapes",
    )(col_taps, row_taps, late_code, late_templates)

    cell_shape = (wide, share, frames, LANES)
    tables = (wide, total_frames, total_frames) if wide <= share else (1, BLOCK, LANES)
    traces = call(
        functools.partial(mix_kernel, wide), "mix", [cell_shape[1:]] * wide, 2, wide, 20000000, mib,
        scratch=[
            pltpu.VMEM(cell_shape, BF16), pltpu.VMEM((wide, lag_rows, LANES), F32),
            pltpu.VMEM(cell_shape, BF16), pltpu.VMEM(tables, BF16),
        ],
    )(place, tile_owner[:, 0], *blocks)
    traces = jnp.stack([exchange(cells, "wide", k) if k else cells for k, cells in enumerate(traces)])

    residual, edges, ordered = [], [], []
    for flip in range(plane_count):
        got = exchange(traces, "planes", flip) if flip else traces
        part, tip, sorted_rows = call(
            functools.partial(residual_kernel, flip), "residual",
            [(here * frames, width), (edge, width), (here, frames, LANES)], 1, 4, 70000000, 6 * mib,
        )(place, got, shapes, filtered[flip], code)
        residual.append(part)
        edges.append(tip)
        ordered.append(sorted_rows)

    outer = plane ^ jnp.where(rep == 0, plane_count - 1, 0)
    tip = edges[0]
    for flip in range(1, plane_count):
        tip = jnp.where(outer == flip, edges[flip], tip)
    tip = exchange(tip, "rep", 1)

    foot_share = support.shape[1] // plane_count
    in_order = []
    for q in range(plane_count):
        rows_q = ordered[0]
        for flip in range(1, plane_count):
            rows_q = jnp.where(plane ^ q == flip, ordered[flip], rows_q)
        in_order.append(rows_q)
    mine = lax.dynamic_slice_in_dim(jnp.concatenate(in_order), plane * foot_share, foot_share, 2)
    trace_out = jnp.transpose(mine, (2, 1, 0))

    (back_projected,) = call(
        functools.partial(backward_kernel, plane_count), "backward", [movie_frames.shape],
        1, 3 + plane_count, 1000000000, 3 * mib,
        scratch=[pltpu.VMEM(((rows + 2 * BLOCK) * frames, width), BF16)],
    )(place, tip, col_adj, row_adj, *residual)
    return trace_out, back_projected


def solution(mesh):
    return jax.shard_map(
        on_device,
        mesh=mesh,
        in_specs=(
            P("planes", ("groups", "wide"), "rep", None),
            P("rep", None),
            P("rep", None),
            P("rep", None),
            P(None, "planes", None),
            P(),
            P(),
            P("wide", None, None),
            P("wide", None),
        ),
        out_specs=(
            P("planes", ("groups", "wide"), "rep"),
            P("planes", ("groups", "wide"), "rep", None),
        ),
        check_vma=False,
    )
```

```python
import functools

import jax
import jax.numpy as jnp
from jax import lax
from jax.experimental import pallas as pl
from jax.experimental.pallas import tpu as pltpu
from jax.sharding import PartitionSpec as P

BLOCK = 16
LANES = 128
F32 = jnp.float32
BF16 = jnp.bfloat16
REP, PLANE, WIDE = 0, 1, 2


def exchange(cells, axis, flip):
    count = lax.axis_size(axis)
    return lax.ppermute(cells, axis, [(i, i ^ flip) for i in range(count)])


def iota(shape, dim):
    return lax.broadcasted_iota(jnp.int32, shape, dim)


def tap_row(taps_ref, place):
    lane = iota((8, LANES), 1)
    row = jnp.zeros((8, LANES), F32)
    for k in range(taps_ref.shape[0]):
        row = jnp.where(lane == place(k) % LANES, taps_ref[k], row)
    return row[:1]


def toeplitz(row, count, shift=0):
    return pltpu.roll(
        jnp.broadcast_to(row, (count, row.shape[1])), shift, 1, stride=1, stride_axis=0
    )


def column_band(taps_ref, rim, sign):
    rolled = toeplitz(tap_row(taps_ref, lambda k: sign * (k - rim)), LANES)
    gap = iota((LANES, LANES), 1) - iota((LANES, LANES), 0)
    return jnp.where(jnp.abs(gap) <= rim, rolled, 0.0).astype(BF16)


def row_band_forward(taps_ref, rim, frames):
    out_rows, depth, span = BLOCK * frames, 3 * BLOCK * frames, 3 * BLOCK
    band = toeplitz(tap_row(taps_ref, lambda k: k + BLOCK - rim), BLOCK)[:, :span].astype(BF16)
    left = (iota((out_rows, BLOCK), 0) // frames == iota((out_rows, BLOCK), 1)).astype(BF16)
    right = (lax.rem(iota((span, depth), 1), span) == iota((span, depth), 0)).astype(BF16)
    tall = jnp.dot(left, band, preferred_element_type=F32).astype(BF16)
    spread = jnp.dot(tall, right, preferred_element_type=F32)
    start = iota((out_rows, depth), 1) - span * lax.rem(iota((out_rows, depth), 0), frames)
    return jnp.where((start >= 0) & (start < span), spread, 0.0).astype(BF16)


def row_band_adjoint(taps_ref, rim, frames):
    out_rows, depth, span = BLOCK * frames, 3 * BLOCK * frames, 3 * BLOCK
    band = toeplitz(tap_row(taps_ref, lambda k: BLOCK + rim - k), BLOCK)[:, :span].astype(BF16)
    left = (lax.rem(iota((out_rows, BLOCK), 0), BLOCK) == iota((out_rows, BLOCK), 1)).astype(BF16)
    right = (iota((span, depth), 1) // frames == iota((span, depth), 0)).astype(BF16)
    tall = jnp.dot(left, band, preferred_element_type=F32).astype(BF16)
    spread = jnp.dot(tall, right, preferred_element_type=F32)
    same = lax.rem(iota((out_rows, depth), 1), frames) == iota((out_rows, depth), 0) // BLOCK
    return jnp.where(same, spread, 0.0).astype(BF16)


def per_frame(rows, frames, copies):
    tall = jnp.broadcast_to(rows[:, None, :], (BLOCK, frames, LANES)).reshape(BLOCK * frames, LANES)
    return tall if copies == 1 else jnp.concatenate([tall] * copies, axis=1)


def prepare_kernel(
    rim, cuts, col_hbm, row_hbm, movie_hbm, mask_hbm, support_hbm, templates_hbm,
    smooth_ref, col_fwd_ref, row_fwd_ref, code_ref, templates_ref,
    movie_ref, mask_ref, support_ref, packed_ref, loose_ref, col_ref, row_ref, sems,
):
    planes, frames, rows, _ = movie_ref.shape
    some = frames // cuts

    def fetch(n, source, target):
        copy = pltpu.make_async_copy(source, target, sems.at[n])
        copy.start()
        return copy

    tap_copies = [fetch(0, col_hbm, col_ref), fetch(1, row_hbm, row_ref)]
    movie_copies = []
    for n in range(planes * cuts):
        piece = (n // cuts, pl.ds(n % cuts * some, some))
        movie_copies.append(fetch(5 + n, movie_hbm.at[piece], movie_ref.at[piece]))
    packed_copy = fetch(2, templates_hbm, packed_ref)
    code_copies = [fetch(3, mask_hbm, mask_ref), fetch(4, support_hbm, support_ref)]
    for copy in tap_copies:
        copy.wait()
    col_fwd = column_band(col_ref, rim, -1)
    col_fwd_ref[...] = col_fwd
    row_fwd_ref[...] = row_band_forward(row_ref, rim, frames)
    for n, copy in enumerate(movie_copies):
        p, first = n // cuts, n % cuts * some
        copy.wait()
        full = jnp.dot(
            movie_ref[p, first : first + some].reshape(some * rows, LANES), col_fwd,
            preferred_element_type=F32,
        )
        smooth_ref[first : first + some, BLOCK : BLOCK + rows, p * LANES : (p + 1) * LANES] = (
            full.astype(BF16).reshape(some, rows, LANES)
        )
    packed_copy.wait()
    loose_ref[...] = packed_ref[...].astype(F32)
    unit = (iota((LANES, LANES), 0) == iota((LANES, LANES), 1)).astype(BF16)
    for p in range(planes):
        shapes = loose_ref[pl.ds(p, templates_ref.shape[1], stride=planes), :].astype(BF16)
        templates_ref[p * LANES : (p + 1) * LANES, :] = lax.dot_general(
            unit, shapes, (((1,), (1,)), ((), ())), preferred_element_type=F32
        ).astype(BF16)
    for copy in code_copies:
        copy.wait()
    code_ref[...] = support_ref[...] * 2 + mask_ref[...]


def forward_kernel(
    flip, fill, place_ref, smooth_in_ref, edge_ref, col_fwd_ref, row_fwd_ref, code_ref,
    templates_ref, smooth_ref, filtered_ref, *refs
):
    outs, projected_ref = refs[:-1], refs[-1]
    frames, padded_rows, width = smooth_ref.shape
    planes, rows = width // LANES, padded_rows - 2 * BLOCK
    if fill:
        for p in range(planes):
            edge = jnp.dot(
                edge_ref[p].reshape(frames * BLOCK, LANES), col_fwd_ref[...],
                preferred_element_type=F32,
            ).reshape(frames, BLOCK, LANES)
            lanes = slice(p * LANES, (p + 1) * LANES)
            above = jnp.where(place_ref[REP] > 0, edge, 0.0).astype(BF16)
            below = jnp.where(place_ref[REP] > 0, 0.0, edge).astype(BF16)
            smooth_ref[:, :BLOCK, lanes] = above
            smooth_ref[:, BLOCK + rows :, lanes] = below
    here = filtered_ref.shape[0] // frames
    first = (place_ref[PLANE] ^ flip) * here
    tiles = templates_ref.shape[1] // LANES
    for b in range(here // BLOCK):
        top = pl.multiple_of(first + b * BLOCK, BLOCK)
        near = smooth_ref[:, pl.ds(top, 3 * BLOCK), :].reshape(frames * 3 * BLOCK, width)
        along = jnp.dot(row_fwd_ref[...], near, preferred_element_type=F32)
        code = code_ref[pl.ds(top, BLOCK), :]
        mask = per_frame((code & 1).astype(F32), frames, planes)
        filtered = (along * mask).astype(BF16)
        spot = slice(b * BLOCK * frames, (b + 1) * BLOCK * frames)
        filtered_ref[spot, :] = filtered
        dense = jnp.dot(filtered, templates_ref[...], preferred_element_type=F32)
        picked = per_frame(code >> 1, frames, 1)
        lane, tile = picked & (LANES - 1), picked // LANES
        chosen = jnp.zeros(picked.shape, F32)
        for t in range(tiles):
            found = jnp.take_along_axis(
                dense[:, t * LANES : (t + 1) * LANES], lane, axis=1, mode="promise_in_bounds"
            )
            chosen = jnp.where(tile == t, found, chosen)
        projected_ref[spot, :] = chosen.astype(BF16)
    size = outs[0].shape[0]
    for k, out_ref in enumerate(outs):
        start = pl.multiple_of((place_ref[WIDE] ^ k) * size, size)
        out_ref[...] = projected_ref[pl.ds(start, size), :]


def add_all(parts):
    total = parts[0][...].astype(F32)
    for part in parts[1:]:
        total = total + part[...].astype(F32)
    return total.astype(BF16)


def sum_kernel(lag_ref, *refs):
    parts, out_ref = refs[:-1], refs[-1]
    rows = parts[0].shape[0]
    out_ref[:rows, :] = add_all(parts)
    out_ref[rows:, :] = lag_ref[...]


def mix_kernel(wide, count, place_ref, owner_ref, lag_ref, *refs):
    parts, refs = refs[:count], refs[count:]
    blocks, outs = refs[: wide - 1], refs[wide - 1 : 2 * wide - 1]
    cells_ref, kernels_ref, traces_ref, tables_ref = refs[2 * wide - 1 :]
    _, share, frames, lanes = cells_ref.shape
    total = wide * frames
    here = place_ref[WIDE]
    cells_ref[here] = add_all(parts).reshape(share, frames, lanes)
    kernels_ref[here] = lag_ref[...].astype(F32)
    for k, block in enumerate(blocks, 1):
        cells_ref[here ^ k] = block[: share * frames, :].reshape(share, frames, lanes)
        kernels_ref[here ^ k] = block[share * frames :, :].astype(F32)

    def table(values):
        row = jnp.concatenate([values[i : i + 1, :] for i in range(2 * total // LANES)], axis=1)
        return toeplitz(row, total, total + 1)[:, :total].astype(BF16)

    if wide <= share:
        for d in range(wide):
            tables_ref[d] = table(kernels_ref[d])
    first = (place_ref[PLANE] * wide + here) * share
    for h in range(share):
        owner = owner_ref[first + h]
        lag = tables_ref[owner] if wide <= share else table(kernels_ref[owner])
        mixed = jnp.dot(lag, cells_ref[:, h].reshape(total, lanes), preferred_element_type=F32)
        traces_ref[:, h] = jnp.maximum(mixed, 0.0).astype(BF16).reshape(wide, frames, lanes)
    for k, out_ref in enumerate(outs):
        out_ref[...] = traces_ref[here ^ k]


def shapes_kernel(flip, rim, frames, place_ref, *refs):
    if rim:
        col_ref, row_ref, code_ref, templates_ref, shapes_ref, col_adj_ref, row_adj_ref = refs
        band = column_band(col_ref, rim, 1)
        planes = templates_ref.shape[0] // LANES
        col_adj_ref[...] = jnp.zeros_like(col_adj_ref)
        for p in range(planes):
            lanes = slice(p * LANES, (p + 1) * LANES)
            col_adj_ref[lanes, lanes] = band
        row_adj_ref[...] = row_band_adjoint(row_ref, rim, frames)
    else:
        code_ref, templates_ref, shapes_ref = refs
    count, here = templates_ref.shape[1], shapes_ref.shape[0]
    first = pl.multiple_of((place_ref[PLANE] ^ flip) * here, here)

    @pl.loop(0, here // 8)
    def _(g):
        support = code_ref[pl.ds(pl.multiple_of(first + g * 8, 8), 8), :] >> 1
        for i in range(0, 8, 2):
            both = jnp.concatenate([support[i : i + 1, :], support[i + 1 : i + 2, :]], axis=1)
            hits = iota((count, 2 * LANES), 0) == jnp.broadcast_to(both, (count, 2 * LANES))
            pair = jnp.dot(
                templates_ref[...], hits.astype(BF16), preferred_element_type=F32
            ).astype(BF16)
            shapes_ref[g * 8 + i] = pair[:, :LANES]
            shapes_ref[g * 8 + i + 1] = pair[:, LANES:]


def residual_kernel(
    flip, place_ref, shapes_ref, filtered_ref, code_ref, *refs
):
    traces, (out_ref, edge_ref, ordered_ref) = refs[:-3], refs[-3:]
    wide = len(traces)
    share, frames, lanes = traces[0].shape
    copies = filtered_ref.shape[1] // LANES
    base = (place_ref[PLANE] ^ flip) * wide * share
    for k in range(wide):
        block = place_ref[WIDE] ^ k
        for h in range(share):
            row = block * share + h
            model = lax.dot_general(
                traces[k][h], shapes_ref[row], (((1,), (1,)), ((), ())),
                preferred_element_type=F32,
            )
            mask = (code_ref[pl.ds(base + row, 1), :] & 1).astype(F32)
            spot = pl.ds(pl.multiple_of(row * frames, frames), frames)
            out_ref[spot, :] = (
                filtered_ref[spot, :].astype(F32) - jnp.concatenate([mask] * copies, axis=1) * model
            ).astype(BF16)
        ordered_ref[pl.ds(block * share, share)] = traces[k][...]
    edge = edge_ref.shape[0]
    start = jnp.where(place_ref[REP] > 0, 0, out_ref.shape[0] - edge)
    edge_ref[...] = out_ref[pl.ds(pl.multiple_of(start, edge), edge), :]


def backward_kernel(count, place_ref, edge_ref, col_adj_ref, row_adj_ref, *refs):
    parts, (out_hbm, padded_ref, out_ref, sems) = refs[:count], refs[count:]
    planes, frames, rows, _ = out_ref.shape
    edge, size = BLOCK * frames, parts[0].shape[0]
    zero = jnp.zeros_like(edge_ref)
    padded_ref[:edge, :] = jnp.where(place_ref[REP] > 0, edge_ref[...], zero)
    padded_ref[edge + rows * frames :, :] = jnp.where(place_ref[REP] > 0, zero, edge_ref[...])
    for flip, part in enumerate(parts):
        spot = pl.multiple_of(edge + (place_ref[PLANE] ^ flip) * size, edge)
        padded_ref[pl.ds(spot, size), :] = part[...]
    copies = []
    for b in range(rows // BLOCK):
        near = padded_ref[b * edge : (b + 3) * edge, :]
        back = jnp.dot(row_adj_ref[...], near, preferred_element_type=F32).astype(BF16)
        full = jnp.dot(back, col_adj_ref[...], preferred_element_type=F32).astype(BF16)
        piece = (slice(None), slice(None), pl.ds(b * BLOCK, BLOCK))
        for p in range(planes):
            out_ref[p, :, b * BLOCK : (b + 1) * BLOCK, :] = full[
                :, p * LANES : (p + 1) * LANES
            ].reshape(frames, BLOCK, LANES)
        copy = pltpu.make_async_copy(out_ref.at[piece], out_hbm.at[piece], sems.at[b])
        copy.start()
        copies.append(copy)
    for copy in copies:
        copy.wait()


VMEM = pl.BlockSpec(memory_space=pltpu.VMEM)
SMEM = pl.BlockSpec(memory_space=pltpu.SMEM)
HBM = pl.BlockSpec(memory_space=pltpu.HBM)


def shaped(shape):
    return jax.ShapeDtypeStruct(shape, BF16)


def call(kernel, name, outs, smem, vmem, flops, moved, scratch=(), aliases=None):
    return pl.pallas_call(
        kernel,
        out_shape=tuple(shaped(s) for s in outs),
        in_specs=[SMEM] * smem + [VMEM] * vmem,
        out_specs=(VMEM,) * len(outs),
        scratch_shapes=scratch,
        input_output_aliases=aliases or {},
        compiler_params=pltpu.CompilerParams(vmem_limit_bytes=32 * 1024 * 1024),
        cost_estimate=pl.CostEstimate(flops=flops, bytes_accessed=moved, transcendentals=0),
        name=name,
    )


def lag_kernel_values(gains, lags, frame_count):
    taps = gains.shape[1]
    lag_values = jnp.arange(2 * frame_count, dtype=jnp.int32) - (frame_count - 1)
    offsets = jnp.arange(taps, dtype=jnp.int32) - (taps - 1) // 2
    hits = lag_values[None, :, None] == lags[:, None, None] * offsets[None, None, :]
    spread = jnp.where(hits, gains[:, None, :], jnp.zeros((), gains.dtype))
    return jnp.sum(spread, axis=(0, 2)).astype(BF16)


def on_device(
    movie_frames, pixel_mask, tile_owner, support, templates, row_taps, col_taps, lag_gains, dilations
):
    planes, frames, rows, cols = movie_frames.shape
    wide, plane_count = lax.axis_size("wide"), lax.axis_size("planes")
    rim = (row_taps.shape[0] - 1) // 2
    total_frames, width = frames * wide, planes * cols
    here = rows // plane_count
    share = here // wide
    edge = BLOCK * frames
    rep, plane, spot = lax.axis_index("rep"), lax.axis_index("planes"), lax.axis_index("wide")
    place = jnp.stack([rep, plane, spot]).astype(jnp.int32)
    mib = 1 << 20

    start = jnp.where(rep == 0, rows - BLOCK, 0)
    rim_rows = exchange(lax.dynamic_slice_in_dim(movie_frames, start, BLOCK, axis=2), "rep", 1)
    cuts = 2
    depth, names = 3 * BLOCK * frames, templates.shape[0]
    smooth, col_fwd, row_fwd, code, tall_templates = pl.pallas_call(
        functools.partial(prepare_kernel, rim, cuts),
        out_shape=(
            shaped((frames, rows + 2 * BLOCK, width)), shaped((cols, cols)), shaped((edge, depth)),
            jax.ShapeDtypeStruct(support.shape, jnp.int32), shaped((width, names)),
        ),
        in_specs=[HBM] * 6,
        out_specs=(VMEM,) * 5,
        scratch_shapes=[
            pltpu.VMEM(movie_frames.shape, BF16),
            pltpu.VMEM(pixel_mask.shape, jnp.int32),
            pltpu.VMEM(support.shape, jnp.int32),
            pltpu.VMEM((names * planes, cols), BF16),
            pltpu.VMEM((names * planes, cols), F32),
            pltpu.SMEM(col_taps.shape, F32),
            pltpu.SMEM(row_taps.shape, F32),
            pltpu.SemaphoreType.DMA((5 + planes * cuts,)),
        ],
        compiler_params=pltpu.CompilerParams(vmem_limit_bytes=32 * mib),
        cost_estimate=pl.CostEstimate(flops=200000000, bytes_accessed=3 * mib, transcendentals=0),
        name="prepare",
    )(
        *[
            pltpu.with_memory_space_constraint(x, pltpu.HBM)
            for x in (
                col_taps, row_taps, movie_frames, pixel_mask, support,
                templates.reshape(names * planes, cols),
            )
        ]
    )

    order = list(range(wide // 2, wide)) + list(range(1, wide // 2)) + [0]
    filtered, projected = [None] * plane_count, [None] * plane_count
    for turn in range(plane_count):
        flip = (turn + 1) % plane_count
        smooth, filtered[flip], *mine = call(
            functools.partial(forward_kernel, flip, turn == 0), "forward",
            [smooth.shape, (here * frames, width)] + [(share * frames, LANES)] * wide,
            1, 6, 800000000, 3 * mib, aliases={1: 0},
            scratch=[pltpu.VMEM((here * frames, LANES), BF16)],
        )(place, smooth, rim_rows, col_fwd, row_fwd, code, tall_templates)
        projected[flip] = {k: exchange(mine[k], "planes", flip) if flip else mine[k] for k in order}
        if turn == 0:
            gains, lags, _ = lax.optimization_barrier((lag_gains[0], dilations[0], mine[0]))
            kernel_row = lag_kernel_values(gains, lags, total_frames)
            lag_rows = -(-2 * total_frames // (LANES * BLOCK)) * BLOCK
            kernel_row = jnp.pad(kernel_row, (0, lag_rows * LANES - 2 * total_frames))
            kernel_row = kernel_row.reshape(lag_rows, LANES)

    block_rows = share * frames + lag_rows
    sums, blocks = {}, {}
    for k in order[:-1]:
        (sums[k],) = call(
            sum_kernel, "sum", [(block_rows, LANES)], 0, 1 + plane_count, 100000, mib // 4
        )(kernel_row, *[part[k] for part in projected])
        blocks[k] = exchange(sums[k], "wide", k)

    def make_shapes(flip, after, bands):
        late_code, late_templates, _ = lax.optimization_barrier((code, tall_templates, after))
        outs = [(here, width, LANES)]
        taps = ()
        if bands:
            outs += [(width, width), (edge, depth)]
            taps = (col_taps, row_taps)
        return call(
            functools.partial(shapes_kernel, flip, rim if bands else 0, frames), "shapes",
            outs, 1 + len(taps), 2, 2150000000, 5 * mib,
        )(place, *taps, late_code, late_templates)

    shapes = [None] * plane_count
    shapes[0], col_adj, row_adj = make_shapes(0, [sums[k] for k in order[:-1]], True)
    first, col_adj = lax.optimization_barrier((projected[0][0], col_adj))

    cell_shape = (wide, share, frames, LANES)
    tables = (wide, total_frames, total_frames) if wide <= share else (1, BLOCK, LANES)
    traces = call(
        functools.partial(mix_kernel, wide, plane_count), "mix", [cell_shape[1:]] * wide,
        2, wide + plane_count, 20000000, mib,
        scratch=[
            pltpu.VMEM(cell_shape, BF16), pltpu.VMEM((wide, lag_rows, LANES), F32),
            pltpu.VMEM(cell_shape, BF16), pltpu.VMEM(tables, BF16),
        ],
    )(
        place, tile_owner[:, 0], kernel_row, first, *[part[0] for part in projected[1:]],
        *[blocks[k] for k in range(1, wide)],
    )
    for flip in range(1, plane_count):
        (shapes[flip],) = make_shapes(flip, traces[0], False)
    swapped = {k: exchange(traces[k], "wide", k) if k else traces[0] for k in order}
    for k in range(1, wide):
        swapped[k], _ = lax.optimization_barrier((swapped[k], shapes[1:]))
    passed = [swapped] + [
        {k: exchange(swapped[k], "planes", flip) for k in order[::-1]}
        for flip in range(1, plane_count)
    ]

    residual, edges, ordered = [], [], []
    for flip in range(plane_count):
        part, tip, sorted_rows = call(
            functools.partial(residual_kernel, flip), "residual",
            [(here * frames, width), (edge, width), (here, frames, LANES)],
            1, 3 + wide, 70000000, 6 * mib,
        )(place, shapes[flip], filtered[flip], code, *[passed[flip][k] for k in range(wide)])
        residual.append(part)
        edges.append(tip)
        ordered.append(sorted_rows)

    outer = plane ^ jnp.where(rep == 0, plane_count - 1, 0)
    tip = edges[0]
    for flip in range(1, plane_count):
        tip = jnp.where(outer == flip, edges[flip], tip)
    tip = exchange(tip, "rep", 1)

    foot_share = support.shape[1] // plane_count
    in_order = []
    for q in range(plane_count):
        rows_q = ordered[0]
        for flip in range(1, plane_count):
            rows_q = jnp.where(plane ^ q == flip, ordered[flip], rows_q)
        in_order.append(rows_q)
    mine = lax.dynamic_slice_in_dim(jnp.concatenate(in_order), plane * foot_share, foot_share, 2)
    trace_out = jnp.transpose(mine, (2, 1, 0))

    back_projected = pl.pallas_call(
        functools.partial(backward_kernel, plane_count),
        out_shape=shaped(movie_frames.shape),
        in_specs=[SMEM] + [VMEM] * (3 + plane_count),
        out_specs=HBM,
        scratch_shapes=[
            pltpu.VMEM(((rows + 2 * BLOCK) * frames, width), BF16),
            pltpu.VMEM(movie_frames.shape, BF16),
            pltpu.SemaphoreType.DMA((rows // BLOCK,)),
        ],
        compiler_params=pltpu.CompilerParams(vmem_limit_bytes=32 * mib),
        cost_estimate=pl.CostEstimate(flops=1000000000, bytes_accessed=3 * mib, transcendentals=0),
        name="backward",
    )(place, tip, col_adj, row_adj, *residual)
    return trace_out, back_projected


def solution(mesh):
    return jax.shard_map(
        on_device,
        mesh=mesh,
        in_specs=(
            P("planes", ("groups", "wide"), "rep", None),
            P("rep", None),
            P("rep", None),
            P("rep", None),
            P(None, "planes", None),
            P(),
            P(),
            P("wide", None, None),
            P("wide", None),
        ),
        out_specs=(
            P("planes", ("groups", "wide"), "rep"),
            P("planes", ("groups", "wide"), "rep", None),
        ),
        check_vma=False,
    )
```

```python
import functools

import jax
import jax.numpy as jnp
from jax import lax
from jax.experimental import pallas as pl
from jax.experimental.pallas import tpu as pltpu
from jax.sharding import PartitionSpec as P

BLOCK = 16
LANES = 128
F32 = jnp.float32
BF16 = jnp.bfloat16
REP, PLANE, WIDE = 0, 1, 2


def exchange(cells, axis, flip):
    count = lax.axis_size(axis)
    return lax.ppermute(cells, axis, [(i, i ^ flip) for i in range(count)])


def iota(shape, dim):
    return lax.broadcasted_iota(jnp.int32, shape, dim)


def tap_row(taps_ref, place):
    lane = iota((8, LANES), 1)
    row = jnp.zeros((8, LANES), F32)
    for k in range(taps_ref.shape[0]):
        row = jnp.where(lane == place(k) % LANES, taps_ref[k], row)
    return row[:1]


def toeplitz(row, count, shift=0):
    return pltpu.roll(
        jnp.broadcast_to(row, (count, row.shape[1])), shift, 1, stride=1, stride_axis=0
    )


def column_band(taps_ref, rim, sign):
    rolled = toeplitz(tap_row(taps_ref, lambda k: sign * (k - rim)), LANES)
    gap = iota((LANES, LANES), 1) - iota((LANES, LANES), 0)
    return jnp.where(jnp.abs(gap) <= rim, rolled, 0.0).astype(BF16)


def row_band_forward(taps_ref, rim, frames):
    out_rows, depth, span = BLOCK * frames, 3 * BLOCK * frames, 3 * BLOCK
    band = toeplitz(tap_row(taps_ref, lambda k: k + BLOCK - rim), BLOCK)[:, :span].astype(BF16)
    left = (iota((out_rows, BLOCK), 0) // frames == iota((out_rows, BLOCK), 1)).astype(BF16)
    right = (lax.rem(iota((span, depth), 1), span) == iota((span, depth), 0)).astype(BF16)
    tall = jnp.dot(left, band, preferred_element_type=F32).astype(BF16)
    spread = jnp.dot(tall, right, preferred_element_type=F32)
    start = iota((out_rows, depth), 1) - span * lax.rem(iota((out_rows, depth), 0), frames)
    return jnp.where((start >= 0) & (start < span), spread, 0.0).astype(BF16)


def row_band_adjoint(taps_ref, rim, frames):
    out_rows, depth, span = BLOCK * frames, 3 * BLOCK * frames, 3 * BLOCK
    band = toeplitz(tap_row(taps_ref, lambda k: BLOCK + rim - k), BLOCK)[:, :span].astype(BF16)
    left = (lax.rem(iota((out_rows, BLOCK), 0), BLOCK) == iota((out_rows, BLOCK), 1)).astype(BF16)
    right = (iota((span, depth), 1) // frames == iota((span, depth), 0)).astype(BF16)
    tall = jnp.dot(left, band, preferred_element_type=F32).astype(BF16)
    spread = jnp.dot(tall, right, preferred_element_type=F32)
    same = lax.rem(iota((out_rows, depth), 1), frames) == iota((out_rows, depth), 0) // BLOCK
    return jnp.where(same, spread, 0.0).astype(BF16)


def per_frame(rows, frames, copies):
    tall = jnp.broadcast_to(rows[:, None, :], (BLOCK, frames, LANES)).reshape(BLOCK * frames, LANES)
    return tall if copies == 1 else jnp.concatenate([tall] * copies, axis=1)


def prepare_kernel(
    rim, cuts, col_hbm, row_hbm, movie_hbm, mask_hbm, support_hbm, templates_hbm,
    smooth_ref, col_fwd_ref, row_fwd_ref, code_ref, templates_ref, flat_ref,
    movie_ref, mask_ref, support_ref, packed_ref, loose_ref, col_ref, row_ref, sems,
):
    planes, frames, rows, _ = movie_ref.shape
    some = frames // cuts

    def fetch(n, source, target):
        copy = pltpu.make_async_copy(source, target, sems.at[n])
        copy.start()
        return copy

    tap_copies = [fetch(0, col_hbm, col_ref), fetch(1, row_hbm, row_ref)]
    movie_copies = []
    for n in range(planes * cuts):
        piece = (n // cuts, pl.ds(n % cuts * some, some))
        movie_copies.append(fetch(5 + n, movie_hbm.at[piece], movie_ref.at[piece]))
    packed_copy = fetch(2, templates_hbm, packed_ref)
    code_copies = [fetch(3, mask_hbm, mask_ref), fetch(4, support_hbm, support_ref)]
    for copy in tap_copies:
        copy.wait()
    col_fwd = column_band(col_ref, rim, -1)
    col_fwd_ref[...] = col_fwd
    row_fwd_ref[...] = row_band_forward(row_ref, rim, frames)
    for n, copy in enumerate(movie_copies):
        p, first = n // cuts, n % cuts * some
        copy.wait()
        full = jnp.dot(
            movie_ref[p, first : first + some].reshape(some * rows, LANES), col_fwd,
            preferred_element_type=F32,
        )
        smooth_ref[first : first + some, BLOCK : BLOCK + rows, p * LANES : (p + 1) * LANES] = (
            full.astype(BF16).reshape(some, rows, LANES)
        )
    packed_copy.wait()
    loose_ref[...] = packed_ref[...].astype(F32)
    unit = (iota((LANES, LANES), 0) == iota((LANES, LANES), 1)).astype(BF16)
    for p in range(planes):
        shapes = loose_ref[pl.ds(p, templates_ref.shape[1], stride=planes), :].astype(BF16)
        flat_ref[:, p * LANES : (p + 1) * LANES] = shapes
        templates_ref[p * LANES : (p + 1) * LANES, :] = lax.dot_general(
            unit, shapes, (((1,), (1,)), ((), ())), preferred_element_type=F32
        ).astype(BF16)
    for copy in code_copies:
        copy.wait()
    code_ref[...] = support_ref[...] * 2 + mask_ref[...]


def forward_kernel(
    flip, fill, place_ref, smooth_in_ref, edge_ref, col_fwd_ref, row_fwd_ref, code_ref,
    templates_ref, smooth_ref, filtered_ref, *refs
):
    outs, projected_ref = refs[:-1], refs[-1]
    frames, padded_rows, width = smooth_ref.shape
    planes, rows = width // LANES, padded_rows - 2 * BLOCK
    if fill:
        for p in range(planes):
            edge = jnp.dot(
                edge_ref[p].reshape(frames * BLOCK, LANES), col_fwd_ref[...],
                preferred_element_type=F32,
            ).reshape(frames, BLOCK, LANES)
            lanes = slice(p * LANES, (p + 1) * LANES)
            above = jnp.where(place_ref[REP] > 0, edge, 0.0).astype(BF16)
            below = jnp.where(place_ref[REP] > 0, 0.0, edge).astype(BF16)
            smooth_ref[:, :BLOCK, lanes] = above
            smooth_ref[:, BLOCK + rows :, lanes] = below
    here = filtered_ref.shape[0] // frames
    first = (place_ref[PLANE] ^ flip) * here
    tiles = templates_ref.shape[1] // LANES
    for b in range(here // BLOCK):
        top = pl.multiple_of(first + b * BLOCK, BLOCK)
        near = smooth_ref[:, pl.ds(top, 3 * BLOCK), :].reshape(frames * 3 * BLOCK, width)
        along = jnp.dot(row_fwd_ref[...], near, preferred_element_type=F32)
        code = code_ref[pl.ds(top, BLOCK), :]
        mask = per_frame((code & 1).astype(F32), frames, planes)
        filtered = (along * mask).astype(BF16)
        spot = slice(b * BLOCK * frames, (b + 1) * BLOCK * frames)
        filtered_ref[spot, :] = filtered
        dense = jnp.dot(filtered, templates_ref[...], preferred_element_type=F32)
        picked = per_frame(code >> 1, frames, 1)
        lane, tile = picked & (LANES - 1), picked // LANES
        chosen = jnp.zeros(picked.shape, F32)
        for t in range(tiles):
            found = jnp.take_along_axis(
                dense[:, t * LANES : (t + 1) * LANES], lane, axis=1, mode="promise_in_bounds"
            )
            chosen = jnp.where(tile == t, found, chosen)
        projected_ref[spot, :] = chosen.astype(BF16)
    size = outs[0].shape[0]
    for k, out_ref in enumerate(outs):
        start = pl.multiple_of((place_ref[WIDE] ^ k) * size, size)
        out_ref[...] = projected_ref[pl.ds(start, size), :]


def add_all(parts):
    total = parts[0][...].astype(F32)
    for part in parts[1:]:
        total = total + part[...].astype(F32)
    return total.astype(BF16)


def sum_kernel(lag_ref, *refs):
    parts, out_ref = refs[:-1], refs[-1]
    rows = parts[0].shape[0]
    out_ref[:rows, :] = add_all(parts)
    out_ref[rows:, :] = lag_ref[...]


def mix_kernel(wide, count, place_ref, owner_ref, lag_ref, *refs):
    parts, refs = refs[:count], refs[count:]
    blocks, outs = refs[: wide - 1], refs[wide - 1 : 2 * wide - 1]
    cells_ref, kernels_ref, traces_ref, tables_ref = refs[2 * wide - 1 :]
    _, share, frames, lanes = cells_ref.shape
    total = wide * frames
    here = place_ref[WIDE]
    cells_ref[here] = add_all(parts).reshape(share, frames, lanes)
    kernels_ref[here] = lag_ref[...].astype(F32)
    for k, block in enumerate(blocks, 1):
        cells_ref[here ^ k] = block[: share * frames, :].reshape(share, frames, lanes)
        kernels_ref[here ^ k] = block[share * frames :, :].astype(F32)

    def table(values):
        row = jnp.concatenate([values[i : i + 1, :] for i in range(2 * total // LANES)], axis=1)
        return toeplitz(row, total, total + 1)[:, :total].astype(BF16)

    if wide <= share:
        for d in range(wide):
            tables_ref[d] = table(kernels_ref[d])
    first = (place_ref[PLANE] * wide + here) * share
    for h in range(share):
        owner = owner_ref[first + h]
        lag = tables_ref[owner] if wide <= share else table(kernels_ref[owner])
        mixed = jnp.dot(lag, cells_ref[:, h].reshape(total, lanes), preferred_element_type=F32)
        traces_ref[:, h] = jnp.maximum(mixed, 0.0).astype(BF16).reshape(wide, frames, lanes)
    for k, out_ref in enumerate(outs):
        out_ref[...] = traces_ref[here ^ k]


def shapes_kernel(flip, rim, frames, place_ref, *refs):
    if rim:
        col_ref, row_ref, code_ref, templates_ref, shapes_ref, col_adj_ref, row_adj_ref = refs
        band = column_band(col_ref, rim, 1)
        planes = templates_ref.shape[1] // LANES
        col_adj_ref[...] = jnp.zeros_like(col_adj_ref)
        for p in range(planes):
            lanes = slice(p * LANES, (p + 1) * LANES)
            col_adj_ref[lanes, lanes] = band
        row_adj_ref[...] = row_band_adjoint(row_ref, rim, frames)
    else:
        code_ref, templates_ref, shapes_ref = refs
    count, here = templates_ref.shape[0], shapes_ref.shape[0]
    first = pl.multiple_of((place_ref[PLANE] ^ flip) * here, here)

    @pl.loop(0, here // 8)
    def _(g):
        support = code_ref[pl.ds(pl.multiple_of(first + g * 8, 8), 8), :] >> 1
        columns = jnp.transpose(support)
        lane = iota((LANES, count), 1)
        for i in range(8):
            named = jnp.broadcast_to(columns[:, i : i + 1], (LANES, count))
            shapes_ref[g * 8 + i] = jnp.dot(
                (lane == named).astype(BF16), templates_ref[...], preferred_element_type=F32
            ).astype(BF16)


def residual_kernel(
    flip, place_ref, shapes_ref, filtered_ref, code_ref, *refs
):
    traces, (out_ref, edge_ref, ordered_ref) = refs[:-3], refs[-3:]
    wide = len(traces)
    share, frames, lanes = traces[0].shape
    copies = filtered_ref.shape[1] // LANES
    base = (place_ref[PLANE] ^ flip) * wide * share
    for k in range(wide):
        block = place_ref[WIDE] ^ k
        for h in range(share):
            row = block * share + h
            model = jnp.dot(traces[k][h], shapes_ref[row], preferred_element_type=F32)
            mask = (code_ref[pl.ds(base + row, 1), :] & 1).astype(F32)
            spot = pl.ds(pl.multiple_of(row * frames, frames), frames)
            out_ref[spot, :] = (
                filtered_ref[spot, :].astype(F32) - jnp.concatenate([mask] * copies, axis=1) * model
            ).astype(BF16)
        ordered_ref[pl.ds(block * share, share)] = traces[k][...]
    edge = edge_ref.shape[0]
    start = jnp.where(place_ref[REP] > 0, 0, out_ref.shape[0] - edge)
    edge_ref[...] = out_ref[pl.ds(pl.multiple_of(start, edge), edge), :]


def backward_kernel(count, place_ref, edge_ref, col_adj_ref, row_adj_ref, *refs):
    parts, (out_hbm, padded_ref, out_ref, sems) = refs[:count], refs[count:]
    planes, frames, rows, _ = out_ref.shape
    edge, size = BLOCK * frames, parts[0].shape[0]
    zero = jnp.zeros_like(edge_ref)
    padded_ref[:edge, :] = jnp.where(place_ref[REP] > 0, edge_ref[...], zero)
    padded_ref[edge + rows * frames :, :] = jnp.where(place_ref[REP] > 0, zero, edge_ref[...])
    for flip, part in enumerate(parts):
        spot = pl.multiple_of(edge + (place_ref[PLANE] ^ flip) * size, edge)
        padded_ref[pl.ds(spot, size), :] = part[...]
    def along(b):
        near = padded_ref[b * edge : (b + 3) * edge, :]
        return jnp.dot(row_adj_ref[...], near, preferred_element_type=F32).astype(BF16)

    copies = []
    back = along(0)
    for b in range(rows // BLOCK):
        ahead = along(b + 1) if b + 1 < rows // BLOCK else None
        full = jnp.dot(back, col_adj_ref[...], preferred_element_type=F32).astype(BF16)
        for p in range(planes):
            out_ref[p, :, b * BLOCK : (b + 1) * BLOCK, :] = full[
                :, p * LANES : (p + 1) * LANES
            ].reshape(frames, BLOCK, LANES)
        piece = (slice(None), slice(None), pl.ds(b * BLOCK, BLOCK))
        copy = pltpu.make_async_copy(out_ref.at[piece], out_hbm.at[piece], sems.at[b])
        copy.start()
        copies.append(copy)
        back = ahead
    for copy in copies:
        copy.wait()


VMEM = pl.BlockSpec(memory_space=pltpu.VMEM)
SMEM = pl.BlockSpec(memory_space=pltpu.SMEM)
HBM = pl.BlockSpec(memory_space=pltpu.HBM)


def shaped(shape):
    return jax.ShapeDtypeStruct(shape, BF16)


def call(kernel, name, outs, smem, vmem, flops, moved, scratch=(), aliases=None):
    return pl.pallas_call(
        kernel,
        out_shape=tuple(shaped(s) if isinstance(s, tuple) else s for s in outs),
        in_specs=[SMEM] * smem + [VMEM] * vmem,
        out_specs=(VMEM,) * len(outs),
        scratch_shapes=scratch,
        input_output_aliases=aliases or {},
        compiler_params=pltpu.CompilerParams(vmem_limit_bytes=32 * 1024 * 1024),
        cost_estimate=pl.CostEstimate(flops=flops, bytes_accessed=moved, transcendentals=0),
        name=name,
    )


def lag_kernel_values(gains, lags, frame_count):
    taps = gains.shape[1]
    lag_values = jnp.arange(2 * frame_count, dtype=jnp.int32) - (frame_count - 1)
    offsets = jnp.arange(taps, dtype=jnp.int32) - (taps - 1) // 2
    hits = lag_values[None, :, None] == lags[:, None, None] * offsets[None, None, :]
    spread = jnp.where(hits, gains[:, None, :], jnp.zeros((), gains.dtype))
    return jnp.sum(spread, axis=(0, 2)).astype(BF16)


def on_device(
    movie_frames, pixel_mask, tile_owner, support, templates, row_taps, col_taps, lag_gains, dilations
):
    planes, frames, rows, cols = movie_frames.shape
    wide, plane_count = lax.axis_size("wide"), lax.axis_size("planes")
    rim = (row_taps.shape[0] - 1) // 2
    total_frames, width = frames * wide, planes * cols
    here = rows // plane_count
    share = here // wide
    edge = BLOCK * frames
    rep, plane, spot = lax.axis_index("rep"), lax.axis_index("planes"), lax.axis_index("wide")
    place = jnp.stack([rep, plane, spot]).astype(jnp.int32)
    mib = 1 << 20

    start = jnp.where(rep == 0, rows - BLOCK, 0)
    rim_rows = exchange(lax.dynamic_slice_in_dim(movie_frames, start, BLOCK, axis=2), "rep", 1)
    cuts = 2
    depth, names = 3 * BLOCK * frames, templates.shape[0]
    smooth, col_fwd, row_fwd, code, tall_templates, flat_templates = pl.pallas_call(
        functools.partial(prepare_kernel, rim, cuts),
        out_shape=(
            shaped((frames, rows + 2 * BLOCK, width)), shaped((cols, cols)), shaped((edge, depth)),
            jax.ShapeDtypeStruct(support.shape, jnp.int32), shaped((width, names)),
            shaped((names, width)),
        ),
        in_specs=[HBM] * 6,
        out_specs=(VMEM,) * 6,
        scratch_shapes=[
            pltpu.VMEM(movie_frames.shape, BF16),
            pltpu.VMEM(pixel_mask.shape, jnp.int32),
            pltpu.VMEM(support.shape, jnp.int32),
            pltpu.VMEM((names * planes, cols), BF16),
            pltpu.VMEM((names * planes, cols), F32),
            pltpu.SMEM(col_taps.shape, F32),
            pltpu.SMEM(row_taps.shape, F32),
            pltpu.SemaphoreType.DMA((5 + planes * cuts,)),
        ],
        compiler_params=pltpu.CompilerParams(vmem_limit_bytes=32 * mib),
        cost_estimate=pl.CostEstimate(flops=200000000, bytes_accessed=3 * mib, transcendentals=0),
        name="prepare",
    )(
        *[
            pltpu.with_memory_space_constraint(x, pltpu.HBM)
            for x in (
                col_taps, row_taps, movie_frames, pixel_mask, support,
                templates.reshape(names * planes, cols),
            )
        ]
    )

    order = list(range(wide // 2, wide)) + list(range(1, wide // 2)) + [0]
    filtered, projected = [None] * plane_count, [None] * plane_count
    for turn in range(plane_count):
        flip = (turn + 1) % plane_count
        smooth, filtered[flip], *mine = call(
            functools.partial(forward_kernel, flip, turn == 0), "forward",
            [smooth.shape, (here * frames, width)] + [(share * frames, LANES)] * wide,
            1, 6, 800000000, 3 * mib, aliases={1: 0},
            scratch=[pltpu.VMEM((here * frames, LANES), BF16)],
        )(place, smooth, rim_rows, col_fwd, row_fwd, code, tall_templates)
        if flip:
            halves = [order[: wide // 2], order[wide // 2 :]]
            mine = dict(enumerate(mine))
            for ks in halves:
                both = exchange(jnp.concatenate([mine[k] for k in ks]), "planes", flip)
                for i, k in enumerate(ks):
                    mine[k] = both[i * share * frames : (i + 1) * share * frames]
        projected[flip] = mine
        if turn == 0:
            gains, lags, _ = lax.optimization_barrier((lag_gains, dilations, smooth))
            kernel_row = lag_kernel_values(gains[0], lags[0], total_frames)
            lag_rows = -(-2 * total_frames // (LANES * BLOCK)) * BLOCK
            kernel_row = jnp.pad(kernel_row, (0, lag_rows * LANES - 2 * total_frames))
            kernel_row = kernel_row.reshape(lag_rows, LANES)

    block_rows = share * frames + lag_rows
    sums, blocks = {}, {}
    for k in order[:-1]:
        (sums[k],) = call(
            sum_kernel, "sum", [(block_rows, LANES)], 0, 1 + plane_count, 100000, mib // 4
        )(kernel_row, *[part[k] for part in projected])
        blocks[k] = exchange(sums[k], "wide", k)

    def make_shapes(flip, after, bands):
        late_code, late_templates, _ = lax.optimization_barrier((code, flat_templates, after))
        outs = [pltpu.VMEM((here, LANES, width), BF16)]
        taps = ()
        if bands:
            outs += [(width, width), (edge, depth)]
            taps = (col_taps, row_taps)
        return call(
            functools.partial(shapes_kernel, flip, rim if bands else 0, frames), "shapes",
            outs, 1 + len(taps), 2, 2150000000, 5 * mib,
        )(place, *taps, late_code, late_templates)

    shapes = [None] * plane_count
    shapes[0], col_adj, row_adj = make_shapes(0, [sums[k] for k in order[:-1]], True)
    first, col_adj = lax.optimization_barrier((projected[0][0], col_adj))

    cell_shape = (wide, share, frames, LANES)
    tables = (wide, total_frames, total_frames) if wide <= share else (1, BLOCK, LANES)
    traces = call(
        functools.partial(mix_kernel, wide, plane_count), "mix", [cell_shape[1:]] * wide,
        2, wide + plane_count, 20000000, mib,
        scratch=[
            pltpu.VMEM(cell_shape, BF16), pltpu.VMEM((wide, lag_rows, LANES), F32),
            pltpu.VMEM(cell_shape, BF16), pltpu.VMEM(tables, BF16),
        ],
    )(
        place, tile_owner[:, 0], kernel_row, first, *[part[0] for part in projected[1:]],
        *[blocks[k] for k in range(1, wide)],
    )
    for flip in range(1, plane_count):
        (shapes[flip],) = make_shapes(flip, traces[0], False)
    swapped = {k: exchange(traces[k], "wide", k) if k else traces[0] for k in order}
    for k in range(1, wide):
        swapped[k], _ = lax.optimization_barrier((swapped[k], shapes[1:]))
    passed = [swapped] + [
        {k: exchange(swapped[k], "planes", flip) for k in order[::-1]}
        for flip in range(1, plane_count)
    ]

    residual, edges, ordered = [], [], []
    for flip in range(plane_count):
        part, tip, sorted_rows = call(
            functools.partial(residual_kernel, flip), "residual",
            [(here * frames, width), (edge, width), (here, frames, LANES)],
            1, 3 + wide, 70000000, 6 * mib,
        )(place, shapes[flip], filtered[flip], code, *[passed[flip][k] for k in range(wide)])
        residual.append(part)
        edges.append(tip)
        ordered.append(sorted_rows)

    outer = plane ^ jnp.where(rep == 0, plane_count - 1, 0)
    tip = edges[0]
    for flip in range(1, plane_count):
        tip = jnp.where(outer == flip, edges[flip], tip)
    tip = exchange(tip, "rep", 1)

    foot_share = support.shape[1] // plane_count
    in_order = []
    for q in range(plane_count):
        rows_q = ordered[0]
        for flip in range(1, plane_count):
            rows_q = jnp.where(plane ^ q == flip, ordered[flip], rows_q)
        in_order.append(rows_q)
    mine = lax.dynamic_slice_in_dim(jnp.concatenate(in_order), plane * foot_share, foot_share, 2)
    trace_out = jnp.transpose(mine, (2, 1, 0))

    back_projected = pl.pallas_call(
        functools.partial(backward_kernel, plane_count),
        out_shape=shaped(movie_frames.shape),
        in_specs=[SMEM] + [VMEM] * (3 + plane_count),
        out_specs=HBM,
        scratch_shapes=[
            pltpu.VMEM(((rows + 2 * BLOCK) * frames, width), BF16),
            pltpu.VMEM(movie_frames.shape, BF16),
            pltpu.SemaphoreType.DMA((rows // BLOCK,)),
        ],
        compiler_params=pltpu.CompilerParams(vmem_limit_bytes=32 * mib),
        cost_estimate=pl.CostEstimate(flops=1000000000, bytes_accessed=3 * mib, transcendentals=0),
        name="backward",
    )(place, tip, col_adj, row_adj, *residual)
    return trace_out, back_projected


def solution(mesh):
    return jax.shard_map(
        on_device,
        mesh=mesh,
        in_specs=(
            P("planes", ("groups", "wide"), "rep", None),
            P("rep", None),
            P("rep", None),
            P("rep", None),
            P(None, "planes", None),
            P(),
            P(),
            P("wide", None, None),
            P("wide", None),
        ),
        out_specs=(
            P("planes", ("groups", "wide"), "rep"),
            P("planes", ("groups", "wide"), "rep", None),
        ),
        check_vma=False,
    )
```

```python
import functools

import jax
import jax.numpy as jnp
from jax import lax
from jax.experimental import pallas as pl
from jax.experimental.pallas import tpu as pltpu
from jax.sharding import PartitionSpec as P

BLOCK = 16
LANES = 128
F32 = jnp.float32
BF16 = jnp.bfloat16
REP, PLANE, WIDE = 0, 1, 2


def exchange(cells, axis, flip):
    count = lax.axis_size(axis)
    return lax.ppermute(cells, axis, [(i, i ^ flip) for i in range(count)])


def iota(shape, dim):
    return lax.broadcasted_iota(jnp.int32, shape, dim)


def tap_row(taps_ref, place):
    lane = iota((8, LANES), 1)
    row = jnp.zeros((8, LANES), F32)
    for k in range(taps_ref.shape[0]):
        row = jnp.where(lane == place(k) % LANES, taps_ref[k], row)
    return row[:1]


def toeplitz(row, count, shift=0):
    return pltpu.roll(
        jnp.broadcast_to(row, (count, row.shape[1])), shift, 1, stride=1, stride_axis=0
    )


def column_band(taps_ref, rim, sign):
    rolled = toeplitz(tap_row(taps_ref, lambda k: sign * (k - rim)), LANES)
    gap = iota((LANES, LANES), 1) - iota((LANES, LANES), 0)
    return jnp.where(jnp.abs(gap) <= rim, rolled, 0.0).astype(BF16)


def row_band_forward(taps_ref, rim, frames):
    out_rows, depth, span = BLOCK * frames, 3 * BLOCK * frames, 3 * BLOCK
    band = toeplitz(tap_row(taps_ref, lambda k: k + BLOCK - rim), BLOCK)[:, :span].astype(BF16)
    left = (iota((out_rows, BLOCK), 0) // frames == iota((out_rows, BLOCK), 1)).astype(BF16)
    right = (lax.rem(iota((span, depth), 1), span) == iota((span, depth), 0)).astype(BF16)
    tall = jnp.dot(left, band, preferred_element_type=F32).astype(BF16)
    spread = jnp.dot(tall, right, preferred_element_type=F32)
    start = iota((out_rows, depth), 1) - span * lax.rem(iota((out_rows, depth), 0), frames)
    return jnp.where((start >= 0) & (start < span), spread, 0.0).astype(BF16)


def row_band_adjoint(taps_ref, rim, frames):
    out_rows, depth, span = BLOCK * frames, 3 * BLOCK * frames, 3 * BLOCK
    band = toeplitz(tap_row(taps_ref, lambda k: BLOCK + rim - k), BLOCK)[:, :span].astype(BF16)
    left = (lax.rem(iota((out_rows, BLOCK), 0), BLOCK) == iota((out_rows, BLOCK), 1)).astype(BF16)
    right = (iota((span, depth), 1) // frames == iota((span, depth), 0)).astype(BF16)
    tall = jnp.dot(left, band, preferred_element_type=F32).astype(BF16)
    spread = jnp.dot(tall, right, preferred_element_type=F32)
    same = lax.rem(iota((out_rows, depth), 1), frames) == iota((out_rows, depth), 0) // BLOCK
    return jnp.where(same, spread, 0.0).astype(BF16)


def per_frame(rows, frames, copies):
    tall = jnp.broadcast_to(rows[:, None, :], (BLOCK, frames, LANES)).reshape(BLOCK * frames, LANES)
    return tall if copies == 1 else jnp.concatenate([tall] * copies, axis=1)


def prepare_kernel(
    rim, cuts, col_hbm, row_hbm, movie_hbm, mask_hbm, support_hbm, templates_hbm,
    smooth_ref, col_fwd_ref, row_fwd_ref, code_ref, templates_ref, flat_ref,
    movie_ref, mask_ref, support_ref, packed_ref, loose_ref, col_ref, row_ref, sems,
):
    planes, frames, rows, _ = movie_ref.shape
    some = frames // cuts

    def fetch(n, source, target):
        copy = pltpu.make_async_copy(source, target, sems.at[n])
        copy.start()
        return copy

    tap_copies = [fetch(0, col_hbm, col_ref), fetch(1, row_hbm, row_ref)]
    movie_copies = []
    for n in range(planes * cuts):
        piece = (n // cuts, pl.ds(n % cuts * some, some))
        movie_copies.append(fetch(5 + n, movie_hbm.at[piece], movie_ref.at[piece]))
    packed_copy = fetch(2, templates_hbm, packed_ref)
    code_copies = [fetch(3, mask_hbm, mask_ref), fetch(4, support_hbm, support_ref)]
    for copy in tap_copies:
        copy.wait()
    col_fwd = column_band(col_ref, rim, -1)
    col_fwd_ref[...] = col_fwd
    row_fwd_ref[...] = row_band_forward(row_ref, rim, frames)
    for n, copy in enumerate(movie_copies):
        p, first = n // cuts, n % cuts * some
        copy.wait()
        full = jnp.dot(
            movie_ref[p, first : first + some].reshape(some * rows, LANES), col_fwd,
            preferred_element_type=F32,
        )
        smooth_ref[first : first + some, BLOCK : BLOCK + rows, p * LANES : (p + 1) * LANES] = (
            full.astype(BF16).reshape(some, rows, LANES)
        )
    packed_copy.wait()
    loose_ref[...] = packed_ref[...].astype(F32)
    unit = (iota((LANES, LANES), 0) == iota((LANES, LANES), 1)).astype(BF16)
    for p in range(planes):
        shapes = loose_ref[pl.ds(p, templates_ref.shape[1], stride=planes), :].astype(BF16)
        flat_ref[:, p * LANES : (p + 1) * LANES] = shapes
        templates_ref[p * LANES : (p + 1) * LANES, :] = lax.dot_general(
            unit, shapes, (((1,), (1,)), ((), ())), preferred_element_type=F32
        ).astype(BF16)
    for copy in code_copies:
        copy.wait()
    code_ref[...] = support_ref[...] * 2 + mask_ref[...]


def forward_kernel(
    flip, fill, place_ref, smooth_in_ref, edge_ref, col_fwd_ref, row_fwd_ref, code_ref,
    templates_ref, smooth_ref, filtered_ref, *refs
):
    outs, projected_ref = refs[:-1], refs[-1]
    frames, padded_rows, width = smooth_ref.shape
    planes, rows = width // LANES, padded_rows - 2 * BLOCK
    if fill:
        for p in range(planes):
            edge = jnp.dot(
                edge_ref[p].reshape(frames * BLOCK, LANES), col_fwd_ref[...],
                preferred_element_type=F32,
            ).reshape(frames, BLOCK, LANES)
            lanes = slice(p * LANES, (p + 1) * LANES)
            above = jnp.where(place_ref[REP] > 0, edge, 0.0).astype(BF16)
            below = jnp.where(place_ref[REP] > 0, 0.0, edge).astype(BF16)
            smooth_ref[:, :BLOCK, lanes] = above
            smooth_ref[:, BLOCK + rows :, lanes] = below
    here = filtered_ref.shape[0] // frames
    first = (place_ref[PLANE] ^ flip) * here
    tiles = templates_ref.shape[1] // LANES
    for b in range(here // BLOCK):
        top = pl.multiple_of(first + b * BLOCK, BLOCK)
        near = smooth_ref[:, pl.ds(top, 3 * BLOCK), :].reshape(frames * 3 * BLOCK, width)
        along = jnp.dot(row_fwd_ref[...], near, preferred_element_type=F32)
        code = code_ref[pl.ds(top, BLOCK), :]
        mask = per_frame((code & 1).astype(F32), frames, planes)
        filtered = (along * mask).astype(BF16)
        spot = slice(b * BLOCK * frames, (b + 1) * BLOCK * frames)
        filtered_ref[spot, :] = filtered
        dense = jnp.dot(filtered, templates_ref[...], preferred_element_type=F32)
        picked = per_frame(code >> 1, frames, 1)
        lane, tile = picked & (LANES - 1), picked // LANES
        chosen = jnp.zeros(picked.shape, F32)
        for t in range(tiles):
            found = jnp.take_along_axis(
                dense[:, t * LANES : (t + 1) * LANES], lane, axis=1, mode="promise_in_bounds"
            )
            chosen = jnp.where(tile == t, found, chosen)
        projected_ref[spot, :] = chosen.astype(BF16)
    size = outs[0].shape[0]
    for k, out_ref in enumerate(outs):
        start = pl.multiple_of((place_ref[WIDE] ^ k) * size, size)
        out_ref[...] = projected_ref[pl.ds(start, size), :]


def add_all(parts):
    total = parts[0][...].astype(F32)
    for part in parts[1:]:
        total = total + part[...].astype(F32)
    return total.astype(BF16)


def sum_kernel(lag_ref, *refs):
    parts, out_ref = refs[:-1], refs[-1]
    rows = parts[0].shape[0]
    out_ref[:rows, :] = add_all(parts)
    out_ref[rows:, :] = lag_ref[...]


def mix_kernel(wide, count, place_ref, owner_ref, lag_ref, *refs):
    parts, refs = refs[:count], refs[count:]
    blocks, outs = refs[: wide - 1], refs[wide - 1 : 2 * wide - 1]
    cells_ref, kernels_ref, traces_ref, tables_ref = refs[2 * wide - 1 :]
    _, share, frames, lanes = cells_ref.shape
    total = wide * frames
    here = place_ref[WIDE]
    cells_ref[here] = add_all(parts).reshape(share, frames, lanes)
    kernels_ref[here] = lag_ref[...].astype(F32)
    for k, block in enumerate(blocks, 1):
        cells_ref[here ^ k] = block[: share * frames, :].reshape(share, frames, lanes)
        kernels_ref[here ^ k] = block[share * frames :, :].astype(F32)

    def table(values):
        row = jnp.concatenate([values[i : i + 1, :] for i in range(2 * total // LANES)], axis=1)
        return toeplitz(row, total, total + 1)[:, :total].astype(BF16)

    if wide <= share:
        for d in range(wide):
            tables_ref[d] = table(kernels_ref[d])
    first = (place_ref[PLANE] * wide + here) * share
    for h in range(share):
        owner = owner_ref[first + h]
        lag = tables_ref[owner] if wide <= share else table(kernels_ref[owner])
        mixed = jnp.dot(lag, cells_ref[:, h].reshape(total, lanes), preferred_element_type=F32)
        traces_ref[:, h] = jnp.maximum(mixed, 0.0).astype(BF16).reshape(wide, frames, lanes)
    for k, out_ref in enumerate(outs):
        out_ref[...] = traces_ref[here ^ k]


def bands_kernel(rim, frames, col_ref, row_ref, col_adj_ref, row_adj_ref):
    band = column_band(col_ref, rim, 1)
    col_adj_ref[...] = jnp.zeros_like(col_adj_ref)
    for p in range(col_adj_ref.shape[0] // LANES):
        lanes = slice(p * LANES, (p + 1) * LANES)
        col_adj_ref[lanes, lanes] = band
    row_adj_ref[...] = row_band_adjoint(row_ref, rim, frames)


def residual_kernel(flip, place_ref, filtered_ref, code_ref, templates_ref, *refs):
    traces, (out_ref, edge_ref, ordered_ref, slots_ref) = refs[:-4], refs[-4:]
    wide = len(traces)
    share, frames, lanes = traces[0].shape
    names, width = templates_ref.shape
    tile = 2 * LANES
    base = (place_ref[PLANE] ^ flip) * wide * share
    marks = iota((lanes, tile), 1).astype(F32).astype(BF16)
    group = min(8, share)
    for k in range(wide):
        block = place_ref[WIDE] ^ k
        top = base + block * share
        for g in range(share // group):
            support = code_ref[pl.ds(top + g * group, group), :] >> 1
            support = jnp.concatenate([support] * (8 // group), axis=0)
            columns = [
                jnp.transpose(
                    jnp.where(support // tile == t, support & (tile - 1), -1).astype(F32)
                )
                for t in range(names // tile)
            ]
            for i in range(group):
                h = g * group + i
                hits = jnp.concatenate(
                    [
                        jnp.where(
                            marks
                            == jnp.broadcast_to(column[:, i : i + 1], (lanes, tile)).astype(BF16),
                            jnp.ones((), BF16), jnp.zeros((), BF16),
                        )
                        for column in columns
                    ],
                    axis=1,
                )
                slots_ref[k, h * frames : (h + 1) * frames, :] = jnp.dot(
                    traces[k][h], hits, preferred_element_type=F32
                ).astype(BF16)
        model = jnp.dot(slots_ref[k], templates_ref[...], preferred_element_type=F32)
        mask = (code_ref[pl.ds(top, share), :] & 1).astype(F32)
        mask = jnp.broadcast_to(mask[:, None, :], (share, frames, lanes)).reshape(-1, lanes)
        size = share * frames
        spot = pl.ds(pl.multiple_of(block * size, size), size)
        out_ref[spot, :] = (
            filtered_ref[spot, :].astype(F32)
            - jnp.concatenate([mask] * (width // lanes), axis=1) * model
        ).astype(BF16)
        ordered_ref[pl.ds(block * share, share)] = traces[k][...]
    edge = edge_ref.shape[0]
    start = jnp.where(place_ref[REP] > 0, 0, out_ref.shape[0] - edge)
    edge_ref[...] = out_ref[pl.ds(pl.multiple_of(start, edge), edge), :]


def backward_kernel(count, place_ref, edge_ref, col_adj_ref, row_adj_ref, *refs):
    parts, (out_hbm, padded_ref, out_ref, sems) = refs[:count], refs[count:]
    planes, frames, rows, _ = out_ref.shape
    edge, size = BLOCK * frames, parts[0].shape[0]
    zero = jnp.zeros_like(edge_ref)
    padded_ref[:edge, :] = jnp.where(place_ref[REP] > 0, edge_ref[...], zero)
    padded_ref[edge + rows * frames :, :] = jnp.where(place_ref[REP] > 0, zero, edge_ref[...])
    for flip, part in enumerate(parts):
        spot = pl.multiple_of(edge + (place_ref[PLANE] ^ flip) * size, edge)
        padded_ref[pl.ds(spot, size), :] = part[...]
    def along(b):
        near = padded_ref[b * edge : (b + 3) * edge, :]
        return jnp.dot(row_adj_ref[...], near, preferred_element_type=F32).astype(BF16)

    copies = []
    back = along(0)
    for b in range(rows // BLOCK):
        ahead = along(b + 1) if b + 1 < rows // BLOCK else None
        full = jnp.dot(back, col_adj_ref[...], preferred_element_type=F32).astype(BF16)
        for p in range(planes):
            out_ref[p, :, b * BLOCK : (b + 1) * BLOCK, :] = full[
                :, p * LANES : (p + 1) * LANES
            ].reshape(frames, BLOCK, LANES)
        piece = (slice(None), slice(None), pl.ds(b * BLOCK, BLOCK))
        copy = pltpu.make_async_copy(out_ref.at[piece], out_hbm.at[piece], sems.at[b])
        copy.start()
        copies.append(copy)
        back = ahead
    for copy in copies:
        copy.wait()


VMEM = pl.BlockSpec(memory_space=pltpu.VMEM)
SMEM = pl.BlockSpec(memory_space=pltpu.SMEM)
HBM = pl.BlockSpec(memory_space=pltpu.HBM)


def shaped(shape):
    return jax.ShapeDtypeStruct(shape, BF16)


def call(kernel, name, outs, smem, vmem, flops, moved, scratch=(), aliases=None):
    return pl.pallas_call(
        kernel,
        out_shape=tuple(shaped(s) if isinstance(s, tuple) else s for s in outs),
        in_specs=[SMEM] * smem + [VMEM] * vmem,
        out_specs=(VMEM,) * len(outs),
        scratch_shapes=scratch,
        input_output_aliases=aliases or {},
        compiler_params=pltpu.CompilerParams(vmem_limit_bytes=32 * 1024 * 1024),
        cost_estimate=pl.CostEstimate(flops=flops, bytes_accessed=moved, transcendentals=0),
        name=name,
    )


def lag_kernel_values(gains, lags, frame_count):
    taps = gains.shape[1]
    lag_values = jnp.arange(2 * frame_count, dtype=jnp.int32) - (frame_count - 1)
    offsets = jnp.arange(taps, dtype=jnp.int32) - (taps - 1) // 2
    hits = lag_values[None, :, None] == lags[:, None, None] * offsets[None, None, :]
    spread = jnp.where(hits, gains[:, None, :], jnp.zeros((), gains.dtype))
    return jnp.sum(spread, axis=(0, 2)).astype(BF16)


def on_device(
    movie_frames, pixel_mask, tile_owner, support, templates, row_taps, col_taps, lag_gains, dilations
):
    planes, frames, rows, cols = movie_frames.shape
    wide, plane_count = lax.axis_size("wide"), lax.axis_size("planes")
    rim = (row_taps.shape[0] - 1) // 2
    total_frames, width = frames * wide, planes * cols
    here = rows // plane_count
    share = here // wide
    edge = BLOCK * frames
    rep, plane, spot = lax.axis_index("rep"), lax.axis_index("planes"), lax.axis_index("wide")
    place = jnp.stack([rep, plane, spot]).astype(jnp.int32)
    mib = 1 << 20

    start = jnp.where(rep == 0, rows - BLOCK, 0)
    rim_rows = exchange(lax.dynamic_slice_in_dim(movie_frames, start, BLOCK, axis=2), "rep", 1)
    cuts = 2
    depth, names = 3 * BLOCK * frames, templates.shape[0]
    smooth, col_fwd, row_fwd, code, tall_templates, flat_templates = pl.pallas_call(
        functools.partial(prepare_kernel, rim, cuts),
        out_shape=(
            shaped((frames, rows + 2 * BLOCK, width)), shaped((cols, cols)), shaped((edge, depth)),
            jax.ShapeDtypeStruct(support.shape, jnp.int32), shaped((width, names)),
            shaped((names, width)),
        ),
        in_specs=[HBM] * 6,
        out_specs=(VMEM,) * 6,
        scratch_shapes=[
            pltpu.VMEM(movie_frames.shape, BF16),
            pltpu.VMEM(pixel_mask.shape, jnp.int32),
            pltpu.VMEM(support.shape, jnp.int32),
            pltpu.VMEM((names * planes, cols), BF16),
            pltpu.VMEM((names * planes, cols), F32),
            pltpu.SMEM(col_taps.shape, F32),
            pltpu.SMEM(row_taps.shape, F32),
            pltpu.SemaphoreType.DMA((5 + planes * cuts,)),
        ],
        compiler_params=pltpu.CompilerParams(vmem_limit_bytes=32 * mib),
        cost_estimate=pl.CostEstimate(flops=200000000, bytes_accessed=3 * mib, transcendentals=0),
        name="prepare",
    )(
        *[
            pltpu.with_memory_space_constraint(x, pltpu.HBM)
            for x in (
                col_taps, row_taps, movie_frames, pixel_mask, support,
                templates.reshape(names * planes, cols),
            )
        ]
    )

    order = list(range(wide // 2, wide)) + list(range(1, wide // 2)) + [0]
    filtered, projected = [None] * plane_count, [None] * plane_count
    for turn in range(plane_count):
        flip = (turn + 1) % plane_count
        smooth, filtered[flip], *mine = call(
            functools.partial(forward_kernel, flip, turn == 0), "forward",
            [smooth.shape, (here * frames, width)] + [(share * frames, LANES)] * wide,
            1, 6, 800000000, 3 * mib, aliases={1: 0},
            scratch=[pltpu.VMEM((here * frames, LANES), BF16)],
        )(place, smooth, rim_rows, col_fwd, row_fwd, code, tall_templates)
        if flip:
            halves = [order[: wide // 2], order[wide // 2 :]]
            mine = dict(enumerate(mine))
            for ks in halves:
                both = exchange(jnp.concatenate([mine[k] for k in ks]), "planes", flip)
                for i, k in enumerate(ks):
                    mine[k] = both[i * share * frames : (i + 1) * share * frames]
        projected[flip] = mine
        if turn == 0:
            gains, lags, _ = lax.optimization_barrier((lag_gains, dilations, smooth))
            kernel_row = lag_kernel_values(gains[0], lags[0], total_frames)
            lag_rows = -(-2 * total_frames // (LANES * BLOCK)) * BLOCK
            kernel_row = jnp.pad(kernel_row, (0, lag_rows * LANES - 2 * total_frames))
            kernel_row = kernel_row.reshape(lag_rows, LANES)

    block_rows = share * frames + lag_rows
    sums, blocks = {}, {}
    for k in order[:-1]:
        (sums[k],) = call(
            sum_kernel, "sum", [(block_rows, LANES)], 0, 1 + plane_count, 100000, mib // 4
        )(kernel_row, *[part[k] for part in projected])
        blocks[k] = exchange(sums[k], "wide", k)

    late_col, late_row, _ = lax.optimization_barrier(
        (col_taps, row_taps, [sums[k] for k in order[:-1]])
    )
    col_adj, row_adj = call(
        functools.partial(bands_kernel, rim, frames), "bands", [(width, width), (edge, depth)],
        2, 0, 10000000, mib,
    )(late_col, late_row)
    first, col_adj, row_adj = lax.optimization_barrier((projected[0][0], col_adj, row_adj))

    cell_shape = (wide, share, frames, LANES)
    tables = (wide, total_frames, total_frames) if wide <= share else (1, BLOCK, LANES)
    traces = call(
        functools.partial(mix_kernel, wide, plane_count), "mix", [cell_shape[1:]] * wide,
        2, wide + plane_count, 20000000, mib,
        scratch=[
            pltpu.VMEM(cell_shape, BF16), pltpu.VMEM((wide, lag_rows, LANES), F32),
            pltpu.VMEM(cell_shape, BF16), pltpu.VMEM(tables, BF16),
        ],
    )(
        place, tile_owner[:, 0], kernel_row, first, *[part[0] for part in projected[1:]],
        *[blocks[k] for k in range(1, wide)],
    )
    swapped = {k: exchange(traces[k], "wide", k) if k else traces[0] for k in order}
    passed = [swapped] + [
        {k: exchange(swapped[k], "planes", flip) for k in order[::-1]}
        for flip in range(1, plane_count)
    ]

    residual, edges, ordered = [], [], []
    for flip in range(plane_count):
        part, tip, sorted_rows = call(
            functools.partial(residual_kernel, flip), "residual",
            [(here * frames, width), (edge, width), (here, frames, LANES)],
            1, 3 + wide, 500000000, 2 * mib,
            scratch=[pltpu.VMEM((wide, share * frames, names), BF16)],
        )(place, filtered[flip], code, flat_templates, *[passed[flip][k] for k in range(wide)])
        residual.append(part)
        edges.append(tip)
        ordered.append(sorted_rows)

    outer = plane ^ jnp.where(rep == 0, plane_count - 1, 0)
    tip = edges[0]
    for flip in range(1, plane_count):
        tip = jnp.where(outer == flip, edges[flip], tip)
    tip = exchange(tip, "rep", 1)

    foot_share = support.shape[1] // plane_count
    in_order = []
    for q in range(plane_count):
        rows_q = ordered[0]
        for flip in range(1, plane_count):
            rows_q = jnp.where(plane ^ q == flip, ordered[flip], rows_q)
        in_order.append(rows_q)
    mine = lax.dynamic_slice_in_dim(jnp.concatenate(in_order), plane * foot_share, foot_share, 2)
    trace_out = jnp.transpose(mine, (2, 1, 0))

    back_projected = pl.pallas_call(
        functools.partial(backward_kernel, plane_count),
        out_shape=shaped(movie_frames.shape),
        in_specs=[SMEM] + [VMEM] * (3 + plane_count),
        out_specs=HBM,
        scratch_shapes=[
            pltpu.VMEM(((rows + 2 * BLOCK) * frames, width), BF16),
            pltpu.VMEM(movie_frames.shape, BF16),
            pltpu.SemaphoreType.DMA((rows // BLOCK,)),
        ],
        compiler_params=pltpu.CompilerParams(vmem_limit_bytes=32 * mib),
        cost_estimate=pl.CostEstimate(flops=1000000000, bytes_accessed=3 * mib, transcendentals=0),
        name="backward",
    )(place, tip, col_adj, row_adj, *residual)
    return trace_out, back_projected


def solution(mesh):
    return jax.shard_map(
        on_device,
        mesh=mesh,
        in_specs=(
            P("planes", ("groups", "wide"), "rep", None),
            P("rep", None),
            P("rep", None),
            P("rep", None),
            P(None, "planes", None),
            P(),
            P(),
            P("wide", None, None),
            P("wide", None),
        ),
        out_specs=(
            P("planes", ("groups", "wide"), "rep"),
            P("planes", ("groups", "wide"), "rep", None),
        ),
        check_vma=False,
    )
```

```python
import functools

import jax
import jax.numpy as jnp
from jax import lax
from jax.experimental import pallas as pl
from jax.experimental.pallas import tpu as pltpu
from jax.sharding import PartitionSpec as P

BLOCK = 16
LANES = 128
F32 = jnp.float32
BF16 = jnp.bfloat16
REP, PLANE, WIDE = 0, 1, 2


def exchange(cells, axis, flip):
    count = lax.axis_size(axis)
    return lax.ppermute(cells, axis, [(i, i ^ flip) for i in range(count)])


def crossed(cells, plane_flip, wide_flip):
    count, size = lax.axis_size("planes"), lax.axis_size("wide")
    pairs = [
        (w * count + p, (w ^ wide_flip) * count + (p ^ plane_flip))
        for w in range(size)
        for p in range(count)
    ]
    return lax.ppermute(cells, ("wide", "planes"), pairs)


def iota(shape, dim):
    return lax.broadcasted_iota(jnp.int32, shape, dim)


def tap_row(taps_ref, place):
    lane = iota((8, LANES), 1)
    row = jnp.zeros((8, LANES), F32)
    for k in range(taps_ref.shape[0]):
        row = jnp.where(lane == place(k) % LANES, taps_ref[k], row)
    return row[:1]


def toeplitz(row, count, shift=0):
    return pltpu.roll(
        jnp.broadcast_to(row, (count, row.shape[1])), shift, 1, stride=1, stride_axis=0
    )


def column_band(taps_ref, rim, sign):
    rolled = toeplitz(tap_row(taps_ref, lambda k: sign * (k - rim)), LANES)
    gap = iota((LANES, LANES), 1) - iota((LANES, LANES), 0)
    return jnp.where(jnp.abs(gap) <= rim, rolled, 0.0).astype(BF16)


def row_band_forward(taps_ref, rim, frames):
    out_rows, depth, span = BLOCK * frames, 3 * BLOCK * frames, 3 * BLOCK
    band = toeplitz(tap_row(taps_ref, lambda k: k + BLOCK - rim), BLOCK)[:, :span].astype(BF16)
    left = (iota((out_rows, BLOCK), 0) // frames == iota((out_rows, BLOCK), 1)).astype(BF16)
    right = (lax.rem(iota((span, depth), 1), span) == iota((span, depth), 0)).astype(BF16)
    tall = jnp.dot(left, band, preferred_element_type=F32).astype(BF16)
    spread = jnp.dot(tall, right, preferred_element_type=F32)
    start = iota((out_rows, depth), 1) - span * lax.rem(iota((out_rows, depth), 0), frames)
    return jnp.where((start >= 0) & (start < span), spread, 0.0).astype(BF16)


def row_band_adjoint(taps_ref, rim, frames):
    out_rows, depth, span = BLOCK * frames, 3 * BLOCK * frames, 3 * BLOCK
    band = toeplitz(tap_row(taps_ref, lambda k: BLOCK + rim - k), BLOCK)[:, :span].astype(BF16)
    left = (lax.rem(iota((out_rows, BLOCK), 0), BLOCK) == iota((out_rows, BLOCK), 1)).astype(BF16)
    right = (iota((span, depth), 1) // frames == iota((span, depth), 0)).astype(BF16)
    tall = jnp.dot(left, band, preferred_element_type=F32).astype(BF16)
    spread = jnp.dot(tall, right, preferred_element_type=F32)
    same = lax.rem(iota((out_rows, depth), 1), frames) == iota((out_rows, depth), 0) // BLOCK
    return jnp.where(same, spread, 0.0).astype(BF16)


def half_of(place_ref, flip, far, wide):
    return (place_ref[PLANE] ^ flip) * 2 + ((place_ref[WIDE] // (wide // 2)) ^ far)


def per_frame(rows, frames, copies):
    tall = jnp.broadcast_to(rows[:, None, :], (BLOCK, frames, LANES)).reshape(BLOCK * frames, LANES)
    return tall if copies == 1 else jnp.concatenate([tall] * copies, axis=1)


def prepare_kernel(
    rim, cuts, col_hbm, row_hbm, movie_hbm, mask_hbm, support_hbm, templates_hbm,
    smooth_ref, col_fwd_ref, row_fwd_ref, code_ref, templates_ref, flat_ref,
    movie_ref, mask_ref, support_ref, packed_ref, loose_ref, col_ref, row_ref, sems,
):
    planes, frames, rows, _ = movie_ref.shape
    some = frames // cuts

    def fetch(n, source, target):
        copy = pltpu.make_async_copy(source, target, sems.at[n])
        copy.start()
        return copy

    tap_copies = [fetch(0, col_hbm, col_ref), fetch(1, row_hbm, row_ref)]
    movie_copies = []
    for n in range(planes * cuts):
        piece = (n // cuts, pl.ds(n % cuts * some, some))
        movie_copies.append(fetch(5 + n, movie_hbm.at[piece], movie_ref.at[piece]))
    packed_copy = fetch(2, templates_hbm, packed_ref)
    code_copies = [fetch(3, mask_hbm, mask_ref), fetch(4, support_hbm, support_ref)]
    for copy in tap_copies:
        copy.wait()
    col_fwd = column_band(col_ref, rim, -1)
    col_fwd_ref[...] = col_fwd
    row_fwd_ref[...] = row_band_forward(row_ref, rim, frames)
    for n, copy in enumerate(movie_copies):
        p, first = n // cuts, n % cuts * some
        copy.wait()
        full = jnp.dot(
            movie_ref[p, first : first + some].reshape(some * rows, LANES), col_fwd,
            preferred_element_type=F32,
        )
        smooth_ref[first : first + some, BLOCK : BLOCK + rows, p * LANES : (p + 1) * LANES] = (
            full.astype(BF16).reshape(some, rows, LANES)
        )
    packed_copy.wait()
    loose_ref[...] = packed_ref[...].astype(F32)
    unit = (iota((LANES, LANES), 0) == iota((LANES, LANES), 1)).astype(BF16)
    for p in range(planes):
        shapes = loose_ref[pl.ds(p, templates_ref.shape[1], stride=planes), :].astype(BF16)
        flat_ref[:, p * LANES : (p + 1) * LANES] = shapes
        templates_ref[p * LANES : (p + 1) * LANES, :] = lax.dot_general(
            unit, shapes, (((1,), (1,)), ((), ())), preferred_element_type=F32
        ).astype(BF16)
    for copy in code_copies:
        copy.wait()
    code_ref[...] = support_ref[...] * 2 + mask_ref[...]


def forward_kernel(
    flip, far, fill, wide, ks, place_ref, smooth_in_ref, edge_ref, col_fwd_ref, row_fwd_ref, code_ref,
    templates_ref, smooth_ref, filtered_ref, out_ref, projected_ref,
):
    frames, padded_rows, width = smooth_ref.shape
    planes, rows = width // LANES, padded_rows - 2 * BLOCK
    if fill:
        for p in range(planes):
            edge = jnp.dot(
                edge_ref[p].reshape(frames * BLOCK, LANES), col_fwd_ref[...],
                preferred_element_type=F32,
            ).reshape(frames, BLOCK, LANES)
            lanes = slice(p * LANES, (p + 1) * LANES)
            above = jnp.where(place_ref[REP] > 0, edge, 0.0).astype(BF16)
            below = jnp.where(place_ref[REP] > 0, 0.0, edge).astype(BF16)
            smooth_ref[:, :BLOCK, lanes] = above
            smooth_ref[:, BLOCK + rows :, lanes] = below
    here = filtered_ref.shape[0] // frames
    first = half_of(place_ref, flip, far, wide) * here
    tiles = templates_ref.shape[1] // LANES
    def along(b):
        near = smooth_ref[:, pl.ds(pl.multiple_of(first + b * BLOCK, BLOCK), 3 * BLOCK), :]
        near = near.reshape(frames * 3 * BLOCK, width)
        return jnp.dot(row_fwd_ref[...], near, preferred_element_type=F32)

    cells = along(0)
    for b in range(here // BLOCK):
        code = code_ref[pl.ds(pl.multiple_of(first + b * BLOCK, BLOCK), BLOCK), :]
        mask = per_frame((code & 1).astype(F32), frames, planes)
        filtered = (cells * mask).astype(BF16)
        spot = slice(b * BLOCK * frames, (b + 1) * BLOCK * frames)
        filtered_ref[spot, :] = filtered
        dense = jnp.dot(filtered, templates_ref[...], preferred_element_type=F32)
        cells = along(b + 1) if b + 1 < here // BLOCK else None
        picked = per_frame(code >> 1, frames, 1)
        lane, tile = picked & (LANES - 1), picked // LANES
        chosen = jnp.zeros(picked.shape, F32)
        for t in range(tiles):
            found = jnp.take_along_axis(
                dense[:, t * LANES : (t + 1) * LANES], lane, axis=1, mode="promise_in_bounds"
            )
            chosen = jnp.where(tile == t, found, chosen)
        projected_ref[spot, :] = chosen.astype(BF16)
    size = out_ref.shape[0] // len(ks)
    for i, k in enumerate(ks):
        start = pl.multiple_of(((place_ref[WIDE] ^ k) & (wide // 2 - 1)) * size, size)
        out_ref[i * size : (i + 1) * size, :] = projected_ref[pl.ds(start, size), :]


def add_all(parts, spots, rows):
    total = None
    for part, spot in zip(parts, spots):
        term = part[spot * rows : (spot + 1) * rows, :].astype(F32)
        total = term if total is None else total + term
    return total.astype(BF16)


def sum_kernel(spots, lag_ref, *refs):
    parts, out_ref = refs[:-1], refs[-1]
    rows = out_ref.shape[0] - lag_ref.shape[0]
    out_ref[:rows, :] = add_all(parts, spots, rows)
    out_ref[rows:, :] = lag_ref[...]


def mix_kernel(wide, spots, place_ref, owner_ref, lag_ref, *refs):
    parts, refs = refs[: len(spots)], refs[len(spots) :]
    blocks, outs = refs[: wide - 1], refs[wide - 1 : 2 * wide - 1]
    cells_ref, kernels_ref, traces_ref, tables_ref = refs[2 * wide - 1 :]
    _, share, frames, lanes = cells_ref.shape
    total = wide * frames
    here = place_ref[WIDE]
    cells_ref[here] = add_all(parts, spots, share * frames).reshape(share, frames, lanes)
    kernels_ref[here] = lag_ref[...].astype(F32)
    for k, block in enumerate(blocks, 1):
        cells_ref[here ^ k] = block[: share * frames, :].reshape(share, frames, lanes)
        kernels_ref[here ^ k] = block[share * frames :, :].astype(F32)

    def table(values):
        row = jnp.concatenate([values[i : i + 1, :] for i in range(2 * total // LANES)], axis=1)
        return toeplitz(row, total, total + 1)[:, :total].astype(BF16)

    if wide <= share:
        for d in range(wide):
            tables_ref[d] = table(kernels_ref[d])
    first = (place_ref[PLANE] * wide + here) * share
    for h in range(share):
        owner = owner_ref[first + h]
        lag = tables_ref[owner] if wide <= share else table(kernels_ref[owner])
        mixed = jnp.dot(lag, cells_ref[:, h].reshape(total, lanes), preferred_element_type=F32)
        traces_ref[:, h] = jnp.maximum(mixed, 0.0).astype(BF16).reshape(wide, frames, lanes)
    for k, out_ref in enumerate(outs):
        out_ref[...] = traces_ref[here ^ k]


def bands_kernel(rim, frames, col_ref, row_ref, col_adj_ref, row_adj_ref):
    band = column_band(col_ref, rim, 1)
    col_adj_ref[...] = jnp.zeros_like(col_adj_ref)
    for p in range(col_adj_ref.shape[0] // LANES):
        lanes = slice(p * LANES, (p + 1) * LANES)
        col_adj_ref[lanes, lanes] = band
    row_adj_ref[...] = row_band_adjoint(row_ref, rim, frames)


def residual_kernel(flip, far, wide, spots, place_ref, filtered_ref, code_ref, templates_ref, *refs):
    traces, (out_ref, edge_ref, ordered_ref, slots_ref) = refs[:-4], refs[-4:]
    _, frames, lanes = traces[0].shape
    share = ordered_ref.shape[0] // len(spots)
    names, width = templates_ref.shape
    tile = 2 * LANES
    base = half_of(place_ref, flip, far, wide) * len(spots) * share
    marks = iota((lanes, tile), 1).astype(F32).astype(BF16)
    group = min(8, share)
    for n, (k, source, offset) in enumerate(spots):
        block = (place_ref[WIDE] ^ k) & (wide // 2 - 1)
        source, offset = traces[source], offset * share
        top = base + block * share
        for g in range(share // group):
            support = code_ref[pl.ds(top + g * group, group), :] >> 1
            support = jnp.concatenate([support] * (8 // group), axis=0)
            columns = [
                jnp.transpose(
                    jnp.where(support // tile == t, support & (tile - 1), -1).astype(F32)
                )
                for t in range(names // tile)
            ]
            for i in range(group):
                h = g * group + i
                hits = jnp.concatenate(
                    [
                        jnp.where(
                            marks
                            == jnp.broadcast_to(column[:, i : i + 1], (lanes, tile)).astype(BF16),
                            jnp.ones((), BF16), jnp.zeros((), BF16),
                        )
                        for column in columns
                    ],
                    axis=1,
                )
                slots_ref[n, h * frames : (h + 1) * frames, :] = jnp.dot(
                    source[offset + h], hits, preferred_element_type=F32
                ).astype(BF16)
        model = jnp.dot(slots_ref[n], templates_ref[...], preferred_element_type=F32)
        mask = (code_ref[pl.ds(top, share), :] & 1).astype(F32)
        mask = jnp.broadcast_to(mask[:, None, :], (share, frames, lanes)).reshape(-1, lanes)
        size = share * frames
        spot = pl.ds(pl.multiple_of(block * size, size), size)
        out_ref[spot, :] = (
            filtered_ref[spot, :].astype(F32)
            - jnp.concatenate([mask] * (width // lanes), axis=1) * model
        ).astype(BF16)
        ordered_ref[pl.ds(block * share, share)] = source[offset : offset + share]
    edge = edge_ref.shape[0]
    start = jnp.where(place_ref[REP] > 0, 0, out_ref.shape[0] - edge)
    edge_ref[...] = out_ref[pl.ds(pl.multiple_of(start, edge), edge), :]


def backward_kernel(keys, wide, place_ref, edge_ref, col_adj_ref, row_adj_ref, *refs):
    parts, (out_hbm, padded_ref, out_ref, sems) = refs[: len(keys)], refs[len(keys) :]
    planes, frames, rows, _ = out_ref.shape
    edge, size = BLOCK * frames, parts[0].shape[0]
    zero = jnp.zeros_like(edge_ref)
    padded_ref[:edge, :] = jnp.where(place_ref[REP] > 0, edge_ref[...], zero)
    padded_ref[edge + rows * frames :, :] = jnp.where(place_ref[REP] > 0, zero, edge_ref[...])
    for (flip, far), part in zip(keys, parts):
        spot = pl.multiple_of(edge + half_of(place_ref, flip, far, wide) * size, edge)
        padded_ref[pl.ds(spot, size), :] = part[...]
    def along(b):
        near = padded_ref[b * edge : (b + 3) * edge, :]
        return jnp.dot(row_adj_ref[...], near, preferred_element_type=F32).astype(BF16)

    copies = []
    back = along(0)
    for b in range(rows // BLOCK):
        ahead = along(b + 1) if b + 1 < rows // BLOCK else None
        full = jnp.dot(back, col_adj_ref[...], preferred_element_type=F32).astype(BF16)
        for p in range(planes):
            out_ref[p, :, b * BLOCK : (b + 1) * BLOCK, :] = full[
                :, p * LANES : (p + 1) * LANES
            ].reshape(frames, BLOCK, LANES)
        piece = (slice(None), slice(None), pl.ds(b * BLOCK, BLOCK))
        copy = pltpu.make_async_copy(out_ref.at[piece], out_hbm.at[piece], sems.at[b])
        copy.start()
        copies.append(copy)
        back = ahead
    for copy in copies:
        copy.wait()


VMEM = pl.BlockSpec(memory_space=pltpu.VMEM)
SMEM = pl.BlockSpec(memory_space=pltpu.SMEM)
HBM = pl.BlockSpec(memory_space=pltpu.HBM)


def shaped(shape):
    return jax.ShapeDtypeStruct(shape, BF16)


def call(kernel, name, outs, smem, vmem, scratch=(), aliases=None):
    return pl.pallas_call(
        kernel,
        out_shape=tuple(shaped(s) if isinstance(s, tuple) else s for s in outs),
        in_specs=[SMEM] * smem + [VMEM] * vmem,
        out_specs=(VMEM,) * len(outs),
        scratch_shapes=scratch,
        input_output_aliases=aliases or {},
        compiler_params=pltpu.CompilerParams(vmem_limit_bytes=32 * 1024 * 1024),
        name=name,
    )


def lag_kernel_values(gains, lags, frame_count):
    taps = gains.shape[1]
    lag_values = jnp.arange(2 * frame_count, dtype=jnp.int32) - (frame_count - 1)
    offsets = jnp.arange(taps, dtype=jnp.int32) - (taps - 1) // 2
    hits = lag_values[None, :, None] == lags[:, None, None] * offsets[None, None, :]
    spread = jnp.where(hits, gains[:, None, :], jnp.zeros((), gains.dtype))
    return jnp.sum(spread, axis=(0, 2)).astype(BF16)


def on_device(
    movie_frames, pixel_mask, tile_owner, support, templates, row_taps, col_taps, lag_gains, dilations
):
    planes, frames, rows, cols = movie_frames.shape
    wide, plane_count = lax.axis_size("wide"), lax.axis_size("planes")
    rim = (row_taps.shape[0] - 1) // 2
    total_frames, width = frames * wide, planes * cols
    here = rows // plane_count
    share = here // wide
    edge = BLOCK * frames
    rep, plane, spot = lax.axis_index("rep"), lax.axis_index("planes"), lax.axis_index("wide")
    place = jnp.stack([rep, plane, spot]).astype(jnp.int32)
    mib = 1 << 20

    start = jnp.where(rep == 0, rows - BLOCK, 0)
    rim_rows = exchange(lax.dynamic_slice_in_dim(movie_frames, start, BLOCK, axis=2), "rep", 1)
    cuts = 2
    depth, names = 3 * BLOCK * frames, templates.shape[0]
    smooth, col_fwd, row_fwd, code, tall_templates, flat_templates = pl.pallas_call(
        functools.partial(prepare_kernel, rim, cuts),
        out_shape=(
            shaped((frames, rows + 2 * BLOCK, width)), shaped((cols, cols)), shaped((edge, depth)),
            jax.ShapeDtypeStruct(support.shape, jnp.int32), shaped((width, names)),
            shaped((names, width)),
        ),
        in_specs=[HBM] * 6,
        out_specs=(VMEM,) * 6,
        scratch_shapes=[
            pltpu.VMEM(movie_frames.shape, BF16),
            pltpu.VMEM(pixel_mask.shape, jnp.int32),
            pltpu.VMEM(support.shape, jnp.int32),
            pltpu.VMEM((names * planes, cols), BF16),
            pltpu.VMEM((names * planes, cols), F32),
            pltpu.SMEM(col_taps.shape, F32),
            pltpu.SMEM(row_taps.shape, F32),
            pltpu.SemaphoreType.DMA((5 + planes * cuts,)),
        ],
        compiler_params=pltpu.CompilerParams(vmem_limit_bytes=32 * mib),
        name="prepare",
    )(
        *[
            pltpu.with_memory_space_constraint(x, pltpu.HBM)
            for x in (
                col_taps, row_taps, movie_frames, pixel_mask, support,
                templates.reshape(names * planes, cols),
            )
        ]
    )

    near_ks, far_ks = list(range(wide // 2)), list(range(wide // 2, wide))
    halves = {1: far_ks, 0: near_ks[::-1]}
    half_rows = here // 2
    filtered, projected = {}, {}
    keys = [((turn + 1) % plane_count, far) for turn in range(plane_count) for far in (0, 1)]
    for turn, (flip, far) in enumerate(keys):
        smooth, filtered[flip, far], mine = call(
            functools.partial(forward_kernel, flip, far, turn == 0, wide, halves[far]), "forward",
            [smooth.shape, (half_rows * frames, width), (half_rows * frames, LANES)],
            1, 6, aliases={1: 0},
            scratch=[pltpu.VMEM((half_rows * frames, LANES), BF16)],
        )(place, smooth, rim_rows, col_fwd, row_fwd, code, tall_templates)
        projected[flip, far] = exchange(mine, "planes", flip) if flip else mine
        if turn == 0:
            gains, lags, _ = lax.optimization_barrier((lag_gains, dilations, smooth))
            kernel_row = lag_kernel_values(gains[0], lags[0], total_frames)
            lag_rows = -(-2 * total_frames // (LANES * BLOCK)) * BLOCK
            kernel_row = jnp.pad(kernel_row, (0, lag_rows * LANES - 2 * total_frames))
            kernel_row = kernel_row.reshape(lag_rows, LANES)

    block_rows = share * frames + lag_rows
    sums, blocks = {}, {}

    def parts_of(k):
        far = int(k in far_ks)
        spots = [halves[far].index(k)] * plane_count
        return spots, [projected[flip, far] for flip in range(plane_count)]

    for k in near_ks[1:] + far_ks:
        spots, parts = parts_of(k)
        (sums[k],) = call(
            functools.partial(sum_kernel, spots), "sum", [(block_rows, LANES)],
            0, 1 + plane_count,
        )(kernel_row, *parts)
        blocks[k] = exchange(sums[k], "wide", k)

    late_col, late_row, _ = lax.optimization_barrier(
        (col_taps, row_taps, list(sums.values()))
    )
    col_adj, row_adj = call(
        functools.partial(bands_kernel, rim, frames), "bands", [(width, width), (edge, depth)],
        2, 0,
    )(late_col, late_row)
    own_spots, own_parts = parts_of(0)
    own_parts[0], col_adj, row_adj = lax.optimization_barrier((own_parts[0], col_adj, row_adj))

    cell_shape = (wide, share, frames, LANES)
    tables = (wide, total_frames, total_frames) if wide <= share else (1, BLOCK, LANES)
    traces = call(
        functools.partial(mix_kernel, wide, own_spots), "mix", [cell_shape[1:]] * wide,
        2, wide + plane_count,
        scratch=[
            pltpu.VMEM(cell_shape, BF16), pltpu.VMEM((wide, lag_rows, LANES), F32),
            pltpu.VMEM(cell_shape, BF16), pltpu.VMEM(tables, BF16),
        ],
    )(
        place, tile_owner[:, 0], kernel_row, *own_parts, *[blocks[k] for k in range(1, wide)],
    )
    swapped = {k: exchange(traces[k], "wide", k) for k in far_ks + near_ks[1:]}
    swapped[0] = traces[0]
    late = range(1, plane_count)
    direct = {flip: [crossed(traces[k], flip, k) for k in near_ks] for flip in late}

    residual, edges, ordered = {}, {}, {}
    back_keys = [(flip, far) for flip in range(plane_count) for far in (0, 1)]

    def subtract(flip, far, groups, got):
        spots = [(k, n, i) for n, ks in enumerate(groups) for i, k in enumerate(ks)]
        residual[flip, far], edges[flip, far], ordered[flip, far] = call(
            functools.partial(residual_kernel, flip, far, wide, spots), "residual",
            [(half_rows * frames, width), (edge, width), (half_rows, frames, LANES)],
            1, 3 + len(got), scratch=[pltpu.VMEM((len(spots), share * frames, names), BF16)],
        )(place, filtered[flip, far], code, flat_templates, *got)

    subtract(0, 0, [[k] for k in near_ks], [swapped[k] for k in near_ks])
    distant, direct, _ = lax.optimization_barrier(
        ([swapped[k] for k in far_ks], direct, edges[0, 0])
    )
    joined = jnp.concatenate(distant)
    subtract(0, 1, [[k] for k in far_ks], distant)
    for flip in late:
        subtract(flip, 0, [[k] for k in near_ks], direct[flip])
        subtract(flip, 1, [far_ks], [exchange(joined, "planes", flip)])

    def pick(table, part, half):
        found = table[0, 0]
        for flip, far in back_keys[1:]:
            here_it_is = ((plane ^ part) == flip) & ((spot // (wide // 2) ^ half) == far)
            found = jnp.where(here_it_is, table[flip, far], found)
        return found

    tip = pick(edges, jnp.where(rep == 0, plane_count - 1, 0), jnp.where(rep == 0, 1, 0))
    tip = exchange(tip, "rep", 1)

    foot_share = support.shape[1] // plane_count
    in_order = [pick(ordered, q, half) for q in range(plane_count) for half in (0, 1)]
    mine = lax.dynamic_slice_in_dim(jnp.concatenate(in_order), plane * foot_share, foot_share, 2)
    trace_out = jnp.transpose(mine, (2, 1, 0))

    back_projected = pl.pallas_call(
        functools.partial(backward_kernel, back_keys, wide),
        out_shape=shaped(movie_frames.shape),
        in_specs=[SMEM] + [VMEM] * (3 + len(back_keys)),
        out_specs=HBM,
        scratch_shapes=[
            pltpu.VMEM(((rows + 2 * BLOCK) * frames, width), BF16),
            pltpu.VMEM(movie_frames.shape, BF16),
            pltpu.SemaphoreType.DMA((rows // BLOCK,)),
        ],
        compiler_params=pltpu.CompilerParams(vmem_limit_bytes=32 * mib),
        name="backward",
    )(place, tip, col_adj, row_adj, *[residual[key] for key in back_keys])
    return trace_out, back_projected


def solution(mesh):
    return jax.shard_map(
        on_device,
        mesh=mesh,
        in_specs=(
            P("planes", ("groups", "wide"), "rep", None),
            P("rep", None),
            P("rep", None),
            P("rep", None),
            P(None, "planes", None),
            P(),
            P(),
            P("wide", None, None),
            P("wide", None),
        ),
        out_specs=(
            P("planes", ("groups", "wide"), "rep"),
            P("planes", ("groups", "wide"), "rep", None),
        ),
        check_vma=False,
    )
```

```python
import functools

import jax
import jax.numpy as jnp
from jax import lax
from jax.experimental import pallas as pl
from jax.experimental.pallas import tpu as pltpu
from jax.sharding import PartitionSpec as P

BLOCK = 16
LANES = 128
F32 = jnp.float32
BF16 = jnp.bfloat16
REP, PLANE, WIDE = "rep", "planes", "wide"


def exchange(cells, axis, flip):
    count = lax.axis_size(axis)
    return lax.ppermute(cells, axis, [(i, i ^ flip) for i in range(count)])


def crossed(cells, plane_flip, wide_flip):
    count, size = lax.axis_size("planes"), lax.axis_size("wide")
    pairs = [
        (w * count + p, (w ^ wide_flip) * count + (p ^ plane_flip))
        for w in range(size)
        for p in range(count)
    ]
    return lax.ppermute(cells, ("wide", "planes"), pairs)


def iota(shape, dim):
    return lax.broadcasted_iota(jnp.int32, shape, dim)


def tap_row(taps_ref, place):
    lane = iota((8, LANES), 1)
    row = jnp.zeros((8, LANES), F32)
    for k in range(taps_ref.shape[0]):
        row = jnp.where(lane == place(k) % LANES, taps_ref[k], row)
    return row[:1]


def quotient(x, n):
    if n & (n - 1) == 0:
        return lax.shift_right_logical(x, n.bit_length() - 1)
    return lax.shift_right_logical(x * (65536 // n + 1), 16)


def remainder(x, n):
    return x & (n - 1) if n & (n - 1) == 0 else x - n * quotient(x, n)


def toeplitz(row, count, shift=0):
    return pltpu.roll(
        jnp.broadcast_to(row, (count, row.shape[1])), shift, 1, stride=1, stride_axis=0
    )


def column_band(taps_ref, rim, sign):
    rolled = toeplitz(tap_row(taps_ref, lambda k: sign * (k - rim)), LANES)
    gap = iota((LANES, LANES), 1) - iota((LANES, LANES), 0)
    return jnp.where(jnp.abs(gap) <= rim, rolled, 0.0).astype(BF16)


def row_band_forward(taps_ref, rim, frames):
    out_rows, depth, span = BLOCK * frames, 3 * BLOCK * frames, 3 * BLOCK
    band = toeplitz(tap_row(taps_ref, lambda k: k + BLOCK - rim), BLOCK)[:, :span].astype(BF16)
    left = (quotient(iota((out_rows, BLOCK), 0), frames) == iota((out_rows, BLOCK), 1)).astype(BF16)
    right = (remainder(iota((span, depth), 1), span) == iota((span, depth), 0)).astype(BF16)
    tall = jnp.dot(left, band, preferred_element_type=F32).astype(BF16)
    spread = jnp.dot(tall, right, preferred_element_type=F32)
    start = iota((out_rows, depth), 1) - span * remainder(iota((out_rows, depth), 0), frames)
    return jnp.where((start >= 0) & (start < span), spread, 0.0).astype(BF16)


def row_band_adjoint(taps_ref, rim, frames):
    out_rows, depth, span = BLOCK * frames, 3 * BLOCK * frames, 3 * BLOCK
    band = toeplitz(tap_row(taps_ref, lambda k: BLOCK + rim - k), BLOCK)[:, :span].astype(BF16)
    left = (remainder(iota((out_rows, BLOCK), 0), BLOCK) == iota((out_rows, BLOCK), 1)).astype(BF16)
    right = (quotient(iota((span, depth), 1), frames) == iota((span, depth), 0)).astype(BF16)
    tall = jnp.dot(left, band, preferred_element_type=F32).astype(BF16)
    spread = jnp.dot(tall, right, preferred_element_type=F32)
    same = remainder(iota((out_rows, depth), 1), frames) == quotient(iota((out_rows, depth), 0), BLOCK)
    return jnp.where(same, spread, 0.0).astype(BF16)


def half_of(flip, far, wide):
    return (lax.axis_index(PLANE) ^ flip) * 2 + (quotient(lax.axis_index(WIDE), wide // 2) ^ far)


def per_frame(rows, frames, copies):
    tall = jnp.broadcast_to(rows[:, None, :], (BLOCK, frames, LANES)).reshape(BLOCK * frames, LANES)
    return tall if copies == 1 else jnp.concatenate([tall] * copies, axis=1)


def prepare_kernel(
    rim, cuts, col_hbm, row_hbm, movie_hbm, mask_hbm, support_hbm, templates_hbm,
    smooth_ref, col_fwd_ref, row_fwd_ref, code_ref, templates_ref, flat_ref,
    movie_ref, mask_ref, support_ref, packed_ref, loose_ref, col_ref, row_ref, sems,
):
    planes, frames, rows, _ = movie_ref.shape
    some = frames // cuts

    def fetch(n, source, target):
        copy = pltpu.make_async_copy(source, target, sems.at[n])
        copy.start()
        return copy

    tap_copies = [fetch(0, col_hbm, col_ref), fetch(1, row_hbm, row_ref)]
    movie_copies = []
    for n in range(planes * cuts):
        piece = (n // cuts, pl.ds(n % cuts * some, some))
        movie_copies.append(fetch(5 + n, movie_hbm.at[piece], movie_ref.at[piece]))
    packed_copy = fetch(2, templates_hbm, packed_ref)
    code_copies = [fetch(3, mask_hbm, mask_ref), fetch(4, support_hbm, support_ref)]
    for copy in tap_copies:
        copy.wait()
    col_fwd = column_band(col_ref, rim, -1)
    col_fwd_ref[...] = col_fwd
    row_fwd_ref[...] = row_band_forward(row_ref, rim, frames)
    for n, copy in enumerate(movie_copies):
        p, first = n // cuts, n % cuts * some
        copy.wait()
        full = jnp.dot(
            movie_ref[p, first : first + some].reshape(some * rows, LANES), col_fwd,
            preferred_element_type=F32,
        )
        smooth_ref[first : first + some, BLOCK : BLOCK + rows, p * LANES : (p + 1) * LANES] = (
            full.astype(BF16).reshape(some, rows, LANES)
        )
    packed_copy.wait()
    loose_ref[...] = packed_ref[...].astype(F32)
    unit = (iota((LANES, LANES), 0) == iota((LANES, LANES), 1)).astype(BF16)
    for p in range(planes):
        shapes = loose_ref[pl.ds(p, templates_ref.shape[1], stride=planes), :].astype(BF16)
        flat_ref[:, p * LANES : (p + 1) * LANES] = shapes
        templates_ref[p * LANES : (p + 1) * LANES, :] = lax.dot_general(
            unit, shapes, (((1,), (1,)), ((), ())), preferred_element_type=F32
        ).astype(BF16)
    for copy in code_copies:
        copy.wait()
    code_ref[...] = support_ref[...] * 2 + mask_ref[...]


def forward_kernel(
    flip, far, fill, wide, ks, smooth_in_ref, edge_ref, col_fwd_ref, row_fwd_ref, code_ref,
    templates_ref, smooth_ref, filtered_ref, out_ref, projected_ref,
):
    frames, padded_rows, width = smooth_ref.shape
    planes, rows = width // LANES, padded_rows - 2 * BLOCK
    if fill:
        for p in range(planes):
            edge = jnp.dot(
                edge_ref[p].reshape(frames * BLOCK, LANES), col_fwd_ref[...],
                preferred_element_type=F32,
            ).reshape(frames, BLOCK, LANES)
            lanes = slice(p * LANES, (p + 1) * LANES)
            above = jnp.where(lax.axis_index(REP) > 0, edge, 0.0).astype(BF16)
            below = jnp.where(lax.axis_index(REP) > 0, 0.0, edge).astype(BF16)
            smooth_ref[:, :BLOCK, lanes] = above
            smooth_ref[:, BLOCK + rows :, lanes] = below
    here = filtered_ref.shape[0] // frames
    first = half_of(flip, far, wide) * here
    tiles = templates_ref.shape[1] // LANES
    def along(b):
        near = smooth_ref[:, pl.ds(pl.multiple_of(first + b * BLOCK, BLOCK), 3 * BLOCK), :]
        near = near.reshape(frames * 3 * BLOCK, width)
        return jnp.dot(row_fwd_ref[...], near, preferred_element_type=F32)

    cells = along(0)
    for b in range(here // BLOCK):
        code = code_ref[pl.ds(pl.multiple_of(first + b * BLOCK, BLOCK), BLOCK), :]
        mask = per_frame((code & 1).astype(F32), frames, planes)
        filtered = (cells * mask).astype(BF16)
        spot = slice(b * BLOCK * frames, (b + 1) * BLOCK * frames)
        filtered_ref[spot, :] = filtered
        dense = jnp.dot(filtered, templates_ref[...], preferred_element_type=F32)
        cells = along(b + 1) if b + 1 < here // BLOCK else None
        picked = per_frame(code >> 1, frames, 1)
        lane, tile = picked & (LANES - 1), quotient(picked, LANES)
        chosen = jnp.zeros(picked.shape, F32)
        for t in range(tiles):
            found = jnp.take_along_axis(
                dense[:, t * LANES : (t + 1) * LANES], lane, axis=1, mode="promise_in_bounds"
            )
            chosen = jnp.where(tile == t, found, chosen)
        projected_ref[spot, :] = chosen.astype(BF16)
    size = out_ref.shape[0] // len(ks)
    for i, k in enumerate(ks):
        start = pl.multiple_of(((lax.axis_index(WIDE) ^ k) & (wide // 2 - 1)) * size, size)
        out_ref[i * size : (i + 1) * size, :] = projected_ref[pl.ds(start, size), :]


def add_all(parts, spots, rows):
    total = None
    for part, spot in zip(parts, spots):
        term = part[spot * rows : (spot + 1) * rows, :].astype(F32)
        total = term if total is None else total + term
    return total.astype(BF16)


def sum_kernel(spots, lag_ref, *refs):
    parts, out_ref = refs[:-1], refs[-1]
    rows = out_ref.shape[0] - lag_ref.shape[0]
    out_ref[:rows, :] = add_all(parts, spots, rows)
    out_ref[rows:, :] = lag_ref[...]


def mix_kernel(wide, spots, owner_ref, lag_ref, *refs):
    parts, refs = refs[: len(spots)], refs[len(spots) :]
    blocks, outs = refs[: wide - 1], refs[wide - 1 : 2 * wide - 1]
    cells_ref, kernels_ref, traces_ref = refs[2 * wide - 1 :]
    _, share, frames, lanes = cells_ref.shape
    total = wide * frames
    here = lax.axis_index(WIDE)
    cells_ref[here] = add_all(parts, spots, share * frames).reshape(share, frames, lanes)
    kernels_ref[here] = lag_ref[...].astype(F32)
    for k, block in enumerate(blocks, 1):
        cells_ref[here ^ k] = block[: share * frames, :].reshape(share, frames, lanes)
        kernels_ref[here ^ k] = block[share * frames :, :].astype(F32)
    first = (lax.axis_index(PLANE) * wide + here) * share
    owners = owner_ref[...]
    lane = iota(owners.shape, 1)
    for h in range(share):
        owner = jnp.sum(jnp.where(lane == first + h, owners, 0), axis=1, keepdims=True)
        owner = jnp.broadcast_to(owner, (8, lanes))
        row = []
        for i in range(0, kernels_ref.shape[1], 8):
            values = jnp.zeros((8, lanes), F32)
            for d in range(wide):
                values = jnp.where(owner == d, kernels_ref[d, i : i + 8, :], values)
            row += [values[n : n + 1, :] for n in range(8)]
        row = jnp.concatenate(row[: 2 * total // lanes], axis=1)
        lag = toeplitz(row, total, total + 1)[:, :total].astype(BF16)
        mixed = jnp.dot(lag, cells_ref[:, h].reshape(total, lanes), preferred_element_type=F32)
        traces_ref[:, h] = jnp.maximum(mixed, 0.0).astype(BF16).reshape(wide, frames, lanes)
    for k, out_ref in enumerate(outs):
        out_ref[...] = traces_ref[here ^ k]


def bands_kernel(rim, frames, col_ref, row_ref, col_adj_ref, row_adj_ref):
    band = column_band(col_ref, rim, 1)
    col_adj_ref[...] = jnp.zeros_like(col_adj_ref)
    for p in range(col_adj_ref.shape[0] // LANES):
        lanes = slice(p * LANES, (p + 1) * LANES)
        col_adj_ref[lanes, lanes] = band
    row_adj_ref[...] = row_band_adjoint(row_ref, rim, frames)


def residual_kernel(flip, far, wide, spots, filtered_ref, code_ref, templates_ref, *refs):
    traces, (out_ref, edge_ref, ordered_ref, slots_ref) = refs[:-4], refs[-4:]
    _, frames, lanes = traces[0].shape
    share = ordered_ref.shape[0] // len(spots)
    names, width = templates_ref.shape
    tile = 2 * LANES
    base = half_of(flip, far, wide) * len(spots) * share
    marks = iota((lanes, tile), 1).astype(F32).astype(BF16)
    group = min(8, share)
    for n, (k, source, offset) in enumerate(spots):
        block = (lax.axis_index(WIDE) ^ k) & (wide // 2 - 1)
        source, offset = traces[source], offset * share
        top = base + block * share
        for g in range(share // group):
            support = code_ref[pl.ds(top + g * group, group), :] >> 1
            support = jnp.concatenate([support] * (8 // group), axis=0)
            columns = [
                jnp.transpose(
                    jnp.where(quotient(support, tile) == t, support & (tile - 1), -1).astype(F32)
                )
                for t in range(names // tile)
            ]
            for i in range(group):
                h = g * group + i
                hits = jnp.concatenate(
                    [
                        jnp.where(
                            marks
                            == jnp.broadcast_to(column[:, i : i + 1], (lanes, tile)).astype(BF16),
                            jnp.ones((), BF16), jnp.zeros((), BF16),
                        )
                        for column in columns
                    ],
                    axis=1,
                )
                slots_ref[n, h * frames : (h + 1) * frames, :] = jnp.dot(
                    source[offset + h], hits, preferred_element_type=F32
                ).astype(BF16)
        model = jnp.dot(slots_ref[n], templates_ref[...], preferred_element_type=F32)
        mask = (code_ref[pl.ds(top, share), :] & 1).astype(F32)
        mask = jnp.broadcast_to(mask[:, None, :], (share, frames, lanes)).reshape(-1, lanes)
        size = share * frames
        spot = pl.ds(pl.multiple_of(block * size, size), size)
        out_ref[spot, :] = (
            filtered_ref[spot, :].astype(F32)
            - jnp.concatenate([mask] * (width // lanes), axis=1) * model
        ).astype(BF16)
        ordered_ref[pl.ds(block * share, share)] = source[offset : offset + share]
    edge = edge_ref.shape[0]
    start = jnp.where(lax.axis_index(REP) > 0, 0, out_ref.shape[0] - edge)
    edge_ref[...] = out_ref[pl.ds(pl.multiple_of(start, edge), edge), :]


def backward_kernel(keys, wide, edge_ref, col_adj_ref, row_adj_ref, *refs):
    parts, (out_hbm, padded_ref, out_ref, sems) = refs[: len(keys)], refs[len(keys) :]
    planes, frames, rows, _ = out_ref.shape
    edge, size = BLOCK * frames, parts[0].shape[0]
    zero = jnp.zeros_like(edge_ref)
    padded_ref[:edge, :] = jnp.where(lax.axis_index(REP) > 0, edge_ref[...], zero)
    padded_ref[edge + rows * frames :, :] = jnp.where(lax.axis_index(REP) > 0, zero, edge_ref[...])
    for (flip, far), part in zip(keys, parts):
        spot = pl.multiple_of(edge + half_of(flip, far, wide) * size, edge)
        padded_ref[pl.ds(spot, size), :] = part[...]
    def along(b):
        near = padded_ref[b * edge : (b + 3) * edge, :]
        return jnp.dot(row_adj_ref[...], near, preferred_element_type=F32).astype(BF16)

    copies = []
    back = along(0)
    for b in range(rows // BLOCK):
        ahead = along(b + 1) if b + 1 < rows // BLOCK else None
        full = jnp.dot(back, col_adj_ref[...], preferred_element_type=F32).astype(BF16)
        for p in range(planes):
            out_ref[p, :, b * BLOCK : (b + 1) * BLOCK, :] = full[
                :, p * LANES : (p + 1) * LANES
            ].reshape(frames, BLOCK, LANES)
        piece = (slice(None), slice(None), pl.ds(b * BLOCK, BLOCK))
        copy = pltpu.make_async_copy(out_ref.at[piece], out_hbm.at[piece], sems.at[b])
        copy.start()
        copies.append(copy)
        back = ahead
    for copy in copies:
        copy.wait()


VMEM = pl.BlockSpec(memory_space=pltpu.VMEM)
SMEM = pl.BlockSpec(memory_space=pltpu.SMEM)
HBM = pl.BlockSpec(memory_space=pltpu.HBM)


def shaped(shape):
    return jax.ShapeDtypeStruct(shape, BF16)


def call(kernel, name, outs, smem, vmem, scratch=(), aliases=None):
    return pl.pallas_call(
        kernel,
        out_shape=tuple(shaped(s) if isinstance(s, tuple) else s for s in outs),
        in_specs=[SMEM] * smem + [VMEM] * vmem,
        out_specs=(VMEM,) * len(outs),
        scratch_shapes=scratch,
        input_output_aliases=aliases or {},
        compiler_params=pltpu.CompilerParams(vmem_limit_bytes=32 * 1024 * 1024),
        name=name,
    )


def lag_kernel_values(gains, lags, frame_count):
    taps = gains.shape[1]
    lag_values = jnp.arange(2 * frame_count, dtype=jnp.int32) - (frame_count - 1)
    offsets = jnp.arange(taps, dtype=jnp.int32) - (taps - 1) // 2
    hits = lag_values[None, :, None] == lags[:, None, None] * offsets[None, None, :]
    spread = jnp.where(hits, gains[:, None, :], jnp.zeros((), gains.dtype))
    return jnp.sum(spread, axis=(0, 2)).astype(BF16)


def on_device(
    movie_frames, pixel_mask, tile_owner, support, templates, row_taps, col_taps, lag_gains, dilations
):
    planes, frames, rows, cols = movie_frames.shape
    wide, plane_count = lax.axis_size("wide"), lax.axis_size("planes")
    rim = (row_taps.shape[0] - 1) // 2
    total_frames, width = frames * wide, planes * cols
    here = rows // plane_count
    share = here // wide
    edge = BLOCK * frames
    rep, plane, spot = lax.axis_index("rep"), lax.axis_index("planes"), lax.axis_index("wide")
    mib = 1 << 20

    start = jnp.where(rep == 0, rows - BLOCK, 0)
    rim_rows = exchange(lax.dynamic_slice_in_dim(movie_frames, start, BLOCK, axis=2), "rep", 1)
    cuts = 2
    depth, names = 3 * BLOCK * frames, templates.shape[0]
    smooth, col_fwd, row_fwd, code, tall_templates, flat_templates = pl.pallas_call(
        functools.partial(prepare_kernel, rim, cuts),
        out_shape=(
            shaped((frames, rows + 2 * BLOCK, width)), shaped((cols, cols)), shaped((edge, depth)),
            jax.ShapeDtypeStruct(support.shape, jnp.int32), shaped((width, names)),
            shaped((names, width)),
        ),
        in_specs=[HBM] * 6,
        out_specs=(VMEM,) * 6,
        scratch_shapes=[
            pltpu.VMEM(movie_frames.shape, BF16),
            pltpu.VMEM(pixel_mask.shape, jnp.int32),
            pltpu.VMEM(support.shape, jnp.int32),
            pltpu.VMEM((names * planes, cols), BF16),
            pltpu.VMEM((names * planes, cols), F32),
            pltpu.SMEM(col_taps.shape, F32),
            pltpu.SMEM(row_taps.shape, F32),
            pltpu.SemaphoreType.DMA((5 + planes * cuts,)),
        ],
        compiler_params=pltpu.CompilerParams(vmem_limit_bytes=32 * mib),
        name="prepare",
    )(
        *[
            pltpu.with_memory_space_constraint(x, pltpu.HBM)
            for x in (
                col_taps, row_taps, movie_frames, pixel_mask, support,
                templates.reshape(names * planes, cols),
            )
        ]
    )

    near_ks, far_ks = list(range(wide // 2)), list(range(wide // 2, wide))
    halves = {1: far_ks, 0: near_ks[::-1]}
    half_rows = here // 2
    filtered, projected = {}, {}
    keys = [((turn + 1) % plane_count, far) for turn in range(plane_count) for far in (0, 1)]
    for turn, (flip, far) in enumerate(keys):
        smooth, filtered[flip, far], mine = call(
            functools.partial(forward_kernel, flip, far, turn == 0, wide, halves[far]), "forward",
            [smooth.shape, (half_rows * frames, width), (half_rows * frames, LANES)],
            0, 6, aliases={0: 0},
            scratch=[pltpu.VMEM((half_rows * frames, LANES), BF16)],
        )(smooth, rim_rows, col_fwd, row_fwd, code, tall_templates)
        projected[flip, far] = exchange(mine, "planes", flip) if flip else mine
        if turn == 0:
            gains, lags, _ = lax.optimization_barrier((lag_gains, dilations, smooth))
            kernel_row = lag_kernel_values(gains[0], lags[0], total_frames)
            lag_rows = -(-2 * total_frames // (LANES * BLOCK)) * BLOCK
            kernel_row = jnp.pad(kernel_row, (0, lag_rows * LANES - 2 * total_frames))
            kernel_row = kernel_row.reshape(lag_rows, LANES)

    block_rows = share * frames + lag_rows
    sums, blocks = {}, {}

    def parts_of(k):
        far = int(k in far_ks)
        spots = [halves[far].index(k)] * plane_count
        return spots, [projected[flip, far] for flip in range(plane_count)]

    for k in near_ks[1:] + far_ks:
        spots, parts = parts_of(k)
        (sums[k],) = call(
            functools.partial(sum_kernel, spots), "sum", [(block_rows, LANES)],
            0, 1 + plane_count,
        )(kernel_row, *parts)
        blocks[k] = exchange(sums[k], "wide", k)

    late_col, late_row, _ = lax.optimization_barrier(
        (col_taps, row_taps, list(sums.values()))
    )
    col_adj, row_adj = call(
        functools.partial(bands_kernel, rim, frames), "bands", [(width, width), (edge, depth)],
        2, 0,
    )(late_col, late_row)
    own_spots, own_parts = parts_of(0)
    own_parts[0], col_adj, row_adj = lax.optimization_barrier((own_parts[0], col_adj, row_adj))

    cell_shape = (wide, share, frames, LANES)
    traces = call(
        functools.partial(mix_kernel, wide, own_spots), "mix", [cell_shape[1:]] * wide,
        0, 1 + wide + plane_count,
        scratch=[
            pltpu.VMEM(cell_shape, BF16), pltpu.VMEM((wide, lag_rows, LANES), F32),
            pltpu.VMEM(cell_shape, BF16),
        ],
    )(
        tile_owner.reshape(1, rows), kernel_row, *own_parts, *[blocks[k] for k in range(1, wide)],
    )
    swapped = {k: exchange(traces[k], "wide", k) for k in far_ks + near_ks[1:]}
    swapped[0] = traces[0]
    late = range(1, plane_count)
    direct = {flip: [crossed(traces[k], flip, k) for k in near_ks] for flip in late}

    residual, edges, ordered = {}, {}, {}
    back_keys = [(flip, far) for flip in range(plane_count) for far in (0, 1)]

    def subtract(flip, far, groups, got):
        spots = [(k, n, i) for n, ks in enumerate(groups) for i, k in enumerate(ks)]
        residual[flip, far], edges[flip, far], ordered[flip, far] = call(
            functools.partial(residual_kernel, flip, far, wide, spots), "residual",
            [(half_rows * frames, width), (edge, width), (half_rows, frames, LANES)],
            0, 3 + len(got), scratch=[pltpu.VMEM((len(spots), share * frames, names), BF16)],
        )(filtered[flip, far], code, flat_templates, *got)

    subtract(0, 0, [[k] for k in near_ks], [swapped[k] for k in near_ks])
    distant, direct, _ = lax.optimization_barrier(
        ([swapped[k] for k in far_ks], direct, edges[0, 0])
    )
    joined = jnp.concatenate(distant)
    subtract(0, 1, [[k] for k in far_ks], distant)
    for flip in late:
        subtract(flip, 0, [[k] for k in near_ks], direct[flip])
        subtract(flip, 1, [far_ks], [exchange(joined, "planes", flip)])

    def pick(table, part, half):
        found = table[0, 0]
        for flip, far in back_keys[1:]:
            here_it_is = ((plane ^ part) == flip) & ((spot // (wide // 2) ^ half) == far)
            found = jnp.where(here_it_is, table[flip, far], found)
        return found

    tip = pick(edges, jnp.where(rep == 0, plane_count - 1, 0), jnp.where(rep == 0, 1, 0))
    tip = exchange(tip, "rep", 1)

    foot_share = support.shape[1] // plane_count
    in_order = [pick(ordered, q, half) for q in range(plane_count) for half in (0, 1)]
    mine = lax.dynamic_slice_in_dim(jnp.concatenate(in_order), plane * foot_share, foot_share, 2)
    trace_out = jnp.transpose(mine, (2, 1, 0))

    back_projected = pl.pallas_call(
        functools.partial(backward_kernel, back_keys, wide),
        out_shape=shaped(movie_frames.shape),
        in_specs=[VMEM] * (3 + len(back_keys)),
        out_specs=HBM,
        scratch_shapes=[
            pltpu.VMEM(((rows + 2 * BLOCK) * frames, width), BF16),
            pltpu.VMEM(movie_frames.shape, BF16),
            pltpu.SemaphoreType.DMA((rows // BLOCK,)),
        ],
        compiler_params=pltpu.CompilerParams(vmem_limit_bytes=32 * mib),
        name="backward",
    )(tip, col_adj, row_adj, *[residual[key] for key in back_keys])
    return trace_out, back_projected


def solution(mesh):
    return jax.shard_map(
        on_device,
        mesh=mesh,
        in_specs=(
            P("planes", ("groups", "wide"), "rep", None),
            P("rep", None),
            P("rep", None),
            P("rep", None),
            P(None, "planes", None),
            P(),
            P(),
            P("wide", None, None),
            P("wide", None),
        ),
        out_specs=(
            P("planes", ("groups", "wide"), "rep"),
            P("planes", ("groups", "wide"), "rep", None),
        ),
        check_vma=False,
    )
```

```python
import functools

import jax
import jax.numpy as jnp
from jax import lax
from jax.experimental import pallas as pl
from jax.experimental.pallas import tpu as pltpu
from jax.sharding import PartitionSpec as P

BLOCK = 16
LANES = 128
F32 = jnp.float32
BF16 = jnp.bfloat16
REP, PLANE, WIDE = "rep", "planes", "wide"


def exchange(cells, axis, flip):
    count = lax.axis_size(axis)
    return lax.ppermute(cells, axis, [(i, i ^ flip) for i in range(count)])


def iota(shape, dim):
    return lax.broadcasted_iota(jnp.int32, shape, dim)


def tap_row(taps_ref, place):
    lane = iota((8, LANES), 1)
    row = jnp.zeros((8, LANES), F32)
    for k in range(taps_ref.shape[0]):
        row = jnp.where(lane == place(k) % LANES, taps_ref[k], row)
    return row[:1]


def quotient(x, n):
    if n & (n - 1) == 0:
        return lax.shift_right_logical(x, n.bit_length() - 1)
    return lax.shift_right_logical(x * (65536 // n + 1), 16)


def remainder(x, n):
    return x & (n - 1) if n & (n - 1) == 0 else x - n * quotient(x, n)


def toeplitz(row, count, shift=0):
    return pltpu.roll(
        jnp.broadcast_to(row, (count, row.shape[1])), shift, 1, stride=1, stride_axis=0
    )


def column_band(taps_ref, rim, sign):
    rolled = toeplitz(tap_row(taps_ref, lambda k: sign * (k - rim)), LANES)
    gap = iota((LANES, LANES), 1) - iota((LANES, LANES), 0)
    return jnp.where(jnp.abs(gap) <= rim, rolled, 0.0).astype(BF16)


def row_band_forward(taps_ref, rim, frames):
    out_rows, depth, span = BLOCK * frames, 3 * BLOCK * frames, 3 * BLOCK
    band = toeplitz(tap_row(taps_ref, lambda k: k + BLOCK - rim), BLOCK)[:, :span].astype(BF16)
    left = (quotient(iota((out_rows, BLOCK), 0), frames) == iota((out_rows, BLOCK), 1)).astype(BF16)
    right = (remainder(iota((span, depth), 1), span) == iota((span, depth), 0)).astype(BF16)
    tall = jnp.dot(left, band, preferred_element_type=F32).astype(BF16)
    spread = jnp.dot(tall, right, preferred_element_type=F32)
    start = iota((out_rows, depth), 1) - span * remainder(iota((out_rows, depth), 0), frames)
    return jnp.where((start >= 0) & (start < span), spread, 0.0).astype(BF16)


def row_band_adjoint(taps_ref, rim, frames):
    out_rows, depth, span = BLOCK * frames, 3 * BLOCK * frames, 3 * BLOCK
    band = toeplitz(tap_row(taps_ref, lambda k: BLOCK + rim - k), BLOCK)[:, :span].astype(BF16)
    left = (remainder(iota((out_rows, BLOCK), 0), BLOCK) == iota((out_rows, BLOCK), 1)).astype(BF16)
    right = (quotient(iota((span, depth), 1), frames) == iota((span, depth), 0)).astype(BF16)
    tall = jnp.dot(left, band, preferred_element_type=F32).astype(BF16)
    spread = jnp.dot(tall, right, preferred_element_type=F32)
    same = remainder(iota((out_rows, depth), 1), frames) == quotient(iota((out_rows, depth), 0), BLOCK)
    return jnp.where(same, spread, 0.0).astype(BF16)


def half_of(flip, far, wide):
    return (lax.axis_index(PLANE) ^ flip) * 2 + (quotient(lax.axis_index(WIDE), wide // 2) ^ far)


def per_frame(rows, frames, copies):
    tall = jnp.broadcast_to(rows[:, None, :], (BLOCK, frames, LANES)).reshape(BLOCK * frames, LANES)
    return tall if copies == 1 else jnp.concatenate([tall] * copies, axis=1)


def prepare_kernel(
    rim, cuts, col_hbm, row_hbm, movie_hbm, mask_hbm, support_hbm, templates_hbm,
    smooth_ref, col_fwd_ref, row_fwd_ref, code_ref, templates_ref, flat_ref,
    movie_ref, mask_ref, support_ref, packed_ref, loose_ref, col_ref, row_ref, sems,
):
    planes, frames, rows, _ = movie_ref.shape
    some = frames // cuts

    def fetch(n, source, target):
        copy = pltpu.make_async_copy(source, target, sems.at[n])
        copy.start()
        return copy

    tap_copies = [fetch(0, col_hbm, col_ref), fetch(1, row_hbm, row_ref)]
    movie_copies = []
    for n in range(planes * cuts):
        piece = (n // cuts, pl.ds(n % cuts * some, some))
        movie_copies.append(fetch(5 + n, movie_hbm.at[piece], movie_ref.at[piece]))
    packed_copy = fetch(2, templates_hbm, packed_ref)
    code_copies = [fetch(3, mask_hbm, mask_ref), fetch(4, support_hbm, support_ref)]
    for copy in tap_copies:
        copy.wait()
    col_fwd = column_band(col_ref, rim, -1)
    col_fwd_ref[...] = col_fwd
    row_fwd_ref[...] = row_band_forward(row_ref, rim, frames)
    for copy in (*movie_copies, packed_copy, *code_copies):
        copy.wait()
    loose_ref[...] = packed_ref[...].astype(F32)
    code_ref[...] = support_ref[...] * 2 + mask_ref[...]
    unit = (iota((LANES, LANES), 0) == iota((LANES, LANES), 1)).astype(BF16)
    for n in range(planes * cuts):
        p, first = n // cuts, n % cuts * some
        full = jnp.dot(
            movie_ref[p, first : first + some].reshape(some * rows, LANES), col_fwd,
            preferred_element_type=F32,
        )
        smooth_ref[first : first + some, BLOCK : BLOCK + rows, p * LANES : (p + 1) * LANES] = (
            full.astype(BF16).reshape(some, rows, LANES)
        )
    for p in range(planes):
        shapes = loose_ref[pl.ds(p, templates_ref.shape[1], stride=planes), :].astype(BF16)
        flat_ref[:, p * LANES : (p + 1) * LANES] = shapes
        templates_ref[p * LANES : (p + 1) * LANES, :] = lax.dot_general(
            unit, shapes, (((1,), (1,)), ((), ())), preferred_element_type=F32
        ).astype(BF16)


def forward_kernel(
    flip, far, fill, wide, ks, smooth_in_ref, edge_ref, col_fwd_ref, row_fwd_ref, code_ref,
    templates_ref, smooth_ref, filtered_ref, out_ref, projected_ref,
):
    frames, padded_rows, width = smooth_ref.shape
    planes, rows = width // LANES, padded_rows - 2 * BLOCK
    if fill:
        for p in range(planes):
            edge = jnp.dot(
                edge_ref[p].reshape(frames * BLOCK, LANES), col_fwd_ref[...],
                preferred_element_type=F32,
            ).reshape(frames, BLOCK, LANES)
            lanes = slice(p * LANES, (p + 1) * LANES)
            above = jnp.where(lax.axis_index(REP) > 0, edge, 0.0).astype(BF16)
            below = jnp.where(lax.axis_index(REP) > 0, 0.0, edge).astype(BF16)
            smooth_ref[:, :BLOCK, lanes] = above
            smooth_ref[:, BLOCK + rows :, lanes] = below
    here = filtered_ref.shape[0] // frames
    first = half_of(flip, far, wide) * here
    tiles = templates_ref.shape[1] // LANES
    def along(b):
        near = smooth_ref[:, pl.ds(pl.multiple_of(first + b * BLOCK, BLOCK), 3 * BLOCK), :]
        near = near.reshape(frames * 3 * BLOCK, width)
        return jnp.dot(row_fwd_ref[...], near, preferred_element_type=F32)

    cells = along(0)
    for b in range(here // BLOCK):
        code = code_ref[pl.ds(pl.multiple_of(first + b * BLOCK, BLOCK), BLOCK), :]
        mask = per_frame((code & 1).astype(F32), frames, planes)
        filtered = (cells * mask).astype(BF16)
        spot = slice(b * BLOCK * frames, (b + 1) * BLOCK * frames)
        filtered_ref[spot, :] = filtered
        dense = jnp.dot(filtered, templates_ref[...], preferred_element_type=F32)
        cells = along(b + 1) if b + 1 < here // BLOCK else None
        picked = per_frame(code >> 1, frames, 1)
        lane, tile = picked & (LANES - 1), quotient(picked, LANES)
        chosen = jnp.zeros(picked.shape, F32)
        for t in range(tiles):
            found = jnp.take_along_axis(
                dense[:, t * LANES : (t + 1) * LANES], lane, axis=1, mode="promise_in_bounds"
            )
            chosen = jnp.where(tile == t, found, chosen)
        projected_ref[spot, :] = chosen.astype(BF16)
    size = out_ref.shape[0] // len(ks)
    for i, k in enumerate(ks):
        start = pl.multiple_of(((lax.axis_index(WIDE) ^ k) & (wide // 2 - 1)) * size, size)
        out_ref[i * size : (i + 1) * size, :] = projected_ref[pl.ds(start, size), :]


def add_all(parts, spots, rows):
    total = None
    for part, spot in zip(parts, spots):
        term = part[spot * rows : (spot + 1) * rows, :].astype(F32)
        total = term if total is None else total + term
    return total.astype(BF16)


def sum_kernel(spots, lag_ref, *refs):
    parts, out_ref = refs[:-1], refs[-1]
    rows = out_ref.shape[0] - lag_ref.shape[0]
    out_ref[:rows, :] = add_all(parts, spots, rows)
    out_ref[rows:, :] = lag_ref[...]


def mix_kernel(wide, spots, owner_ref, lag_ref, *refs):
    parts, refs = refs[: len(spots)], refs[len(spots) :]
    blocks, outs = refs[: wide - 1], refs[wide - 1 : 2 * wide - 1]
    cells_ref, kernels_ref, traces_ref = refs[2 * wide - 1 :]
    _, share, frames, lanes = cells_ref.shape
    total = wide * frames
    here = lax.axis_index(WIDE)
    cells_ref[here] = add_all(parts, spots, share * frames).reshape(share, frames, lanes)
    kernels_ref[here] = lag_ref[...].astype(F32)
    for k, block in enumerate(blocks, 1):
        cells_ref[here ^ k] = block[: share * frames, :].reshape(share, frames, lanes)
        kernels_ref[here ^ k] = block[share * frames :, :].astype(F32)
    first = (lax.axis_index(PLANE) * wide + here) * share
    owners = owner_ref[...]
    lane = iota(owners.shape, 1)
    for h in range(share):
        owner = jnp.sum(jnp.where(lane == first + h, owners, 0), axis=1, keepdims=True)
        owner = jnp.broadcast_to(owner, (8, lanes))
        row = []
        for i in range(0, kernels_ref.shape[1], 8):
            values = jnp.zeros((8, lanes), F32)
            for d in range(wide):
                values = jnp.where(owner == d, kernels_ref[d, i : i + 8, :], values)
            row += [values[n : n + 1, :] for n in range(8)]
        row = jnp.concatenate(row[: 2 * total // lanes], axis=1)
        lag = toeplitz(row, total, total + 1)[:, :total].astype(BF16)
        mixed = jnp.dot(lag, cells_ref[:, h].reshape(total, lanes), preferred_element_type=F32)
        traces_ref[:, h] = jnp.maximum(mixed, 0.0).astype(BF16).reshape(wide, frames, lanes)
    for k, out_ref in enumerate(outs):
        out_ref[...] = traces_ref[here ^ k]


def bands_kernel(rim, frames, col_ref, row_ref, col_adj_ref, row_adj_ref):
    band = column_band(col_ref, rim, 1)
    col_adj_ref[...] = jnp.zeros_like(col_adj_ref)
    for p in range(col_adj_ref.shape[0] // LANES):
        lanes = slice(p * LANES, (p + 1) * LANES)
        col_adj_ref[lanes, lanes] = band
    row_adj_ref[...] = row_band_adjoint(row_ref, rim, frames)


def residual_kernel(flip, far, wide, spots, filtered_ref, code_ref, templates_ref, *refs):
    traces, (out_ref, edge_ref, ordered_ref, slots_ref) = refs[:-4], refs[-4:]
    _, frames, lanes = traces[0].shape
    share = ordered_ref.shape[0] // len(spots)
    names, width = templates_ref.shape
    tile = 2 * LANES
    base = half_of(flip, far, wide) * len(spots) * share
    marks = iota((lanes, tile), 1).astype(F32).astype(BF16)
    group = min(8, share)
    for n, (k, source, offset) in enumerate(spots):
        block = (lax.axis_index(WIDE) ^ k) & (wide // 2 - 1)
        source, offset = traces[source], offset * share
        top = base + block * share
        for g in range(share // group):
            support = code_ref[pl.ds(top + g * group, group), :] >> 1
            support = jnp.concatenate([support] * (8 // group), axis=0)
            columns = [
                jnp.transpose(
                    jnp.where(quotient(support, tile) == t, support & (tile - 1), -1).astype(F32)
                )
                for t in range(names // tile)
            ]
            for i in range(group):
                h = g * group + i
                hits = jnp.concatenate(
                    [
                        jnp.where(
                            marks
                            == jnp.broadcast_to(column[:, i : i + 1], (lanes, tile)).astype(BF16),
                            jnp.ones((), BF16), jnp.zeros((), BF16),
                        )
                        for column in columns
                    ],
                    axis=1,
                )
                slots_ref[n, h * frames : (h + 1) * frames, :] = jnp.dot(
                    source[offset + h], hits, preferred_element_type=F32
                ).astype(BF16)
        model = jnp.dot(slots_ref[n], templates_ref[...], preferred_element_type=F32)
        mask = (code_ref[pl.ds(top, share), :] & 1).astype(F32)
        mask = jnp.broadcast_to(mask[:, None, :], (share, frames, lanes)).reshape(-1, lanes)
        size = share * frames
        spot = pl.ds(pl.multiple_of(block * size, size), size)
        out_ref[spot, :] = (
            filtered_ref[spot, :].astype(F32)
            - jnp.concatenate([mask] * (width // lanes), axis=1) * model
        ).astype(BF16)
        ordered_ref[pl.ds(block * share, share)] = source[offset : offset + share]
    edge = edge_ref.shape[0]
    start = jnp.where(lax.axis_index(REP) > 0, 0, out_ref.shape[0] - edge)
    edge_ref[...] = out_ref[pl.ds(pl.multiple_of(start, edge), edge), :]


def backward_kernel(keys, wide, edge_ref, col_adj_ref, row_adj_ref, *refs):
    parts, (out_hbm, padded_ref, out_ref, sems) = refs[: len(keys)], refs[len(keys) :]
    planes, frames, rows, _ = out_ref.shape
    edge, size = BLOCK * frames, parts[0].shape[0]
    zero = jnp.zeros_like(edge_ref)
    padded_ref[:edge, :] = jnp.where(lax.axis_index(REP) > 0, edge_ref[...], zero)
    padded_ref[edge + rows * frames :, :] = jnp.where(lax.axis_index(REP) > 0, zero, edge_ref[...])
    for (flip, far), part in zip(keys, parts):
        spot = pl.multiple_of(edge + half_of(flip, far, wide) * size, edge)
        padded_ref[pl.ds(spot, size), :] = part[...]
    def along(b):
        near = padded_ref[b * edge : (b + 3) * edge, :]
        return jnp.dot(row_adj_ref[...], near, preferred_element_type=F32).astype(BF16)

    copies = []
    back = along(0)
    for b in range(rows // BLOCK):
        ahead = along(b + 1) if b + 1 < rows // BLOCK else None
        full = jnp.dot(back, col_adj_ref[...], preferred_element_type=F32).astype(BF16)
        for p in range(planes):
            out_ref[p, :, b * BLOCK : (b + 1) * BLOCK, :] = full[
                :, p * LANES : (p + 1) * LANES
            ].reshape(frames, BLOCK, LANES)
        piece = (slice(None), slice(None), pl.ds(b * BLOCK, BLOCK))
        copy = pltpu.make_async_copy(out_ref.at[piece], out_hbm.at[piece], sems.at[b])
        copy.start()
        copies.append(copy)
        back = ahead
    for copy in copies:
        copy.wait()


VMEM = pl.BlockSpec(memory_space=pltpu.VMEM)
SMEM = pl.BlockSpec(memory_space=pltpu.SMEM)
HBM = pl.BlockSpec(memory_space=pltpu.HBM)


def shaped(shape):
    return jax.ShapeDtypeStruct(shape, BF16)


def call(kernel, name, outs, smem, vmem, scratch=(), aliases=None):
    return pl.pallas_call(
        kernel,
        out_shape=tuple(shaped(s) if isinstance(s, tuple) else s for s in outs),
        in_specs=[SMEM] * smem + [VMEM] * vmem,
        out_specs=(VMEM,) * len(outs),
        scratch_shapes=scratch,
        input_output_aliases=aliases or {},
        compiler_params=pltpu.CompilerParams(vmem_limit_bytes=32 * 1024 * 1024),
        name=name,
    )


def lag_kernel_values(gains, lags, frame_count):
    taps = gains.shape[1]
    lag_values = jnp.arange(2 * frame_count, dtype=jnp.int32) - (frame_count - 1)
    offsets = jnp.arange(taps, dtype=jnp.int32) - (taps - 1) // 2
    hits = lag_values[None, :, None] == lags[:, None, None] * offsets[None, None, :]
    spread = jnp.where(hits, gains[:, None, :], jnp.zeros((), gains.dtype))
    return jnp.sum(spread, axis=(0, 2)).astype(BF16)


def on_device(
    movie_frames, pixel_mask, tile_owner, support, templates, row_taps, col_taps, lag_gains, dilations
):
    planes, frames, rows, cols = movie_frames.shape
    wide, plane_count = lax.axis_size("wide"), lax.axis_size("planes")
    rim = (row_taps.shape[0] - 1) // 2
    total_frames, width = frames * wide, planes * cols
    here = rows // plane_count
    share = here // wide
    edge = BLOCK * frames
    rep, plane, spot = lax.axis_index("rep"), lax.axis_index("planes"), lax.axis_index("wide")
    mib = 1 << 20

    start = jnp.where(rep == 0, rows - BLOCK, 0)
    rim_rows = exchange(lax.dynamic_slice_in_dim(movie_frames, start, BLOCK, axis=2), "rep", 1)
    cuts = 2
    depth, names = 3 * BLOCK * frames, templates.shape[0]
    smooth, col_fwd, row_fwd, code, tall_templates, flat_templates = pl.pallas_call(
        functools.partial(prepare_kernel, rim, cuts),
        out_shape=(
            shaped((frames, rows + 2 * BLOCK, width)), shaped((cols, cols)), shaped((edge, depth)),
            jax.ShapeDtypeStruct(support.shape, jnp.int32), shaped((width, names)),
            shaped((names, width)),
        ),
        in_specs=[HBM] * 6,
        out_specs=(VMEM,) * 6,
        scratch_shapes=[
            pltpu.VMEM(movie_frames.shape, BF16),
            pltpu.VMEM(pixel_mask.shape, jnp.int32),
            pltpu.VMEM(support.shape, jnp.int32),
            pltpu.VMEM((names * planes, cols), BF16),
            pltpu.VMEM((names * planes, cols), F32),
            pltpu.SMEM(col_taps.shape, F32),
            pltpu.SMEM(row_taps.shape, F32),
            pltpu.SemaphoreType.DMA((5 + planes * cuts,)),
        ],
        compiler_params=pltpu.CompilerParams(vmem_limit_bytes=32 * mib),
        name="prepare",
    )(
        *[
            pltpu.with_memory_space_constraint(x, pltpu.HBM)
            for x in (
                col_taps, row_taps, movie_frames, pixel_mask, support,
                templates.reshape(names * planes, cols),
            )
        ]
    )

    near_ks, far_ks = list(range(wide // 2)), list(range(wide // 2, wide))
    halves = {1: far_ks, 0: near_ks[::-1]}
    half_rows = here // 2
    filtered, projected = {}, {}
    keys = [((turn + 1) % plane_count, far) for turn in range(plane_count) for far in (0, 1)]
    for turn, (flip, far) in enumerate(keys):
        smooth, filtered[flip, far], mine = call(
            functools.partial(forward_kernel, flip, far, turn == 0, wide, halves[far]), "forward",
            [smooth.shape, (half_rows * frames, width), (half_rows * frames, LANES)],
            0, 6, aliases={0: 0},
            scratch=[pltpu.VMEM((half_rows * frames, LANES), BF16)],
        )(smooth, rim_rows, col_fwd, row_fwd, code, tall_templates)
        projected[flip, far] = exchange(mine, "planes", flip) if flip else mine
        if turn == 0:
            gains, lags, _ = lax.optimization_barrier((lag_gains, dilations, smooth))
            kernel_row = lag_kernel_values(gains[0], lags[0], total_frames)
            lag_rows = -(-2 * total_frames // (LANES * BLOCK)) * BLOCK
            kernel_row = jnp.pad(kernel_row, (0, lag_rows * LANES - 2 * total_frames))
            kernel_row = kernel_row.reshape(lag_rows, LANES)

    block_rows = share * frames + lag_rows
    sums, blocks = {}, {}

    def parts_of(k):
        far = int(k in far_ks)
        spots = [halves[far].index(k)] * plane_count
        return spots, [projected[flip, far] for flip in range(plane_count)]

    for k in near_ks[1:] + far_ks:
        spots, parts = parts_of(k)
        (sums[k],) = call(
            functools.partial(sum_kernel, spots), "sum", [(block_rows, LANES)],
            0, 1 + plane_count,
        )(kernel_row, *parts)
        blocks[k] = exchange(sums[k], "wide", k)

    late_col, late_row, _ = lax.optimization_barrier(
        (col_taps, row_taps, list(sums.values()))
    )
    col_adj, row_adj = call(
        functools.partial(bands_kernel, rim, frames), "bands", [(width, width), (edge, depth)],
        2, 0,
    )(late_col, late_row)
    own_spots, own_parts = parts_of(0)
    own_parts[0], col_adj, row_adj = lax.optimization_barrier((own_parts[0], col_adj, row_adj))

    cell_shape = (wide, share, frames, LANES)
    traces = call(
        functools.partial(mix_kernel, wide, own_spots), "mix", [cell_shape[1:]] * wide,
        0, 1 + wide + plane_count,
        scratch=[
            pltpu.VMEM(cell_shape, BF16), pltpu.VMEM((wide, lag_rows, LANES), F32),
            pltpu.VMEM(cell_shape, BF16),
        ],
    )(
        tile_owner.reshape(1, rows), kernel_row, *own_parts, *[blocks[k] for k in range(1, wide)],
    )
    swapped = {k: exchange(traces[k], "wide", k) for k in far_ks + near_ks[1:]}
    swapped[0] = traces[0]
    late = range(1, plane_count)
    near = jnp.concatenate([swapped[k] for k in near_ks])
    passed = {flip: exchange(near, "planes", flip) for flip in late}

    residual, edges, ordered = {}, {}, {}
    back_keys = [(flip, far) for flip in range(plane_count) for far in (0, 1)]

    def subtract(flip, far, groups, got):
        spots = [(k, n, i) for n, ks in enumerate(groups) for i, k in enumerate(ks)]
        residual[flip, far], edges[flip, far], ordered[flip, far] = call(
            functools.partial(residual_kernel, flip, far, wide, spots), "residual",
            [(half_rows * frames, width), (edge, width), (half_rows, frames, LANES)],
            0, 3 + len(got), scratch=[pltpu.VMEM((len(spots), share * frames, names), BF16)],
        )(filtered[flip, far], code, flat_templates, *got)

    subtract(0, 0, [near_ks], [near])
    distant, _ = lax.optimization_barrier(([swapped[k] for k in far_ks], edges[0, 0]))
    joined = jnp.concatenate(distant)
    subtract(0, 1, [[k] for k in far_ks], distant)
    for flip in late:
        subtract(flip, 0, [near_ks], [passed[flip]])
        subtract(flip, 1, [far_ks], [exchange(joined, "planes", flip)])

    def pick(table, part, half):
        found = table[0, 0]
        for flip, far in back_keys[1:]:
            here_it_is = ((plane ^ part) == flip) & ((spot // (wide // 2) ^ half) == far)
            found = jnp.where(here_it_is, table[flip, far], found)
        return found

    tip = pick(edges, jnp.where(rep == 0, plane_count - 1, 0), jnp.where(rep == 0, 1, 0))
    tip = exchange(tip, "rep", 1)

    foot_share = support.shape[1] // plane_count
    in_order = [pick(ordered, q, half) for q in range(plane_count) for half in (0, 1)]
    mine = lax.dynamic_slice_in_dim(jnp.concatenate(in_order), plane * foot_share, foot_share, 2)
    trace_out = jnp.transpose(mine, (2, 1, 0))

    back_projected = pl.pallas_call(
        functools.partial(backward_kernel, back_keys, wide),
        out_shape=shaped(movie_frames.shape),
        in_specs=[VMEM] * (3 + len(back_keys)),
        out_specs=HBM,
        scratch_shapes=[
            pltpu.VMEM(((rows + 2 * BLOCK) * frames, width), BF16),
            pltpu.VMEM(movie_frames.shape, BF16),
            pltpu.SemaphoreType.DMA((rows // BLOCK,)),
        ],
        compiler_params=pltpu.CompilerParams(vmem_limit_bytes=32 * mib),
        name="backward",
    )(tip, col_adj, row_adj, *[residual[key] for key in back_keys])
    return trace_out, back_projected


def solution(mesh):
    return jax.shard_map(
        on_device,
        mesh=mesh,
        in_specs=(
            P("planes", ("groups", "wide"), "rep", None),
            P("rep", None),
            P("rep", None),
            P("rep", None),
            P(None, "planes", None),
            P(),
            P(),
            P("wide", None, None),
            P("wide", None),
        ),
        out_specs=(
            P("planes", ("groups", "wide"), "rep"),
            P("planes", ("groups", "wide"), "rep", None),
        ),
        check_vma=False,
    )
```

```python
import functools

import jax
import jax.numpy as jnp
from jax import lax
from jax.experimental import pallas as pl
from jax.experimental.pallas import tpu as pltpu
from jax.sharding import PartitionSpec as P

BLOCK = 16
LANES = 128
F32 = jnp.float32
BF16 = jnp.bfloat16
REP, PLANE, WIDE = "rep", "planes", "wide"


def exchange(cells, axis, flip):
    count = lax.axis_size(axis)
    return lax.ppermute(cells, axis, [(i, i ^ flip) for i in range(count)])


def iota(shape, dim):
    return lax.broadcasted_iota(jnp.int32, shape, dim)


def tap_row(taps_ref, place):
    lane = iota((8, LANES), 1)
    row = jnp.zeros((8, LANES), F32)
    for k in range(taps_ref.shape[0]):
        row = jnp.where(lane == place(k) % LANES, taps_ref[k], row)
    return row[:1]


def quotient(x, n):
    if n & (n - 1) == 0:
        return lax.shift_right_logical(x, n.bit_length() - 1)
    return lax.shift_right_logical(x * (65536 // n + 1), 16)


def remainder(x, n):
    return x & (n - 1) if n & (n - 1) == 0 else x - n * quotient(x, n)


def toeplitz(row, count, shift=0):
    return pltpu.roll(
        jnp.broadcast_to(row, (count, row.shape[1])), shift, 1, stride=1, stride_axis=0
    )


def column_band(taps_ref, rim, sign):
    rolled = toeplitz(tap_row(taps_ref, lambda k: sign * (k - rim)), LANES)
    gap = iota((LANES, LANES), 1) - iota((LANES, LANES), 0)
    return jnp.where(jnp.abs(gap) <= rim, rolled, 0.0).astype(BF16)


def row_band_forward(taps_ref, rim, frames):
    out_rows, depth, span = BLOCK * frames, 3 * BLOCK * frames, 3 * BLOCK
    band = toeplitz(tap_row(taps_ref, lambda k: k + BLOCK - rim), BLOCK)[:, :span].astype(BF16)
    left = (quotient(iota((out_rows, BLOCK), 0), frames) == iota((out_rows, BLOCK), 1)).astype(BF16)
    right = (remainder(iota((span, depth), 1), span) == iota((span, depth), 0)).astype(BF16)
    tall = jnp.dot(left, band, preferred_element_type=F32).astype(BF16)
    spread = jnp.dot(tall, right, preferred_element_type=F32)
    start = iota((out_rows, depth), 1) - span * remainder(iota((out_rows, depth), 0), frames)
    return jnp.where((start >= 0) & (start < span), spread, 0.0).astype(BF16)


def row_band_adjoint(taps_ref, rim, frames):
    out_rows, depth, span = BLOCK * frames, 3 * BLOCK * frames, 3 * BLOCK
    band = toeplitz(tap_row(taps_ref, lambda k: BLOCK + rim - k), BLOCK)[:, :span].astype(BF16)
    left = (remainder(iota((out_rows, BLOCK), 0), BLOCK) == iota((out_rows, BLOCK), 1)).astype(BF16)
    right = (quotient(iota((span, depth), 1), frames) == iota((span, depth), 0)).astype(BF16)
    tall = jnp.dot(left, band, preferred_element_type=F32).astype(BF16)
    spread = jnp.dot(tall, right, preferred_element_type=F32)
    same = remainder(iota((out_rows, depth), 1), frames) == quotient(iota((out_rows, depth), 0), BLOCK)
    return jnp.where(same, spread, 0.0).astype(BF16)


def half_of(flip, far, wide):
    return (lax.axis_index(PLANE) ^ flip) * 2 + (quotient(lax.axis_index(WIDE), wide // 2) ^ far)


def per_frame(rows, frames, copies):
    tall = jnp.broadcast_to(rows[:, None, :], (BLOCK, frames, LANES)).reshape(BLOCK * frames, LANES)
    return tall if copies == 1 else jnp.concatenate([tall] * copies, axis=1)


def prepare_kernel(
    rim, cuts, col_hbm, row_hbm, movie_hbm, mask_hbm, support_hbm, templates_hbm,
    smooth_ref, col_fwd_ref, row_fwd_ref, code_ref, templates_ref, flat_ref,
    movie_ref, mask_ref, support_ref, packed_ref, loose_ref, col_ref, row_ref, sems,
):
    planes, frames, rows, _ = movie_ref.shape
    some = frames // cuts

    def fetch(n, source, target):
        copy = pltpu.make_async_copy(source, target, sems.at[n])
        copy.start()
        return copy

    tap_copies = [fetch(0, col_hbm, col_ref), fetch(1, row_hbm, row_ref)]
    movie_copies = []
    for n in range(planes * cuts):
        piece = (n // cuts, pl.ds(n % cuts * some, some))
        movie_copies.append(fetch(5 + n, movie_hbm.at[piece], movie_ref.at[piece]))
    packed_copy = fetch(2, templates_hbm, packed_ref)
    code_copies = [fetch(3, mask_hbm, mask_ref), fetch(4, support_hbm, support_ref)]
    for copy in tap_copies:
        copy.wait()
    col_fwd = column_band(col_ref, rim, -1)
    col_fwd_ref[...] = col_fwd
    row_fwd_ref[...] = row_band_forward(row_ref, rim, frames)
    for copy in (*movie_copies, packed_copy, *code_copies):
        copy.wait()
    loose_ref[...] = packed_ref[...].astype(F32)
    code_ref[...] = support_ref[...] * 2 + mask_ref[...]
    unit = (iota((LANES, LANES), 0) == iota((LANES, LANES), 1)).astype(BF16)
    for n in range(planes * cuts):
        p, first = n // cuts, n % cuts * some
        full = jnp.dot(
            movie_ref[p, first : first + some].reshape(some * rows, LANES), col_fwd,
            preferred_element_type=F32,
        )
        smooth_ref[first : first + some, BLOCK : BLOCK + rows, p * LANES : (p + 1) * LANES] = (
            full.astype(BF16).reshape(some, rows, LANES)
        )
    for p in range(planes):
        shapes = loose_ref[pl.ds(p, templates_ref.shape[1], stride=planes), :].astype(BF16)
        flat_ref[:, p * LANES : (p + 1) * LANES] = shapes
        templates_ref[p * LANES : (p + 1) * LANES, :] = lax.dot_general(
            unit, shapes, (((1,), (1,)), ((), ())), preferred_element_type=F32
        ).astype(BF16)


def forward_kernel(
    flip, far, fill, wide, ks, smooth_in_ref, edge_ref, col_fwd_ref, row_fwd_ref, code_ref,
    templates_ref, smooth_ref, filtered_ref, out_ref, projected_ref,
):
    frames, padded_rows, width = smooth_ref.shape
    planes, rows = width // LANES, padded_rows - 2 * BLOCK
    if fill:
        for p in range(planes):
            edge = jnp.dot(
                edge_ref[p].reshape(frames * BLOCK, LANES), col_fwd_ref[...],
                preferred_element_type=F32,
            ).reshape(frames, BLOCK, LANES)
            lanes = slice(p * LANES, (p + 1) * LANES)
            above = jnp.where(lax.axis_index(REP) > 0, edge, 0.0).astype(BF16)
            below = jnp.where(lax.axis_index(REP) > 0, 0.0, edge).astype(BF16)
            smooth_ref[:, :BLOCK, lanes] = above
            smooth_ref[:, BLOCK + rows :, lanes] = below
    here = filtered_ref.shape[0] // frames
    first = half_of(flip, far, wide) * here
    tiles = templates_ref.shape[1] // LANES
    def along(b):
        near = smooth_ref[:, pl.ds(pl.multiple_of(first + b * BLOCK, BLOCK), 3 * BLOCK), :]
        near = near.reshape(frames * 3 * BLOCK, width)
        return jnp.dot(row_fwd_ref[...], near, preferred_element_type=F32)

    cells = along(0)
    for b in range(here // BLOCK):
        code = code_ref[pl.ds(pl.multiple_of(first + b * BLOCK, BLOCK), BLOCK), :]
        mask = per_frame((code & 1).astype(F32), frames, planes)
        filtered = (cells * mask).astype(BF16)
        spot = slice(b * BLOCK * frames, (b + 1) * BLOCK * frames)
        filtered_ref[spot, :] = filtered
        dense = jnp.dot(filtered, templates_ref[...], preferred_element_type=F32)
        cells = along(b + 1) if b + 1 < here // BLOCK else None
        picked = per_frame(code >> 1, frames, 1)
        lane, tile = picked & (LANES - 1), quotient(picked, LANES)
        chosen = jnp.zeros(picked.shape, F32)
        for t in range(tiles):
            found = jnp.take_along_axis(
                dense[:, t * LANES : (t + 1) * LANES], lane, axis=1, mode="promise_in_bounds"
            )
            chosen = jnp.where(tile == t, found, chosen)
        projected_ref[spot, :] = chosen.astype(BF16)
    size = out_ref.shape[0] // len(ks)
    for i, k in enumerate(ks):
        start = pl.multiple_of(((lax.axis_index(WIDE) ^ k) & (wide // 2 - 1)) * size, size)
        out_ref[i * size : (i + 1) * size, :] = projected_ref[pl.ds(start, size), :]


def add_all(parts, spots, rows):
    total = None
    for part, spot in zip(parts, spots):
        term = part[spot * rows : (spot + 1) * rows, :].astype(F32)
        total = term if total is None else total + term
    return total.astype(BF16)


def sum_kernel(spots, lag_ref, *refs):
    parts, out_ref = refs[:-1], refs[-1]
    rows = out_ref.shape[0] - lag_ref.shape[0]
    out_ref[:rows, :] = add_all(parts, spots, rows)
    out_ref[rows:, :] = lag_ref[...]


def mix_kernel(wide, spots, owner_ref, lag_ref, *refs):
    parts, refs = refs[: len(spots)], refs[len(spots) :]
    blocks, outs = refs[: wide - 1], refs[wide - 1 : 2 * wide - 1]
    cells_ref, kernels_ref, traces_ref = refs[2 * wide - 1 :]
    _, share, frames, lanes = cells_ref.shape
    total = wide * frames
    here = lax.axis_index(WIDE)
    cells_ref[here] = add_all(parts, spots, share * frames).reshape(share, frames, lanes)
    kernels_ref[here] = lag_ref[...].astype(F32)
    for k, block in enumerate(blocks, 1):
        cells_ref[here ^ k] = block[: share * frames, :].reshape(share, frames, lanes)
        kernels_ref[here ^ k] = block[share * frames :, :].astype(F32)
    first = (lax.axis_index(PLANE) * wide + here) * share
    owners = owner_ref[...]
    lane = iota(owners.shape, 1)
    for h in range(share):
        owner = jnp.sum(jnp.where(lane == first + h, owners, 0), axis=1, keepdims=True)
        owner = jnp.broadcast_to(owner, (8, lanes))
        row = []
        for i in range(0, kernels_ref.shape[1], 8):
            values = jnp.zeros((8, lanes), F32)
            for d in range(wide):
                values = jnp.where(owner == d, kernels_ref[d, i : i + 8, :], values)
            row += [values[n : n + 1, :] for n in range(8)]
        row = jnp.concatenate(row[: 2 * total // lanes], axis=1)
        lag = toeplitz(row, total, total + 1)[:, :total].astype(BF16)
        mixed = jnp.dot(lag, cells_ref[:, h].reshape(total, lanes), preferred_element_type=F32)
        traces_ref[:, h] = jnp.maximum(mixed, 0.0).astype(BF16).reshape(wide, frames, lanes)
    for k, out_ref in enumerate(outs):
        out_ref[...] = traces_ref[here ^ k]


def bands_kernel(rim, frames, col_ref, row_ref, col_adj_ref, row_adj_ref):
    band = column_band(col_ref, rim, 1)
    col_adj_ref[...] = jnp.zeros_like(col_adj_ref)
    for p in range(col_adj_ref.shape[0] // LANES):
        lanes = slice(p * LANES, (p + 1) * LANES)
        col_adj_ref[lanes, lanes] = band
    row_adj_ref[...] = row_band_adjoint(row_ref, rim, frames)


def residual_kernel(flip, far, wide, spots, filtered_ref, code_ref, templates_ref, *refs):
    traces, (out_ref, edge_ref, ordered_ref, slots_ref) = refs[:-4], refs[-4:]
    _, frames, lanes = traces[0].shape
    share = ordered_ref.shape[0] // len(spots)
    names, width = templates_ref.shape
    tile = 2 * LANES
    base = half_of(flip, far, wide) * len(spots) * share
    marks = iota((lanes, tile), 1).astype(F32).astype(BF16)
    group = min(8, share)
    for n, (k, source, offset) in enumerate(spots):
        block = (lax.axis_index(WIDE) ^ k) & (wide // 2 - 1)
        source, offset = traces[source], offset * share
        top = base + block * share
        for g in range(share // group):
            support = code_ref[pl.ds(top + g * group, group), :] >> 1
            support = jnp.concatenate([support] * (8 // group), axis=0)
            columns = [
                jnp.transpose(
                    jnp.where(quotient(support, tile) == t, support & (tile - 1), -1).astype(F32)
                )
                for t in range(names // tile)
            ]
            for i in range(group):
                h = g * group + i
                hits = jnp.concatenate(
                    [
                        jnp.where(
                            marks
                            == jnp.broadcast_to(column[:, i : i + 1], (lanes, tile)).astype(BF16),
                            jnp.ones((), BF16), jnp.zeros((), BF16),
                        )
                        for column in columns
                    ],
                    axis=1,
                )
                slots_ref[n, h * frames : (h + 1) * frames, :] = jnp.dot(
                    source[offset + h], hits, preferred_element_type=F32
                ).astype(BF16)
        model = jnp.dot(slots_ref[n], templates_ref[...], preferred_element_type=F32)
        mask = (code_ref[pl.ds(top, share), :] & 1).astype(F32)
        mask = jnp.broadcast_to(mask[:, None, :], (share, frames, lanes)).reshape(-1, lanes)
        size = share * frames
        spot = pl.ds(pl.multiple_of(block * size, size), size)
        out_ref[spot, :] = (
            filtered_ref[spot, :].astype(F32)
            - jnp.concatenate([mask] * (width // lanes), axis=1) * model
        ).astype(BF16)
        ordered_ref[pl.ds(block * share, share)] = source[offset : offset + share]
    edge = edge_ref.shape[0]
    start = jnp.where(lax.axis_index(REP) > 0, 0, out_ref.shape[0] - edge)
    edge_ref[...] = out_ref[pl.ds(pl.multiple_of(start, edge), edge), :]


def backward_kernel(keys, wide, edge_ref, col_adj_ref, row_adj_ref, *refs):
    parts, (out_hbm, padded_ref, out_ref, sems) = refs[: len(keys)], refs[len(keys) :]
    planes, frames, rows, _ = out_ref.shape
    edge, size = BLOCK * frames, parts[0].shape[0]
    zero = jnp.zeros_like(edge_ref)
    padded_ref[:edge, :] = jnp.where(lax.axis_index(REP) > 0, edge_ref[...], zero)
    padded_ref[edge + rows * frames :, :] = jnp.where(lax.axis_index(REP) > 0, zero, edge_ref[...])
    for (flip, far), part in zip(keys, parts):
        spot = pl.multiple_of(edge + half_of(flip, far, wide) * size, edge)
        padded_ref[pl.ds(spot, size), :] = part[...]
    def along(b):
        near = padded_ref[b * edge : (b + 3) * edge, :]
        return jnp.dot(row_adj_ref[...], near, preferred_element_type=F32).astype(BF16)

    copies = []
    back = along(0)
    for b in range(rows // BLOCK):
        ahead = along(b + 1) if b + 1 < rows // BLOCK else None
        full = jnp.dot(back, col_adj_ref[...], preferred_element_type=F32).astype(BF16)
        for p in range(planes):
            out_ref[p, :, b * BLOCK : (b + 1) * BLOCK, :] = full[
                :, p * LANES : (p + 1) * LANES
            ].reshape(frames, BLOCK, LANES)
        piece = (slice(None), slice(None), pl.ds(b * BLOCK, BLOCK))
        copy = pltpu.make_async_copy(out_ref.at[piece], out_hbm.at[piece], sems.at[b])
        copy.start()
        copies.append(copy)
        back = ahead
    for copy in copies:
        copy.wait()


VMEM = pl.BlockSpec(memory_space=pltpu.VMEM)
SMEM = pl.BlockSpec(memory_space=pltpu.SMEM)
HBM = pl.BlockSpec(memory_space=pltpu.HBM)


def shaped(shape):
    return jax.ShapeDtypeStruct(shape, BF16)


def call(kernel, name, outs, smem, vmem, scratch=(), aliases=None):
    return pl.pallas_call(
        kernel,
        out_shape=tuple(shaped(s) if isinstance(s, tuple) else s for s in outs),
        in_specs=[SMEM] * smem + [VMEM] * vmem,
        out_specs=(VMEM,) * len(outs),
        scratch_shapes=scratch,
        input_output_aliases=aliases or {},
        compiler_params=pltpu.CompilerParams(vmem_limit_bytes=32 * 1024 * 1024),
        name=name,
    )


def lag_kernel_values(gains, lags, frame_count):
    taps = gains.shape[1]
    lag_values = jnp.arange(2 * frame_count, dtype=jnp.int32) - (frame_count - 1)
    offsets = jnp.arange(taps, dtype=jnp.int32) - (taps - 1) // 2
    hits = lag_values[None, :, None] == lags[:, None, None] * offsets[None, None, :]
    spread = jnp.where(hits, gains[:, None, :], jnp.zeros((), gains.dtype))
    return jnp.sum(spread, axis=(0, 2)).astype(BF16)


def on_device(
    movie_frames, pixel_mask, tile_owner, support, templates, row_taps, col_taps, lag_gains, dilations
):
    planes, frames, rows, cols = movie_frames.shape
    wide, plane_count = lax.axis_size("wide"), lax.axis_size("planes")
    rim = (row_taps.shape[0] - 1) // 2
    total_frames, width = frames * wide, planes * cols
    here = rows // plane_count
    share = here // wide
    edge = BLOCK * frames
    rep, plane, spot = lax.axis_index("rep"), lax.axis_index("planes"), lax.axis_index("wide")
    mib = 1 << 20

    start = jnp.where(rep == 0, rows - BLOCK, 0)
    rim_rows = exchange(lax.dynamic_slice_in_dim(movie_frames, start, BLOCK, axis=2), "rep", 1)
    cuts = 2
    depth, names = 3 * BLOCK * frames, templates.shape[0]
    smooth, col_fwd, row_fwd, code, tall_templates, flat_templates = pl.pallas_call(
        functools.partial(prepare_kernel, rim, cuts),
        out_shape=(
            shaped((frames, rows + 2 * BLOCK, width)), shaped((cols, cols)), shaped((edge, depth)),
            jax.ShapeDtypeStruct(support.shape, jnp.int32), shaped((width, names)),
            shaped((names, width)),
        ),
        in_specs=[HBM] * 6,
        out_specs=(VMEM,) * 6,
        scratch_shapes=[
            pltpu.VMEM(movie_frames.shape, BF16),
            pltpu.VMEM(pixel_mask.shape, jnp.int32),
            pltpu.VMEM(support.shape, jnp.int32),
            pltpu.VMEM((names * planes, cols), BF16),
            pltpu.VMEM((names * planes, cols), F32),
            pltpu.SMEM(col_taps.shape, F32),
            pltpu.SMEM(row_taps.shape, F32),
            pltpu.SemaphoreType.DMA((5 + planes * cuts,)),
        ],
        compiler_params=pltpu.CompilerParams(vmem_limit_bytes=32 * mib),
        name="prepare",
    )(
        *[
            pltpu.with_memory_space_constraint(x, pltpu.HBM)
            for x in (
                col_taps, row_taps, movie_frames, pixel_mask, support,
                templates.reshape(names * planes, cols),
            )
        ]
    )

    near_ks, far_ks = list(range(wide // 2)), list(range(wide // 2, wide))
    halves = {1: far_ks, 0: near_ks[::-1]}
    half_rows = here // 2
    filtered, projected = {}, {}
    flips = [(turn + 1) % plane_count for turn in range(plane_count)]
    keys = [(flip, far) for far in (1, 0) for flip in flips]
    for turn, (flip, far) in enumerate(keys):
        smooth, filtered[flip, far], mine = call(
            functools.partial(forward_kernel, flip, far, turn == 0, wide, halves[far]), "forward",
            [smooth.shape, (half_rows * frames, width), (half_rows * frames, LANES)],
            0, 6, aliases={0: 0},
            scratch=[pltpu.VMEM((half_rows * frames, LANES), BF16)],
        )(smooth, rim_rows, col_fwd, row_fwd, code, tall_templates)
        projected[flip, far] = exchange(mine, "planes", flip) if flip else mine
        if turn == 0:
            gains, lags, _ = lax.optimization_barrier((lag_gains, dilations, smooth))
            kernel_row = lag_kernel_values(gains[0], lags[0], total_frames)
            lag_rows = -(-2 * total_frames // (LANES * BLOCK)) * BLOCK
            kernel_row = jnp.pad(kernel_row, (0, lag_rows * LANES - 2 * total_frames))
            kernel_row = kernel_row.reshape(lag_rows, LANES)

    block_rows = share * frames + lag_rows
    sums, blocks = {}, {}

    def parts_of(k):
        far = int(k in far_ks)
        spots = [halves[far].index(k)] * plane_count
        return spots, [projected[flip, far] for flip in range(plane_count)]

    for k in near_ks[1:] + far_ks:
        spots, parts = parts_of(k)
        (sums[k],) = call(
            functools.partial(sum_kernel, spots), "sum", [(block_rows, LANES)],
            0, 1 + plane_count,
        )(kernel_row, *parts)
        blocks[k] = exchange(sums[k], "wide", k)

    late_col, late_row, _ = lax.optimization_barrier(
        (col_taps, row_taps, list(sums.values()))
    )
    col_adj, row_adj = call(
        functools.partial(bands_kernel, rim, frames), "bands", [(width, width), (edge, depth)],
        2, 0,
    )(late_col, late_row)
    own_spots, own_parts = parts_of(0)
    own_parts[0], col_adj, row_adj = lax.optimization_barrier((own_parts[0], col_adj, row_adj))

    cell_shape = (wide, share, frames, LANES)
    traces = call(
        functools.partial(mix_kernel, wide, own_spots), "mix", [cell_shape[1:]] * wide,
        0, 1 + wide + plane_count,
        scratch=[
            pltpu.VMEM(cell_shape, BF16), pltpu.VMEM((wide, lag_rows, LANES), F32),
            pltpu.VMEM(cell_shape, BF16),
        ],
    )(
        tile_owner.reshape(1, rows), kernel_row, *own_parts, *[blocks[k] for k in range(1, wide)],
    )
    swapped = {k: exchange(traces[k], "wide", k) for k in far_ks + near_ks[1:]}
    swapped[0] = traces[0]
    late = range(1, plane_count)
    near = jnp.concatenate([swapped[k] for k in near_ks])
    passed = {flip: exchange(near, "planes", flip) for flip in late}

    residual, edges, ordered = {}, {}, {}
    back_keys = [(flip, far) for flip in range(plane_count) for far in (0, 1)]

    def subtract(flip, far, groups, got):
        spots = [(k, n, i) for n, ks in enumerate(groups) for i, k in enumerate(ks)]
        residual[flip, far], edges[flip, far], ordered[flip, far] = call(
            functools.partial(residual_kernel, flip, far, wide, spots), "residual",
            [(half_rows * frames, width), (edge, width), (half_rows, frames, LANES)],
            0, 3 + len(got), scratch=[pltpu.VMEM((len(spots), share * frames, names), BF16)],
        )(filtered[flip, far], code, flat_templates, *got)

    subtract(0, 0, [near_ks], [near])
    distant, _ = lax.optimization_barrier(([swapped[k] for k in far_ks], edges[0, 0]))
    joined = jnp.concatenate(distant)
    subtract(0, 1, [[k] for k in far_ks], distant)
    for flip in late:
        subtract(flip, 0, [near_ks], [passed[flip]])
        subtract(flip, 1, [far_ks], [exchange(joined, "planes", flip)])

    def pick(table, part, half):
        found = table[0, 0]
        for flip, far in back_keys[1:]:
            here_it_is = ((plane ^ part) == flip) & ((spot // (wide // 2) ^ half) == far)
            found = jnp.where(here_it_is, table[flip, far], found)
        return found

    tip = pick(edges, jnp.where(rep == 0, plane_count - 1, 0), jnp.where(rep == 0, 1, 0))
    tip = exchange(tip, "rep", 1)

    foot_share = support.shape[1] // plane_count
    in_order = [pick(ordered, q, half) for q in range(plane_count) for half in (0, 1)]
    mine = lax.dynamic_slice_in_dim(jnp.concatenate(in_order), plane * foot_share, foot_share, 2)
    trace_out = jnp.transpose(mine, (2, 1, 0))

    back_projected = pl.pallas_call(
        functools.partial(backward_kernel, back_keys, wide),
        out_shape=shaped(movie_frames.shape),
        in_specs=[VMEM] * (3 + len(back_keys)),
        out_specs=HBM,
        scratch_shapes=[
            pltpu.VMEM(((rows + 2 * BLOCK) * frames, width), BF16),
            pltpu.VMEM(movie_frames.shape, BF16),
            pltpu.SemaphoreType.DMA((rows // BLOCK,)),
        ],
        compiler_params=pltpu.CompilerParams(vmem_limit_bytes=32 * mib),
        name="backward",
    )(tip, col_adj, row_adj, *[residual[key] for key in back_keys])
    return trace_out, back_projected


def solution(mesh):
    return jax.shard_map(
        on_device,
        mesh=mesh,
        in_specs=(
            P("planes", ("groups", "wide"), "rep", None),
            P("rep", None),
            P("rep", None),
            P("rep", None),
            P(None, "planes", None),
            P(),
            P(),
            P("wide", None, None),
            P("wide", None),
        ),
        out_specs=(
            P("planes", ("groups", "wide"), "rep"),
            P("planes", ("groups", "wide"), "rep", None),
        ),
        check_vma=False,
    )
```

```python
import functools

import jax
import jax.numpy as jnp
from jax import lax
from jax.experimental import pallas as pl
from jax.experimental.pallas import tpu as pltpu
from jax.sharding import PartitionSpec as P

BLOCK = 16
LANES = 128
F32 = jnp.float32
BF16 = jnp.bfloat16
REP, PLANE, WIDE = "rep", "planes", "wide"


def exchange(cells, axis, flip):
    count = lax.axis_size(axis)
    return lax.ppermute(cells, axis, [(i, i ^ flip) for i in range(count)])


def iota(shape, dim):
    return lax.broadcasted_iota(jnp.int32, shape, dim)


def tap_row(taps_ref, place):
    lane = iota((8, LANES), 1)
    row = jnp.zeros((8, LANES), F32)
    for k in range(taps_ref.shape[0]):
        row = jnp.where(lane == place(k) % LANES, taps_ref[k], row)
    return row[:1]


def quotient(x, n):
    if n & (n - 1) == 0:
        return lax.shift_right_logical(x, n.bit_length() - 1)
    return lax.shift_right_logical(x * (65536 // n + 1), 16)


def remainder(x, n):
    return x & (n - 1) if n & (n - 1) == 0 else x - n * quotient(x, n)


def toeplitz(row, count, shift=0):
    return pltpu.roll(
        jnp.broadcast_to(row, (count, row.shape[1])), shift, 1, stride=1, stride_axis=0
    )


def column_band(taps_ref, rim, sign):
    rolled = toeplitz(tap_row(taps_ref, lambda k: sign * (k - rim)), LANES)
    gap = iota((LANES, LANES), 1) - iota((LANES, LANES), 0)
    return jnp.where(jnp.abs(gap) <= rim, rolled, 0.0).astype(BF16)


def row_band_forward(taps_ref, rim, frames):
    out_rows, depth, span = BLOCK * frames, 3 * BLOCK * frames, 3 * BLOCK
    band = toeplitz(tap_row(taps_ref, lambda k: k + BLOCK - rim), BLOCK)[:, :span].astype(BF16)
    left = (quotient(iota((out_rows, BLOCK), 0), frames) == iota((out_rows, BLOCK), 1)).astype(BF16)
    right = (remainder(iota((span, depth), 1), span) == iota((span, depth), 0)).astype(BF16)
    tall = jnp.dot(left, band, preferred_element_type=F32).astype(BF16)
    spread = jnp.dot(tall, right, preferred_element_type=F32)
    start = iota((out_rows, depth), 1) - span * remainder(iota((out_rows, depth), 0), frames)
    return jnp.where((start >= 0) & (start < span), spread, 0.0).astype(BF16)


def row_band_adjoint(taps_ref, rim, frames):
    out_rows, depth, span = BLOCK * frames, 3 * BLOCK * frames, 3 * BLOCK
    band = toeplitz(tap_row(taps_ref, lambda k: BLOCK + rim - k), BLOCK)[:, :span].astype(BF16)
    left = (remainder(iota((out_rows, BLOCK), 0), BLOCK) == iota((out_rows, BLOCK), 1)).astype(BF16)
    right = (quotient(iota((span, depth), 1), frames) == iota((span, depth), 0)).astype(BF16)
    tall = jnp.dot(left, band, preferred_element_type=F32).astype(BF16)
    spread = jnp.dot(tall, right, preferred_element_type=F32)
    same = remainder(iota((out_rows, depth), 1), frames) == quotient(iota((out_rows, depth), 0), BLOCK)
    return jnp.where(same, spread, 0.0).astype(BF16)


def aligned(start, size):
    return pl.ds(start if size % 8 else pl.multiple_of(start, size), size)


def half_of(flip, far, wide):
    return (lax.axis_index(PLANE) ^ flip) * 2 + (quotient(lax.axis_index(WIDE), wide // 2) ^ far)


def per_frame(rows, frames, copies):
    tall = jnp.broadcast_to(rows[:, None, :], (BLOCK, frames, LANES)).reshape(BLOCK * frames, LANES)
    return tall if copies == 1 else jnp.concatenate([tall] * copies, axis=1)


def prepare_kernel(
    rim, cuts, col_hbm, row_hbm, movie_hbm, mask_hbm, support_hbm, templates_hbm,
    smooth_ref, col_fwd_ref, row_fwd_ref, code_ref, templates_ref, flat_ref,
    movie_ref, mask_ref, support_ref, packed_ref, loose_ref, col_ref, row_ref, sems,
):
    planes, frames, rows, _ = movie_ref.shape
    some = frames // cuts

    def fetch(n, source, target):
        copy = pltpu.make_async_copy(source, target, sems.at[n])
        copy.start()
        return copy

    tap_copies = [fetch(0, col_hbm, col_ref), fetch(1, row_hbm, row_ref)]
    movie_copies = []
    for n in range(planes * cuts):
        piece = (n // cuts, pl.ds(n % cuts * some, some))
        movie_copies.append(fetch(5 + n, movie_hbm.at[piece], movie_ref.at[piece]))
    packed_copy = fetch(2, templates_hbm, packed_ref)
    code_copies = [fetch(3, mask_hbm, mask_ref), fetch(4, support_hbm, support_ref)]
    for copy in tap_copies:
        copy.wait()
    col_fwd = column_band(col_ref, rim, -1)
    col_fwd_ref[...] = col_fwd
    row_fwd_ref[...] = row_band_forward(row_ref, rim, frames)
    for copy in (*movie_copies, packed_copy, *code_copies):
        copy.wait()
    loose_ref[...] = packed_ref[...].astype(F32)
    code_ref[...] = support_ref[...] * 2 + mask_ref[...]
    unit = (iota((LANES, LANES), 0) == iota((LANES, LANES), 1)).astype(BF16)
    for n in range(planes * cuts):
        p, first = n // cuts, n % cuts * some
        full = jnp.dot(
            movie_ref[p, first : first + some].reshape(some * rows, LANES), col_fwd,
            preferred_element_type=F32,
        )
        smooth_ref[first : first + some, BLOCK : BLOCK + rows, p * LANES : (p + 1) * LANES] = (
            full.astype(BF16).reshape(some, rows, LANES)
        )
    for p in range(planes):
        shapes = loose_ref[pl.ds(p, templates_ref.shape[1], stride=planes), :].astype(BF16)
        flat_ref[:, p * LANES : (p + 1) * LANES] = shapes
        templates_ref[p * LANES : (p + 1) * LANES, :] = lax.dot_general(
            unit, shapes, (((1,), (1,)), ((), ())), preferred_element_type=F32
        ).astype(BF16)


def forward_kernel(
    flip, far, fill, wide, ks, smooth_in_ref, edge_ref, col_fwd_ref, row_fwd_ref, code_ref,
    templates_ref, smooth_ref, filtered_ref, out_ref, projected_ref,
):
    frames, padded_rows, width = smooth_ref.shape
    planes, rows = width // LANES, padded_rows - 2 * BLOCK
    if fill:
        for p in range(planes):
            edge = jnp.dot(
                edge_ref[p].reshape(frames * BLOCK, LANES), col_fwd_ref[...],
                preferred_element_type=F32,
            ).reshape(frames, BLOCK, LANES)
            lanes = slice(p * LANES, (p + 1) * LANES)
            above = jnp.where(lax.axis_index(REP) > 0, edge, 0.0).astype(BF16)
            below = jnp.where(lax.axis_index(REP) > 0, 0.0, edge).astype(BF16)
            smooth_ref[:, :BLOCK, lanes] = above
            smooth_ref[:, BLOCK + rows :, lanes] = below
    here = filtered_ref.shape[0] // frames
    first = half_of(flip, far, wide) * here
    tiles = templates_ref.shape[1] // LANES
    def along(b):
        near = smooth_ref[:, pl.ds(pl.multiple_of(first + b * BLOCK, BLOCK), 3 * BLOCK), :]
        near = near.reshape(frames * 3 * BLOCK, width)
        return jnp.dot(row_fwd_ref[...], near, preferred_element_type=F32)

    cells = along(0)
    for b in range(here // BLOCK):
        code = code_ref[pl.ds(pl.multiple_of(first + b * BLOCK, BLOCK), BLOCK), :]
        mask = per_frame((code & 1).astype(F32), frames, planes)
        filtered = (cells * mask).astype(BF16)
        spot = slice(b * BLOCK * frames, (b + 1) * BLOCK * frames)
        filtered_ref[spot, :] = filtered
        dense = jnp.dot(filtered, templates_ref[...], preferred_element_type=F32)
        cells = along(b + 1) if b + 1 < here // BLOCK else None
        picked = per_frame(code >> 1, frames, 1)
        lane, tile = picked & (LANES - 1), quotient(picked, LANES)
        chosen = jnp.zeros(picked.shape, F32)
        for t in range(tiles):
            found = jnp.take_along_axis(
                dense[:, t * LANES : (t + 1) * LANES], lane, axis=1, mode="promise_in_bounds"
            )
            chosen = jnp.where(tile == t, found, chosen)
        projected_ref[spot, :] = chosen.astype(BF16)
    size = out_ref.shape[0] // len(ks)
    for i, k in enumerate(ks):
        start = pl.multiple_of(((lax.axis_index(WIDE) ^ k) & (wide // 2 - 1)) * size, size)
        out_ref[i * size : (i + 1) * size, :] = projected_ref[pl.ds(start, size), :]


def add_all(parts, spots, rows):
    total = None
    for part, spot in zip(parts, spots):
        term = part[spot * rows : (spot + 1) * rows, :].astype(F32)
        total = term if total is None else total + term
    return total.astype(BF16)


def sum_kernel(spots, lag_ref, *refs):
    parts, out_ref = refs[:-1], refs[-1]
    rows = out_ref.shape[0] - lag_ref.shape[0]
    out_ref[:rows, :] = add_all(parts, spots, rows)
    out_ref[rows:, :] = lag_ref[...]


def mix_kernel(wide, spots, owner_ref, lag_ref, *refs):
    parts, refs = refs[: len(spots)], refs[len(spots) :]
    blocks, outs = refs[: wide - 1], refs[wide - 1 : 2 * wide - 1]
    cells_ref, kernels_ref, traces_ref = refs[2 * wide - 1 :]
    _, share, frames, lanes = cells_ref.shape
    total = wide * frames
    here = lax.axis_index(WIDE)
    cells_ref[here] = add_all(parts, spots, share * frames).reshape(share, frames, lanes)
    kernels_ref[here] = lag_ref[...].astype(F32)
    for k, block in enumerate(blocks, 1):
        cells_ref[here ^ k] = block[: share * frames, :].reshape(share, frames, lanes)
        kernels_ref[here ^ k] = block[share * frames :, :].astype(F32)
    first = (lax.axis_index(PLANE) * wide + here) * share
    owners = owner_ref[...]
    lane = iota(owners.shape, 1)
    for h in range(share):
        owner = jnp.sum(jnp.where(lane == first + h, owners, 0), axis=1, keepdims=True)
        owner = jnp.broadcast_to(owner, (8, lanes))
        row = []
        for i in range(0, kernels_ref.shape[1], 8):
            values = jnp.zeros((8, lanes), F32)
            for d in range(wide):
                values = jnp.where(owner == d, kernels_ref[d, i : i + 8, :], values)
            row += [values[n : n + 1, :] for n in range(8)]
        row = jnp.concatenate(row[: 2 * total // lanes], axis=1)
        lag = toeplitz(row, total, total + 1)[:, :total].astype(BF16)
        mixed = jnp.dot(lag, cells_ref[:, h].reshape(total, lanes), preferred_element_type=F32)
        traces_ref[:, h] = jnp.maximum(mixed, 0.0).astype(BF16).reshape(wide, frames, lanes)
    for k, out_ref in enumerate(outs):
        out_ref[...] = traces_ref[here ^ k]


def bands_kernel(rim, frames, col_ref, row_ref, col_adj_ref, row_adj_ref):
    band = column_band(col_ref, rim, 1)
    col_adj_ref[...] = jnp.zeros_like(col_adj_ref)
    for p in range(col_adj_ref.shape[0] // LANES):
        lanes = slice(p * LANES, (p + 1) * LANES)
        col_adj_ref[lanes, lanes] = band
    row_adj_ref[...] = row_band_adjoint(row_ref, rim, frames)


def residual_kernel(flip, far, wide, spots, filtered_ref, code_ref, templates_ref, *refs):
    traces, (out_ref, edge_ref, ordered_ref, slots_ref) = refs[:-4], refs[-4:]
    _, frames, lanes = traces[0].shape
    share = ordered_ref.shape[0] // len(spots)
    names, width = templates_ref.shape
    tile = 2 * LANES
    base = half_of(flip, far, wide) * len(spots) * share
    marks = iota((lanes, tile), 1).astype(F32).astype(BF16)
    group = min(8, share)
    for n, (k, source, offset) in enumerate(spots):
        block = (lax.axis_index(WIDE) ^ k) & (wide // 2 - 1)
        source, offset = traces[source], offset * share
        top = base + block * share
        for g in range(share // group):
            support = code_ref[aligned(top + g * group, group), :] >> 1
            support = jnp.concatenate([support] * (8 // group), axis=0)
            columns = jnp.transpose(support.astype(F32))
            for i in range(group):
                h = g * group + i
                named = jnp.broadcast_to(columns[:, i : i + 1], (lanes, lanes))
                hits = []
                for t in range(names // tile):
                    offset_name = (named - float(t * tile)).astype(BF16)
                    hits.append(
                        jnp.where(
                            marks == jnp.concatenate([offset_name] * 2, axis=1),
                            jnp.ones((), BF16), jnp.zeros((), BF16),
                        )
                    )
                hits = jnp.concatenate(hits, axis=1)
                slots_ref[n, h * frames : (h + 1) * frames, :] = jnp.dot(
                    source[offset + h], hits, preferred_element_type=F32
                ).astype(BF16)
        model = jnp.dot(slots_ref[n], templates_ref[...], preferred_element_type=F32)
        mask = (code_ref[aligned(top, share), :] & 1).astype(F32)
        mask = jnp.broadcast_to(mask[:, None, :], (share, frames, lanes)).reshape(-1, lanes)
        size = share * frames
        spot = pl.ds(pl.multiple_of(block * size, size), size)
        out_ref[spot, :] = (
            filtered_ref[spot, :].astype(F32)
            - jnp.concatenate([mask] * (width // lanes), axis=1) * model
        ).astype(BF16)
        ordered_ref[pl.ds(block * share, share)] = source[offset : offset + share]
    edge = edge_ref.shape[0]
    start = jnp.where(lax.axis_index(REP) > 0, 0, out_ref.shape[0] - edge)
    edge_ref[...] = out_ref[pl.ds(pl.multiple_of(start, edge), edge), :]


def backward_kernel(keys, wide, edge_ref, col_adj_ref, row_adj_ref, *refs):
    parts, (out_hbm, padded_ref, out_ref, sems) = refs[: len(keys)], refs[len(keys) :]
    planes, frames, rows, _ = out_ref.shape
    edge, size = BLOCK * frames, parts[0].shape[0]
    zero = jnp.zeros_like(edge_ref)
    padded_ref[:edge, :] = jnp.where(lax.axis_index(REP) > 0, edge_ref[...], zero)
    padded_ref[edge + rows * frames :, :] = jnp.where(lax.axis_index(REP) > 0, zero, edge_ref[...])
    for (flip, far), part in zip(keys, parts):
        spot = pl.multiple_of(edge + half_of(flip, far, wide) * size, edge)
        padded_ref[pl.ds(spot, size), :] = part[...]
    def along(b):
        near = padded_ref[b * edge : (b + 3) * edge, :]
        return jnp.dot(row_adj_ref[...], near, preferred_element_type=F32).astype(BF16)

    copies = []
    back = along(0)
    for b in range(rows // BLOCK):
        ahead = along(b + 1) if b + 1 < rows // BLOCK else None
        full = jnp.dot(back, col_adj_ref[...], preferred_element_type=F32).astype(BF16)
        for p in range(planes):
            out_ref[p, :, b * BLOCK : (b + 1) * BLOCK, :] = full[
                :, p * LANES : (p + 1) * LANES
            ].reshape(frames, BLOCK, LANES)
        piece = (slice(None), slice(None), pl.ds(b * BLOCK, BLOCK))
        copy = pltpu.make_async_copy(out_ref.at[piece], out_hbm.at[piece], sems.at[b])
        copy.start()
        copies.append(copy)
        back = ahead
    for copy in copies:
        copy.wait()


VMEM = pl.BlockSpec(memory_space=pltpu.VMEM)
SMEM = pl.BlockSpec(memory_space=pltpu.SMEM)
HBM = pl.BlockSpec(memory_space=pltpu.HBM)


def shaped(shape):
    return jax.ShapeDtypeStruct(shape, BF16)


def call(kernel, name, outs, smem, vmem, scratch=(), aliases=None):
    return pl.pallas_call(
        kernel,
        out_shape=tuple(shaped(s) if isinstance(s, tuple) else s for s in outs),
        in_specs=[SMEM] * smem + [VMEM] * vmem,
        out_specs=(VMEM,) * len(outs),
        scratch_shapes=scratch,
        input_output_aliases=aliases or {},
        compiler_params=pltpu.CompilerParams(vmem_limit_bytes=32 * 1024 * 1024),
        name=name,
    )


def lag_kernel_values(gains, lags, frame_count):
    taps = gains.shape[1]
    lag_values = jnp.arange(2 * frame_count, dtype=jnp.int32) - (frame_count - 1)
    offsets = jnp.arange(taps, dtype=jnp.int32) - (taps - 1) // 2
    hits = lag_values[None, :, None] == lags[:, None, None] * offsets[None, None, :]
    spread = jnp.where(hits, gains[:, None, :], jnp.zeros((), gains.dtype))
    return jnp.sum(spread, axis=(0, 2)).astype(BF16)


def on_device(
    movie_frames, pixel_mask, tile_owner, support, templates, row_taps, col_taps, lag_gains, dilations
):
    planes, frames, rows, cols = movie_frames.shape
    wide, plane_count = lax.axis_size("wide"), lax.axis_size("planes")
    rim = (row_taps.shape[0] - 1) // 2
    total_frames, width = frames * wide, planes * cols
    here = rows // plane_count
    share = here // wide
    edge = BLOCK * frames
    rep, plane, spot = lax.axis_index("rep"), lax.axis_index("planes"), lax.axis_index("wide")
    mib = 1 << 20

    start = jnp.where(rep == 0, rows - BLOCK, 0)
    rim_rows = exchange(lax.dynamic_slice_in_dim(movie_frames, start, BLOCK, axis=2), "rep", 1)
    cuts = 2
    depth, names = 3 * BLOCK * frames, templates.shape[0]
    smooth, col_fwd, row_fwd, code, tall_templates, flat_templates = pl.pallas_call(
        functools.partial(prepare_kernel, rim, cuts),
        out_shape=(
            shaped((frames, rows + 2 * BLOCK, width)), shaped((cols, cols)), shaped((edge, depth)),
            jax.ShapeDtypeStruct(support.shape, jnp.int32), shaped((width, names)),
            shaped((names, width)),
        ),
        in_specs=[HBM] * 6,
        out_specs=(VMEM,) * 6,
        scratch_shapes=[
            pltpu.VMEM(movie_frames.shape, BF16),
            pltpu.VMEM(pixel_mask.shape, jnp.int32),
            pltpu.VMEM(support.shape, jnp.int32),
            pltpu.VMEM((names * planes, cols), BF16),
            pltpu.VMEM((names * planes, cols), F32),
            pltpu.SMEM(col_taps.shape, F32),
            pltpu.SMEM(row_taps.shape, F32),
            pltpu.SemaphoreType.DMA((5 + planes * cuts,)),
        ],
        compiler_params=pltpu.CompilerParams(vmem_limit_bytes=32 * mib),
        name="prepare",
    )(
        *[
            pltpu.with_memory_space_constraint(x, pltpu.HBM)
            for x in (
                col_taps, row_taps, movie_frames, pixel_mask, support,
                templates.reshape(names * planes, cols),
            )
        ]
    )

    near_ks, far_ks = list(range(wide // 2)), list(range(wide // 2, wide))
    halves = {1: far_ks, 0: near_ks[::-1]}
    half_rows = here // 2
    filtered, projected = {}, {}
    flips = [(turn + 1) % plane_count for turn in range(plane_count)]
    keys = [(flip, far) for far in (1, 0) for flip in flips]
    for turn, (flip, far) in enumerate(keys):
        smooth, filtered[flip, far], mine = call(
            functools.partial(forward_kernel, flip, far, turn == 0, wide, halves[far]), "forward",
            [smooth.shape, (half_rows * frames, width), (half_rows * frames, LANES)],
            0, 6, aliases={0: 0},
            scratch=[pltpu.VMEM((half_rows * frames, LANES), BF16)],
        )(smooth, rim_rows, col_fwd, row_fwd, code, tall_templates)
        projected[flip, far] = exchange(mine, "planes", flip) if flip else mine
        if turn == 0:
            gains, lags, _ = lax.optimization_barrier((lag_gains, dilations, smooth))
            kernel_row = lag_kernel_values(gains[0], lags[0], total_frames)
            lag_rows = -(-2 * total_frames // (LANES * BLOCK)) * BLOCK
            kernel_row = jnp.pad(kernel_row, (0, lag_rows * LANES - 2 * total_frames))
            kernel_row = kernel_row.reshape(lag_rows, LANES)

    block_rows = share * frames + lag_rows
    sums, blocks = {}, {}

    def parts_of(k):
        far = int(k in far_ks)
        spots = [halves[far].index(k)] * plane_count
        return spots, [projected[flip, far] for flip in range(plane_count)]

    for k in near_ks[1:] + far_ks:
        spots, parts = parts_of(k)
        (sums[k],) = call(
            functools.partial(sum_kernel, spots), "sum", [(block_rows, LANES)],
            0, 1 + plane_count,
        )(kernel_row, *parts)
        blocks[k] = exchange(sums[k], "wide", k)

    late_col, late_row, _ = lax.optimization_barrier(
        (col_taps, row_taps, list(sums.values()))
    )
    col_adj, row_adj = call(
        functools.partial(bands_kernel, rim, frames), "bands", [(width, width), (edge, depth)],
        2, 0,
    )(late_col, late_row)
    own_spots, own_parts = parts_of(0)
    own_parts[0], col_adj, row_adj = lax.optimization_barrier((own_parts[0], col_adj, row_adj))

    cell_shape = (wide, share, frames, LANES)
    traces = call(
        functools.partial(mix_kernel, wide, own_spots), "mix", [cell_shape[1:]] * wide,
        0, 1 + wide + plane_count,
        scratch=[
            pltpu.VMEM(cell_shape, BF16), pltpu.VMEM((wide, lag_rows, LANES), F32),
            pltpu.VMEM(cell_shape, BF16),
        ],
    )(
        tile_owner.reshape(1, rows), kernel_row, *own_parts, *[blocks[k] for k in range(1, wide)],
    )
    swapped = {k: exchange(traces[k], "wide", k) for k in far_ks + near_ks[1:]}
    swapped[0] = traces[0]
    late = range(1, plane_count)
    near = jnp.concatenate([swapped[k] for k in near_ks])
    passed = {flip: exchange(near, "planes", flip) for flip in late}

    residual, edges, ordered = {}, {}, {}
    back_keys = [(flip, far) for flip in range(plane_count) for far in (0, 1)]

    def subtract(flip, far, groups, got):
        spots = [(k, n, i) for n, ks in enumerate(groups) for i, k in enumerate(ks)]
        residual[flip, far], edges[flip, far], ordered[flip, far] = call(
            functools.partial(residual_kernel, flip, far, wide, spots), "residual",
            [(half_rows * frames, width), (edge, width), (half_rows, frames, LANES)],
            0, 3 + len(got), scratch=[pltpu.VMEM((len(spots), share * frames, names), BF16)],
        )(filtered[flip, far], code, flat_templates, *got)

    subtract(0, 0, [near_ks], [near])
    distant, _ = lax.optimization_barrier(([swapped[k] for k in far_ks], edges[0, 0]))
    joined = jnp.concatenate(distant)
    subtract(0, 1, [[k] for k in far_ks], distant)
    for flip in late:
        subtract(flip, 0, [near_ks], [passed[flip]])
        subtract(flip, 1, [far_ks], [exchange(joined, "planes", flip)])

    def pick(table, part, half):
        found = table[0, 0]
        for flip, far in back_keys[1:]:
            here_it_is = ((plane ^ part) == flip) & ((spot // (wide // 2) ^ half) == far)
            found = jnp.where(here_it_is, table[flip, far], found)
        return found

    tip = pick(edges, jnp.where(rep == 0, plane_count - 1, 0), jnp.where(rep == 0, 1, 0))
    tip = exchange(tip, "rep", 1)

    foot_share = support.shape[1] // plane_count
    in_order = [pick(ordered, q, half) for q in range(plane_count) for half in (0, 1)]
    mine = lax.dynamic_slice_in_dim(jnp.concatenate(in_order), plane * foot_share, foot_share, 2)
    trace_out = jnp.transpose(mine, (2, 1, 0))

    back_projected = pl.pallas_call(
        functools.partial(backward_kernel, back_keys, wide),
        out_shape=shaped(movie_frames.shape),
        in_specs=[VMEM] * (3 + len(back_keys)),
        out_specs=HBM,
        scratch_shapes=[
            pltpu.VMEM(((rows + 2 * BLOCK) * frames, width), BF16),
            pltpu.VMEM(movie_frames.shape, BF16),
            pltpu.SemaphoreType.DMA((rows // BLOCK,)),
        ],
        compiler_params=pltpu.CompilerParams(vmem_limit_bytes=32 * mib),
        name="backward",
    )(tip, col_adj, row_adj, *[residual[key] for key in back_keys])
    return trace_out, back_projected


def solution(mesh):
    return jax.shard_map(
        on_device,
        mesh=mesh,
        in_specs=(
            P("planes", ("groups", "wide"), "rep", None),
            P("rep", None),
            P("rep", None),
            P("rep", None),
            P(None, "planes", None),
            P(),
            P(),
            P("wide", None, None),
            P("wide", None),
        ),
        out_specs=(
            P("planes", ("groups", "wide"), "rep"),
            P("planes", ("groups", "wide"), "rep", None),
        ),
        check_vma=False,
    )
```

```python
import functools

import jax
import jax.numpy as jnp
from jax import lax
from jax.experimental import pallas as pl
from jax.experimental.pallas import tpu as pltpu
from jax.sharding import PartitionSpec as P

BLOCK = 16
LANES = 128
F32 = jnp.float32
BF16 = jnp.bfloat16
REP, PLANE, WIDE = "rep", "planes", "wide"


def exchange(cells, axis, flip):
    count = lax.axis_size(axis)
    return lax.ppermute(cells, axis, [(i, i ^ flip) for i in range(count)])


def iota(shape, dim):
    return lax.broadcasted_iota(jnp.int32, shape, dim)


def tap_row(taps_ref, place):
    lane = iota((8, LANES), 1)
    row = jnp.zeros((8, LANES), F32)
    for k in range(taps_ref.shape[0]):
        row = jnp.where(lane == place(k) % LANES, taps_ref[k], row)
    return row[:1]


def quotient(x, n):
    if n & (n - 1) == 0:
        return lax.shift_right_logical(x, n.bit_length() - 1)
    return lax.shift_right_logical(x * (65536 // n + 1), 16)


def remainder(x, n):
    return x & (n - 1) if n & (n - 1) == 0 else x - n * quotient(x, n)


def toeplitz(row, count, shift=0):
    return pltpu.roll(
        jnp.broadcast_to(row, (count, row.shape[1])), shift, 1, stride=1, stride_axis=0
    )


def column_band(taps_ref, rim, sign):
    rolled = toeplitz(tap_row(taps_ref, lambda k: sign * (k - rim)), LANES)
    gap = iota((LANES, LANES), 1) - iota((LANES, LANES), 0)
    return jnp.where(jnp.abs(gap) <= rim, rolled, 0.0).astype(BF16)


def row_band_forward(taps_ref, rim, frames):
    out_rows, depth, span = BLOCK * frames, 3 * BLOCK * frames, 3 * BLOCK
    band = toeplitz(tap_row(taps_ref, lambda k: k + BLOCK - rim), BLOCK)[:, :span].astype(BF16)
    left = (quotient(iota((out_rows, BLOCK), 0), frames) == iota((out_rows, BLOCK), 1)).astype(BF16)
    right = (remainder(iota((span, depth), 1), span) == iota((span, depth), 0)).astype(BF16)
    tall = jnp.dot(left, band, preferred_element_type=F32).astype(BF16)
    spread = jnp.dot(tall, right, preferred_element_type=F32)
    start = iota((out_rows, depth), 1) - span * remainder(iota((out_rows, depth), 0), frames)
    return jnp.where((start >= 0) & (start < span), spread, 0.0).astype(BF16)


def row_band_adjoint(taps_ref, rim, frames):
    out_rows, depth, span = BLOCK * frames, 3 * BLOCK * frames, 3 * BLOCK
    band = toeplitz(tap_row(taps_ref, lambda k: BLOCK + rim - k), BLOCK)[:, :span].astype(BF16)
    left = (remainder(iota((out_rows, BLOCK), 0), BLOCK) == iota((out_rows, BLOCK), 1)).astype(BF16)
    right = (quotient(iota((span, depth), 1), frames) == iota((span, depth), 0)).astype(BF16)
    tall = jnp.dot(left, band, preferred_element_type=F32).astype(BF16)
    spread = jnp.dot(tall, right, preferred_element_type=F32)
    same = remainder(iota((out_rows, depth), 1), frames) == quotient(iota((out_rows, depth), 0), BLOCK)
    return jnp.where(same, spread, 0.0).astype(BF16)


def aligned(start, size):
    return pl.ds(start if size % 8 else pl.multiple_of(start, size), size)


def half_of(flip, far, wide):
    return (lax.axis_index(PLANE) ^ flip) * 2 + (quotient(lax.axis_index(WIDE), wide // 2) ^ far)


def per_frame(rows, frames, copies):
    tall = jnp.broadcast_to(rows[:, None, :], (BLOCK, frames, LANES)).reshape(BLOCK * frames, LANES)
    return tall if copies == 1 else jnp.concatenate([tall] * copies, axis=1)


def prepare_kernel(
    rim, cuts, col_hbm, row_hbm, movie_hbm, mask_hbm, support_hbm, templates_hbm,
    smooth_ref, col_fwd_ref, row_fwd_ref, code_ref, templates_ref, flat_ref,
    movie_ref, mask_ref, support_ref, packed_ref, loose_ref, col_ref, row_ref, sems,
):
    planes, frames, rows, _ = movie_ref.shape
    some = frames // cuts

    def fetch(n, source, target):
        copy = pltpu.make_async_copy(source, target, sems.at[n])
        copy.start()
        return copy

    tap_copies = [fetch(0, col_hbm, col_ref), fetch(1, row_hbm, row_ref)]
    movie_copies = []
    for n in range(planes * cuts):
        piece = (n // cuts, pl.ds(n % cuts * some, some))
        movie_copies.append(fetch(5 + n, movie_hbm.at[piece], movie_ref.at[piece]))
    packed_copy = fetch(2, templates_hbm, packed_ref)
    code_copies = [fetch(3, mask_hbm, mask_ref), fetch(4, support_hbm, support_ref)]
    for copy in tap_copies:
        copy.wait()
    col_fwd = column_band(col_ref, rim, -1)
    col_fwd_ref[...] = col_fwd
    row_fwd_ref[...] = row_band_forward(row_ref, rim, frames)
    for copy in (*movie_copies, packed_copy, *code_copies):
        copy.wait()
    loose_ref[...] = packed_ref[...].astype(F32)
    code_ref[...] = support_ref[...] * 2 + mask_ref[...]
    unit = (iota((LANES, LANES), 0) == iota((LANES, LANES), 1)).astype(BF16)
    for n in range(planes * cuts):
        p, first = n // cuts, n % cuts * some
        full = jnp.dot(
            movie_ref[p, first : first + some].reshape(some * rows, LANES), col_fwd,
            preferred_element_type=F32,
        )
        smooth_ref[first : first + some, BLOCK : BLOCK + rows, p * LANES : (p + 1) * LANES] = (
            full.astype(BF16).reshape(some, rows, LANES)
        )
    for p in range(planes):
        shapes = loose_ref[pl.ds(p, templates_ref.shape[1], stride=planes), :].astype(BF16)
        flat_ref[:, p * LANES : (p + 1) * LANES] = shapes
        templates_ref[p * LANES : (p + 1) * LANES, :] = lax.dot_general(
            unit, shapes, (((1,), (1,)), ((), ())), preferred_element_type=F32
        ).astype(BF16)


def forward_kernel(
    flip, far, fill, wide, ks, smooth_in_ref, edge_ref, col_fwd_ref, row_fwd_ref, code_ref,
    templates_ref, smooth_ref, filtered_ref, out_ref, projected_ref,
):
    frames, padded_rows, width = smooth_ref.shape
    planes, rows = width // LANES, padded_rows - 2 * BLOCK
    if fill:
        for p in range(planes):
            edge = jnp.dot(
                edge_ref[p].reshape(frames * BLOCK, LANES), col_fwd_ref[...],
                preferred_element_type=F32,
            ).reshape(frames, BLOCK, LANES)
            lanes = slice(p * LANES, (p + 1) * LANES)
            above = jnp.where(lax.axis_index(REP) > 0, edge, 0.0).astype(BF16)
            below = jnp.where(lax.axis_index(REP) > 0, 0.0, edge).astype(BF16)
            smooth_ref[:, :BLOCK, lanes] = above
            smooth_ref[:, BLOCK + rows :, lanes] = below
    here = filtered_ref.shape[0] // frames
    first = half_of(flip, far, wide) * here
    tiles = templates_ref.shape[1] // LANES
    def along(b):
        near = smooth_ref[:, pl.ds(pl.multiple_of(first + b * BLOCK, BLOCK), 3 * BLOCK), :]
        near = near.reshape(frames * 3 * BLOCK, width)
        return jnp.dot(row_fwd_ref[...], near, preferred_element_type=F32)

    cells = along(0)
    for b in range(here // BLOCK):
        code = code_ref[pl.ds(pl.multiple_of(first + b * BLOCK, BLOCK), BLOCK), :]
        mask = per_frame((code & 1).astype(F32), frames, planes)
        filtered = (cells * mask).astype(BF16)
        spot = slice(b * BLOCK * frames, (b + 1) * BLOCK * frames)
        filtered_ref[spot, :] = filtered
        dense = jnp.dot(filtered, templates_ref[...], preferred_element_type=F32)
        cells = along(b + 1) if b + 1 < here // BLOCK else None
        picked = per_frame(code >> 1, frames, 1)
        lane, tile = picked & (LANES - 1), quotient(picked, LANES)
        chosen = jnp.zeros(picked.shape, F32)
        for t in range(tiles):
            found = jnp.take_along_axis(
                dense[:, t * LANES : (t + 1) * LANES], lane, axis=1, mode="promise_in_bounds"
            )
            chosen = jnp.where(tile == t, found, chosen)
        projected_ref[spot, :] = chosen.astype(BF16)
    size = out_ref.shape[0] // len(ks)
    for i, k in enumerate(ks):
        start = pl.multiple_of(((lax.axis_index(WIDE) ^ k) & (wide // 2 - 1)) * size, size)
        out_ref[i * size : (i + 1) * size, :] = projected_ref[pl.ds(start, size), :]


def add_all(parts, spots, rows):
    total = None
    for part, spot in zip(parts, spots):
        term = part[spot * rows : (spot + 1) * rows, :].astype(F32)
        total = term if total is None else total + term
    return total.astype(BF16)


def sum_kernel(spots, lag_ref, *refs):
    parts, out_ref = refs[:-1], refs[-1]
    rows = out_ref.shape[0] - lag_ref.shape[0]
    out_ref[:rows, :] = add_all(parts, spots, rows)
    out_ref[rows:, :] = lag_ref[...]


def mix_kernel(wide, spots, owner_ref, lag_ref, *refs):
    parts, refs = refs[: len(spots)], refs[len(spots) :]
    blocks, outs = refs[: wide - 1], refs[wide - 1 : 2 * wide - 1]
    cells_ref, kernels_ref, traces_ref = refs[2 * wide - 1 :]
    _, share, frames, lanes = cells_ref.shape
    total = wide * frames
    here = lax.axis_index(WIDE)
    cells_ref[here] = add_all(parts, spots, share * frames).reshape(share, frames, lanes)
    kernels_ref[here] = lag_ref[...].astype(F32)
    for k, block in enumerate(blocks, 1):
        cells_ref[here ^ k] = block[: share * frames, :].reshape(share, frames, lanes)
        kernels_ref[here ^ k] = block[share * frames :, :].astype(F32)
    first = (lax.axis_index(PLANE) * wide + here) * share
    owners = owner_ref[...]
    lane = iota(owners.shape, 1)
    for h in range(share):
        owner = jnp.sum(jnp.where(lane == first + h, owners, 0), axis=1, keepdims=True)
        owner = jnp.broadcast_to(owner, (8, lanes))
        row = []
        for i in range(0, kernels_ref.shape[1], 8):
            values = jnp.zeros((8, lanes), F32)
            for d in range(wide):
                values = jnp.where(owner == d, kernels_ref[d, i : i + 8, :], values)
            row += [values[n : n + 1, :] for n in range(8)]
        row = jnp.concatenate(row[: 2 * total // lanes], axis=1)
        lag = toeplitz(row, total, total + 1)[:, :total].astype(BF16)
        mixed = jnp.dot(lag, cells_ref[:, h].reshape(total, lanes), preferred_element_type=F32)
        traces_ref[:, h] = jnp.maximum(mixed, 0.0).astype(BF16).reshape(wide, frames, lanes)
    for k, out_ref in enumerate(outs):
        out_ref[...] = traces_ref[here ^ k]


def bands_kernel(rim, frames, col_ref, row_ref, col_adj_ref, row_adj_ref):
    band = column_band(col_ref, rim, 1)
    col_adj_ref[...] = jnp.zeros_like(col_adj_ref)
    for p in range(col_adj_ref.shape[0] // LANES):
        lanes = slice(p * LANES, (p + 1) * LANES)
        col_adj_ref[lanes, lanes] = band
    row_adj_ref[...] = row_band_adjoint(row_ref, rim, frames)


def residual_kernel(flip, far, wide, spots, filtered_ref, code_ref, templates_ref, *refs):
    traces, (out_ref, edge_ref, ordered_ref, slots_ref) = refs[:-4], refs[-4:]
    _, frames, lanes = traces[0].shape
    share = ordered_ref.shape[0] // len(spots)
    names, width = templates_ref.shape
    tile = 2 * LANES
    base = half_of(flip, far, wide) * len(spots) * share
    marks = iota((lanes, tile), 1).astype(F32).astype(BF16)
    group = min(8, share)
    for n, (k, source, offset) in enumerate(spots):
        block = (lax.axis_index(WIDE) ^ k) & (wide // 2 - 1)
        source, offset = traces[source], offset * share
        top = base + block * share
        for g in range(share // group):
            support = code_ref[aligned(top + g * group, group), :] >> 1
            support = jnp.concatenate([support] * (8 // group), axis=0)
            columns = jnp.transpose(support.astype(F32))
            for i in range(group):
                h = g * group + i
                named = jnp.broadcast_to(columns[:, i : i + 1], (lanes, lanes))
                hits = []
                for t in range(names // tile):
                    offset_name = (named - float(t * tile)).astype(BF16)
                    hits.append(
                        jnp.where(
                            marks == jnp.concatenate([offset_name] * 2, axis=1),
                            jnp.ones((), BF16), jnp.zeros((), BF16),
                        )
                    )
                hits = jnp.concatenate(hits, axis=1)
                slots_ref[n, h * frames : (h + 1) * frames, :] = jnp.dot(
                    source[offset + h], hits, preferred_element_type=F32
                ).astype(BF16)
        model = jnp.dot(slots_ref[n], templates_ref[...], preferred_element_type=F32)
        mask = (code_ref[aligned(top, share), :] & 1).astype(F32)
        mask = jnp.broadcast_to(mask[:, None, :], (share, frames, lanes)).reshape(-1, lanes)
        size = share * frames
        spot = pl.ds(pl.multiple_of(block * size, size), size)
        out_ref[spot, :] = (
            filtered_ref[spot, :].astype(F32)
            - jnp.concatenate([mask] * (width // lanes), axis=1) * model
        ).astype(BF16)
        ordered_ref[pl.ds(block * share, share)] = source[offset : offset + share]
    edge = edge_ref.shape[0]
    start = jnp.where(lax.axis_index(REP) > 0, 0, out_ref.shape[0] - edge)
    edge_ref[...] = out_ref[pl.ds(pl.multiple_of(start, edge), edge), :]


def backward_kernel(keys, wide, edge_ref, col_adj_ref, row_adj_ref, *refs):
    parts, (out_hbm, padded_ref, out_ref, sems) = refs[: len(keys)], refs[len(keys) :]
    planes, frames, rows, _ = out_ref.shape
    edge, size = BLOCK * frames, parts[0].shape[0]
    zero = jnp.zeros_like(edge_ref)
    padded_ref[:edge, :] = jnp.where(lax.axis_index(REP) > 0, edge_ref[...], zero)
    padded_ref[edge + rows * frames :, :] = jnp.where(lax.axis_index(REP) > 0, zero, edge_ref[...])
    for (flip, far), part in zip(keys, parts):
        spot = pl.multiple_of(edge + half_of(flip, far, wide) * size, edge)
        padded_ref[pl.ds(spot, size), :] = part[...]
    def along(b):
        near = padded_ref[b * edge : (b + 3) * edge, :]
        return jnp.dot(row_adj_ref[...], near, preferred_element_type=F32).astype(BF16)

    copies = []
    back = along(0)
    for b in range(rows // BLOCK):
        ahead = along(b + 1) if b + 1 < rows // BLOCK else None
        full = jnp.dot(back, col_adj_ref[...], preferred_element_type=F32).astype(BF16)
        for p in range(planes):
            out_ref[p, :, b * BLOCK : (b + 1) * BLOCK, :] = full[
                :, p * LANES : (p + 1) * LANES
            ].reshape(frames, BLOCK, LANES)
        piece = (slice(None), slice(None), pl.ds(b * BLOCK, BLOCK))
        copy = pltpu.make_async_copy(out_ref.at[piece], out_hbm.at[piece], sems.at[b])
        copy.start()
        copies.append(copy)
        back = ahead
    for copy in copies:
        copy.wait()


VMEM = pl.BlockSpec(memory_space=pltpu.VMEM)
SMEM = pl.BlockSpec(memory_space=pltpu.SMEM)
HBM = pl.BlockSpec(memory_space=pltpu.HBM)


def shaped(shape):
    return jax.ShapeDtypeStruct(shape, BF16)


def call(kernel, name, outs, smem, vmem, scratch=(), aliases=None):
    return pl.pallas_call(
        kernel,
        out_shape=tuple(shaped(s) if isinstance(s, tuple) else s for s in outs),
        in_specs=[SMEM] * smem + [VMEM] * vmem,
        out_specs=(VMEM,) * len(outs),
        scratch_shapes=scratch,
        input_output_aliases=aliases or {},
        compiler_params=pltpu.CompilerParams(vmem_limit_bytes=32 * 1024 * 1024),
        name=name,
    )


def lag_kernel_values(gains, lags, frame_count):
    taps = gains.shape[1]
    lag_values = jnp.arange(2 * frame_count, dtype=jnp.int32) - (frame_count - 1)
    offsets = jnp.arange(taps, dtype=jnp.int32) - (taps - 1) // 2
    hits = lag_values[None, :, None] == lags[:, None, None] * offsets[None, None, :]
    spread = jnp.where(hits, gains[:, None, :], jnp.zeros((), gains.dtype))
    return jnp.sum(spread, axis=(0, 2)).astype(BF16)


def on_device(
    movie_frames, pixel_mask, tile_owner, support, templates, row_taps, col_taps, lag_gains, dilations
):
    planes, frames, rows, cols = movie_frames.shape
    wide, plane_count = lax.axis_size("wide"), lax.axis_size("planes")
    rim = (row_taps.shape[0] - 1) // 2
    total_frames, width = frames * wide, planes * cols
    here = rows // plane_count
    share = here // wide
    edge = BLOCK * frames
    rep, plane, spot = lax.axis_index("rep"), lax.axis_index("planes"), lax.axis_index("wide")
    mib = 1 << 20

    start = jnp.where(rep == 0, rows - BLOCK, 0)
    rim_rows = exchange(lax.dynamic_slice_in_dim(movie_frames, start, BLOCK, axis=2), "rep", 1)
    cuts = 2
    depth, names = 3 * BLOCK * frames, templates.shape[0]
    smooth, col_fwd, row_fwd, code, tall_templates, flat_templates = pl.pallas_call(
        functools.partial(prepare_kernel, rim, cuts),
        out_shape=(
            shaped((frames, rows + 2 * BLOCK, width)), shaped((cols, cols)), shaped((edge, depth)),
            jax.ShapeDtypeStruct(support.shape, jnp.int32), shaped((width, names)),
            shaped((names, width)),
        ),
        in_specs=[HBM] * 6,
        out_specs=(VMEM,) * 6,
        scratch_shapes=[
            pltpu.VMEM(movie_frames.shape, BF16),
            pltpu.VMEM(pixel_mask.shape, jnp.int32),
            pltpu.VMEM(support.shape, jnp.int32),
            pltpu.VMEM((names * planes, cols), BF16),
            pltpu.VMEM((names * planes, cols), F32),
            pltpu.SMEM(col_taps.shape, F32),
            pltpu.SMEM(row_taps.shape, F32),
            pltpu.SemaphoreType.DMA((5 + planes * cuts,)),
        ],
        compiler_params=pltpu.CompilerParams(vmem_limit_bytes=32 * mib),
        name="prepare",
    )(
        *[
            pltpu.with_memory_space_constraint(x, pltpu.HBM)
            for x in (
                col_taps, row_taps, movie_frames, pixel_mask, support,
                templates.reshape(names * planes, cols),
            )
        ]
    )

    near_ks, far_ks = list(range(wide // 2)), list(range(wide // 2, wide))
    halves = {1: far_ks, 0: near_ks[::-1]}
    half_rows = here // 2
    filtered, projected = {}, {}
    flips = [(turn + 1) % plane_count for turn in range(plane_count)]
    keys = [(flip, far) for far in (1, 0) for flip in flips]
    for turn, (flip, far) in enumerate(keys):
        smooth, filtered[flip, far], mine = call(
            functools.partial(forward_kernel, flip, far, turn == 0, wide, halves[far]), "forward",
            [smooth.shape, (half_rows * frames, width), (half_rows * frames, LANES)],
            0, 6, aliases={0: 0},
            scratch=[pltpu.VMEM((half_rows * frames, LANES), BF16)],
        )(smooth, rim_rows, col_fwd, row_fwd, code, tall_templates)
        projected[flip, far] = exchange(mine, "planes", flip) if flip else mine
        if turn == 0:
            gains, lags, _ = lax.optimization_barrier((lag_gains, dilations, smooth))
            kernel_row = lag_kernel_values(gains[0], lags[0], total_frames)
            lag_rows = -(-2 * total_frames // (LANES * BLOCK)) * BLOCK
            kernel_row = jnp.pad(kernel_row, (0, lag_rows * LANES - 2 * total_frames))
            kernel_row = kernel_row.reshape(lag_rows, LANES)

    block_rows = share * frames + lag_rows
    sums, blocks = {}, {}

    def parts_of(k):
        far = int(k in far_ks)
        spots = [halves[far].index(k)] * plane_count
        return spots, [projected[flip, far] for flip in range(plane_count)]

    for k in near_ks[1:] + far_ks:
        spots, parts = parts_of(k)
        (sums[k],) = call(
            functools.partial(sum_kernel, spots), "sum", [(block_rows, LANES)],
            0, 1 + plane_count,
        )(kernel_row, *parts)
        blocks[k] = exchange(sums[k], "wide", k)

    late_col, late_row, _ = lax.optimization_barrier(
        (col_taps, row_taps, list(sums.values()))
    )
    col_adj, row_adj = call(
        functools.partial(bands_kernel, rim, frames), "bands", [(width, width), (edge, depth)],
        2, 0,
    )(late_col, late_row)
    own_spots, own_parts = parts_of(0)
    own_parts[0], col_adj, row_adj = lax.optimization_barrier((own_parts[0], col_adj, row_adj))

    cell_shape = (wide, share, frames, LANES)
    traces = call(
        functools.partial(mix_kernel, wide, own_spots), "mix", [cell_shape[1:]] * wide,
        0, 1 + wide + plane_count,
        scratch=[
            pltpu.VMEM(cell_shape, BF16), pltpu.VMEM((wide, lag_rows, LANES), F32),
            pltpu.VMEM(cell_shape, BF16),
        ],
    )(
        tile_owner.reshape(1, rows), kernel_row, *own_parts, *[blocks[k] for k in range(1, wide)],
    )
    swapped = {k: exchange(traces[k], "wide", k) for k in far_ks + near_ks[1:]}
    swapped[0] = traces[0]
    late = range(1, plane_count)
    near = jnp.concatenate([swapped[k] for k in near_ks])
    passed = {flip: exchange(near, "planes", flip) for flip in late}

    residual, edges, ordered = {}, {}, {}
    back_keys = [(flip, far) for flip in range(plane_count) for far in (0, 1)]

    def subtract(flip, far, groups, got):
        spots = [(k, n, i) for n, ks in enumerate(groups) for i, k in enumerate(ks)]
        residual[flip, far], edges[flip, far], ordered[flip, far] = call(
            functools.partial(residual_kernel, flip, far, wide, spots), "residual",
            [(half_rows * frames, width), (edge, width), (half_rows, frames, LANES)],
            0, 3 + len(got), scratch=[pltpu.VMEM((len(spots), share * frames, names), BF16)],
        )(filtered[flip, far], code, flat_templates, *got)

    distant = [swapped[k] for k in far_ks]
    joined = jnp.concatenate(distant)
    subtract(0, 1, [[k] for k in far_ks], distant)
    late_near, _ = lax.optimization_barrier((near, edges[0, 1]))
    subtract(0, 0, [near_ks], [late_near])
    for flip in late:
        subtract(flip, 0, [near_ks], [passed[flip]])
        subtract(flip, 1, [far_ks], [exchange(joined, "planes", flip)])

    def pick(table, part, half):
        found = table[0, 0]
        for flip, far in back_keys[1:]:
            here_it_is = ((plane ^ part) == flip) & ((spot // (wide // 2) ^ half) == far)
            found = jnp.where(here_it_is, table[flip, far], found)
        return found

    tip = pick(edges, jnp.where(rep == 0, plane_count - 1, 0), jnp.where(rep == 0, 1, 0))
    tip = exchange(tip, "rep", 1)

    foot_share = support.shape[1] // plane_count
    in_order = [pick(ordered, q, half) for q in range(plane_count) for half in (0, 1)]
    mine = lax.dynamic_slice_in_dim(jnp.concatenate(in_order), plane * foot_share, foot_share, 2)
    trace_out = jnp.transpose(mine, (2, 1, 0))

    back_projected = pl.pallas_call(
        functools.partial(backward_kernel, back_keys, wide),
        out_shape=shaped(movie_frames.shape),
        in_specs=[VMEM] * (3 + len(back_keys)),
        out_specs=HBM,
        scratch_shapes=[
            pltpu.VMEM(((rows + 2 * BLOCK) * frames, width), BF16),
            pltpu.VMEM(movie_frames.shape, BF16),
            pltpu.SemaphoreType.DMA((rows // BLOCK,)),
        ],
        compiler_params=pltpu.CompilerParams(vmem_limit_bytes=32 * mib),
        name="backward",
    )(tip, col_adj, row_adj, *[residual[key] for key in back_keys])
    return trace_out, back_projected


def solution(mesh):
    return jax.shard_map(
        on_device,
        mesh=mesh,
        in_specs=(
            P("planes", ("groups", "wide"), "rep", None),
            P("rep", None),
            P("rep", None),
            P("rep", None),
            P(None, "planes", None),
            P(),
            P(),
            P("wide", None, None),
            P("wide", None),
        ),
        out_specs=(
            P("planes", ("groups", "wide"), "rep"),
            P("planes", ("groups", "wide"), "rep", None),
        ),
        check_vma=False,
    )
```

```python
import functools

import jax
import jax.numpy as jnp
from jax import lax
from jax.experimental import pallas as pl
from jax.experimental.pallas import tpu as pltpu
from jax.sharding import PartitionSpec as P

BLOCK = 16
LANES = 128
F32 = jnp.float32
BF16 = jnp.bfloat16
REP, PLANE, WIDE = "rep", "planes", "wide"


def exchange(cells, axis, flip):
    count = lax.axis_size(axis)
    return lax.ppermute(cells, axis, [(i, i ^ flip) for i in range(count)])


def iota(shape, dim):
    return lax.broadcasted_iota(jnp.int32, shape, dim)


def tap_row(taps_ref, place):
    lane = iota((8, LANES), 1)
    row = jnp.zeros((8, LANES), F32)
    for k in range(taps_ref.shape[0]):
        row = jnp.where(lane == place(k) % LANES, taps_ref[k], row)
    return row[:1]


def quotient(x, n):
    if n & (n - 1) == 0:
        return lax.shift_right_logical(x, n.bit_length() - 1)
    return lax.shift_right_logical(x * (65536 // n + 1), 16)


def remainder(x, n):
    return x & (n - 1) if n & (n - 1) == 0 else x - n * quotient(x, n)


def toeplitz(row, count, shift=0):
    return pltpu.roll(
        jnp.broadcast_to(row, (count, row.shape[1])), shift, 1, stride=1, stride_axis=0
    )


def column_band(taps_ref, rim, sign):
    rolled = toeplitz(tap_row(taps_ref, lambda k: sign * (k - rim)), LANES)
    gap = iota((LANES, LANES), 1) - iota((LANES, LANES), 0)
    return jnp.where(jnp.abs(gap) <= rim, rolled, 0.0).astype(BF16)


def row_band_forward(taps_ref, rim, frames):
    out_rows, depth, span = BLOCK * frames, 3 * BLOCK * frames, 3 * BLOCK
    band = toeplitz(tap_row(taps_ref, lambda k: k + BLOCK - rim), BLOCK)[:, :span].astype(BF16)
    left = (quotient(iota((out_rows, BLOCK), 0), frames) == iota((out_rows, BLOCK), 1)).astype(BF16)
    right = (remainder(iota((span, depth), 1), span) == iota((span, depth), 0)).astype(BF16)
    tall = jnp.dot(left, band, preferred_element_type=F32).astype(BF16)
    spread = jnp.dot(tall, right, preferred_element_type=F32)
    start = iota((out_rows, depth), 1) - span * remainder(iota((out_rows, depth), 0), frames)
    return jnp.where((start >= 0) & (start < span), spread, 0.0).astype(BF16)


def row_band_adjoint(taps_ref, rim, frames):
    out_rows, depth, span = BLOCK * frames, 3 * BLOCK * frames, 3 * BLOCK
    band = toeplitz(tap_row(taps_ref, lambda k: BLOCK + rim - k), BLOCK)[:, :span].astype(BF16)
    left = (remainder(iota((out_rows, BLOCK), 0), BLOCK) == iota((out_rows, BLOCK), 1)).astype(BF16)
    right = (quotient(iota((span, depth), 1), frames) == iota((span, depth), 0)).astype(BF16)
    tall = jnp.dot(left, band, preferred_element_type=F32).astype(BF16)
    spread = jnp.dot(tall, right, preferred_element_type=F32)
    same = remainder(iota((out_rows, depth), 1), frames) == quotient(iota((out_rows, depth), 0), BLOCK)
    return jnp.where(same, spread, 0.0).astype(BF16)


def aligned(start, size):
    return pl.ds(start if size % 8 else pl.multiple_of(start, size), size)


def half_of(flip, far, wide):
    return (lax.axis_index(PLANE) ^ flip) * 2 + (quotient(lax.axis_index(WIDE), wide // 2) ^ far)


def per_frame(rows, frames, copies):
    tall = jnp.broadcast_to(rows[:, None, :], (BLOCK, frames, LANES)).reshape(BLOCK * frames, LANES)
    return tall if copies == 1 else jnp.concatenate([tall] * copies, axis=1)


def prepare_kernel(
    rim, cuts, col_hbm, row_hbm, movie_hbm, mask_hbm, support_hbm, templates_hbm,
    smooth_ref, col_fwd_ref, row_fwd_ref, code_ref, templates_ref, flat_ref,
    movie_ref, mask_ref, support_ref, packed_ref, loose_ref, col_ref, row_ref, sems,
):
    planes, frames, rows, _ = movie_ref.shape
    some = frames // cuts

    def fetch(n, source, target):
        copy = pltpu.make_async_copy(source, target, sems.at[n])
        copy.start()
        return copy

    tap_copies = [fetch(0, col_hbm, col_ref), fetch(1, row_hbm, row_ref)]
    movie_copies = []
    for n in range(planes * cuts):
        piece = (n // cuts, pl.ds(n % cuts * some, some))
        movie_copies.append(fetch(5 + n, movie_hbm.at[piece], movie_ref.at[piece]))
    packed_copy = fetch(2, templates_hbm, packed_ref)
    code_copies = [fetch(3, mask_hbm, mask_ref), fetch(4, support_hbm, support_ref)]
    for copy in tap_copies:
        copy.wait()
    col_fwd = column_band(col_ref, rim, -1)
    col_fwd_ref[...] = col_fwd
    row_fwd_ref[...] = row_band_forward(row_ref, rim, frames)
    for copy in (*movie_copies, packed_copy, *code_copies):
        copy.wait()
    loose_ref[...] = packed_ref[...].astype(F32)
    code_ref[...] = support_ref[...] * 2 + mask_ref[...]
    unit = (iota((LANES, LANES), 0) == iota((LANES, LANES), 1)).astype(BF16)
    for n in range(planes * cuts):
        p, first = n // cuts, n % cuts * some
        full = jnp.dot(
            movie_ref[p, first : first + some].reshape(some * rows, LANES), col_fwd,
            preferred_element_type=F32,
        )
        smooth_ref[first : first + some, BLOCK : BLOCK + rows, p * LANES : (p + 1) * LANES] = (
            full.astype(BF16).reshape(some, rows, LANES)
        )
    for p in range(planes):
        shapes = loose_ref[pl.ds(p, templates_ref.shape[1], stride=planes), :].astype(BF16)
        flat_ref[:, p * LANES : (p + 1) * LANES] = shapes
        templates_ref[p * LANES : (p + 1) * LANES, :] = lax.dot_general(
            unit, shapes, (((1,), (1,)), ((), ())), preferred_element_type=F32
        ).astype(BF16)


def forward_kernel(
    flip, far, fill, wide, ks, smooth_in_ref, edge_ref, col_fwd_ref, row_fwd_ref, code_ref,
    templates_ref, smooth_ref, filtered_ref, out_ref, projected_ref,
):
    frames, padded_rows, width = smooth_ref.shape
    planes, rows = width // LANES, padded_rows - 2 * BLOCK
    if fill:
        for p in range(planes):
            edge = jnp.dot(
                edge_ref[p].reshape(frames * BLOCK, LANES), col_fwd_ref[...],
                preferred_element_type=F32,
            ).reshape(frames, BLOCK, LANES)
            lanes = slice(p * LANES, (p + 1) * LANES)
            above = jnp.where(lax.axis_index(REP) > 0, edge, 0.0).astype(BF16)
            below = jnp.where(lax.axis_index(REP) > 0, 0.0, edge).astype(BF16)
            smooth_ref[:, :BLOCK, lanes] = above
            smooth_ref[:, BLOCK + rows :, lanes] = below
    here = filtered_ref.shape[0] // frames
    first = half_of(flip, far, wide) * here
    tiles = templates_ref.shape[1] // LANES
    def along(b):
        near = smooth_ref[:, pl.ds(pl.multiple_of(first + b * BLOCK, BLOCK), 3 * BLOCK), :]
        near = near.reshape(frames * 3 * BLOCK, width)
        return jnp.dot(row_fwd_ref[...], near, preferred_element_type=F32)

    cells = along(0)
    for b in range(here // BLOCK):
        code = code_ref[pl.ds(pl.multiple_of(first + b * BLOCK, BLOCK), BLOCK), :]
        mask = per_frame((code & 1).astype(F32), frames, planes)
        filtered = (cells * mask).astype(BF16)
        spot = slice(b * BLOCK * frames, (b + 1) * BLOCK * frames)
        filtered_ref[spot, :] = filtered
        dense = jnp.dot(filtered, templates_ref[...], preferred_element_type=F32)
        cells = along(b + 1) if b + 1 < here // BLOCK else None
        picked = per_frame(code >> 1, frames, 1)
        lane, tile = picked & (LANES - 1), quotient(picked, LANES)
        chosen = jnp.zeros(picked.shape, F32)
        for t in range(tiles):
            found = jnp.take_along_axis(
                dense[:, t * LANES : (t + 1) * LANES], lane, axis=1, mode="promise_in_bounds"
            )
            chosen = jnp.where(tile == t, found, chosen)
        projected_ref[spot, :] = chosen.astype(BF16)
    size = out_ref.shape[0] // len(ks)
    for i, k in enumerate(ks):
        start = pl.multiple_of(((lax.axis_index(WIDE) ^ k) & (wide // 2 - 1)) * size, size)
        out_ref[i * size : (i + 1) * size, :] = projected_ref[pl.ds(start, size), :]


def add_all(parts, spots, rows):
    total = None
    for part, spot in zip(parts, spots):
        term = part[spot * rows : (spot + 1) * rows, :].astype(F32)
        total = term if total is None else total + term
    return total.astype(BF16)


def sum_kernel(spots, lag_ref, *refs):
    parts, out_ref = refs[:-1], refs[-1]
    rows = out_ref.shape[0] - lag_ref.shape[0]
    out_ref[:rows, :] = add_all(parts, spots, rows)
    out_ref[rows:, :] = lag_ref[...]


def mix_kernel(wide, spots, owner_ref, lag_ref, *refs):
    parts, refs = refs[: len(spots)], refs[len(spots) :]
    blocks, outs = refs[: wide - 1], refs[wide - 1 : 2 * wide - 1]
    cells_ref, kernels_ref, traces_ref = refs[2 * wide - 1 :]
    _, share, frames, lanes = cells_ref.shape
    total = wide * frames
    here = lax.axis_index(WIDE)
    cells_ref[here] = add_all(parts, spots, share * frames).reshape(share, frames, lanes)
    kernels_ref[here] = lag_ref[...].astype(F32)
    for k, block in enumerate(blocks, 1):
        cells_ref[here ^ k] = block[: share * frames, :].reshape(share, frames, lanes)
        kernels_ref[here ^ k] = block[share * frames :, :].astype(F32)
    first = (lax.axis_index(PLANE) * wide + here) * share
    owners = owner_ref[...]
    lane = iota(owners.shape, 1)
    for h in range(share):
        owner = jnp.sum(jnp.where(lane == first + h, owners, 0), axis=1, keepdims=True)
        owner = jnp.broadcast_to(owner, (8, lanes))
        row = []
        for i in range(0, kernels_ref.shape[1], 8):
            values = jnp.zeros((8, lanes), F32)
            for d in range(wide):
                values = jnp.where(owner == d, kernels_ref[d, i : i + 8, :], values)
            row += [values[n : n + 1, :] for n in range(8)]
        row = jnp.concatenate(row[: 2 * total // lanes], axis=1)
        lag = toeplitz(row, total, total + 1)[:, :total].astype(BF16)
        mixed = jnp.dot(lag, cells_ref[:, h].reshape(total, lanes), preferred_element_type=F32)
        traces_ref[:, h] = jnp.maximum(mixed, 0.0).astype(BF16).reshape(wide, frames, lanes)
    for k, out_ref in enumerate(outs):
        out_ref[...] = traces_ref[here ^ k]


def bands_kernel(rim, frames, col_ref, row_ref, col_adj_ref, row_adj_ref):
    band = column_band(col_ref, rim, 1)
    col_adj_ref[...] = jnp.zeros_like(col_adj_ref)
    for p in range(col_adj_ref.shape[0] // LANES):
        lanes = slice(p * LANES, (p + 1) * LANES)
        col_adj_ref[lanes, lanes] = band
    row_adj_ref[...] = row_band_adjoint(row_ref, rim, frames)


def residual_kernel(flip, far, wide, spots, filtered_ref, code_ref, templates_ref, *refs):
    traces, (out_ref, edge_ref, ordered_ref, slots_ref) = refs[:-4], refs[-4:]
    _, frames, lanes = traces[0].shape
    share = ordered_ref.shape[0] // len(spots)
    names, width = templates_ref.shape
    tile = 2 * LANES
    base = half_of(flip, far, wide) * len(spots) * share
    marks = iota((lanes, tile), 1).astype(F32).astype(BF16)
    group = min(8, share)
    for n, (k, source, offset) in enumerate(spots):
        block = (lax.axis_index(WIDE) ^ k) & (wide // 2 - 1)
        source, offset = traces[source], offset * share
        top = base + block * share
        for g in range(share // group):
            support = code_ref[aligned(top + g * group, group), :] >> 1
            support = jnp.concatenate([support] * (8 // group), axis=0)
            columns = jnp.transpose(support.astype(F32))
            for i in range(group):
                h = g * group + i
                named = jnp.broadcast_to(columns[:, i : i + 1], (lanes, lanes))
                hits = []
                for t in range(names // tile):
                    offset_name = (named - float(t * tile)).astype(BF16)
                    hits.append(
                        jnp.where(
                            marks == jnp.concatenate([offset_name] * 2, axis=1),
                            jnp.ones((), BF16), jnp.zeros((), BF16),
                        )
                    )
                hits = jnp.concatenate(hits, axis=1)
                slots_ref[n, h * frames : (h + 1) * frames, :] = jnp.dot(
                    source[offset + h], hits, preferred_element_type=F32
                ).astype(BF16)
        model = jnp.dot(slots_ref[n], templates_ref[...], preferred_element_type=F32)
        mask = (code_ref[aligned(top, share), :] & 1).astype(F32)
        mask = jnp.broadcast_to(mask[:, None, :], (share, frames, lanes)).reshape(-1, lanes)
        size = share * frames
        spot = pl.ds(pl.multiple_of(block * size, size), size)
        out_ref[spot, :] = (
            filtered_ref[spot, :].astype(F32)
            - jnp.concatenate([mask] * (width // lanes), axis=1) * model
        ).astype(BF16)
        ordered_ref[pl.ds(block * share, share)] = source[offset : offset + share]
    edge = edge_ref.shape[0]
    start = jnp.where(lax.axis_index(REP) > 0, 0, out_ref.shape[0] - edge)
    edge_ref[...] = out_ref[pl.ds(pl.multiple_of(start, edge), edge), :]


def backward_kernel(keys, wide, edge_ref, col_adj_ref, row_adj_ref, *refs):
    parts, (out_hbm, padded_ref, out_ref, sems) = refs[: len(keys)], refs[len(keys) :]
    planes, frames, rows, _ = out_ref.shape
    edge, size = BLOCK * frames, parts[0].shape[0]
    zero = jnp.zeros_like(edge_ref)
    padded_ref[:edge, :] = jnp.where(lax.axis_index(REP) > 0, edge_ref[...], zero)
    padded_ref[edge + rows * frames :, :] = jnp.where(lax.axis_index(REP) > 0, zero, edge_ref[...])
    for (flip, far), part in zip(keys, parts):
        spot = pl.multiple_of(edge + half_of(flip, far, wide) * size, edge)
        padded_ref[pl.ds(spot, size), :] = part[...]
    def along(b):
        near = padded_ref[b * edge : (b + 3) * edge, :]
        return jnp.dot(row_adj_ref[...], near, preferred_element_type=F32).astype(BF16)

    copies = []
    back = along(0)
    for b in range(rows // BLOCK):
        ahead = along(b + 1) if b + 1 < rows // BLOCK else None
        full = jnp.dot(back, col_adj_ref[...], preferred_element_type=F32).astype(BF16)
        for p in range(planes):
            out_ref[p, :, b * BLOCK : (b + 1) * BLOCK, :] = full[
                :, p * LANES : (p + 1) * LANES
            ].reshape(frames, BLOCK, LANES)
        piece = (slice(None), slice(None), pl.ds(b * BLOCK, BLOCK))
        copy = pltpu.make_async_copy(out_ref.at[piece], out_hbm.at[piece], sems.at[b])
        copy.start()
        copies.append(copy)
        back = ahead
    for copy in copies:
        copy.wait()


def emit_kernel(keys, wide, *refs):
    parts, (out_hbm, rows_ref, turned_ref, out_ref, sem) = refs[: len(keys)], refs[len(keys) :]
    share, frames, rows = out_ref.shape
    size = rows_ref.shape[0] // len(keys)
    for (flip, far), part in zip(keys, parts):
        spot = pl.multiple_of(half_of(flip, far, wide) * size, size)
        rows_ref[pl.ds(spot, size), :] = part[...].reshape(size, LANES).astype(F32)
    first = lax.axis_index(PLANE) * share
    select = (iota((share, LANES), 1) == iota((share, LANES), 0) + first).astype(BF16)
    for f in range(frames):
        cells = rows_ref[pl.ds(f, rows, stride=frames), :].astype(BF16)
        turned_ref[pl.ds(f, share, stride=frames), :] = lax.dot_general(
            select, cells, (((1,), (1,)), ((), ())), preferred_element_type=F32
        )
    out_ref[...] = turned_ref[...].astype(BF16).reshape(share, frames, rows)
    copy = pltpu.make_async_copy(out_ref, out_hbm, sem)
    copy.start()
    copy.wait()


VMEM = pl.BlockSpec(memory_space=pltpu.VMEM)
SMEM = pl.BlockSpec(memory_space=pltpu.SMEM)
HBM = pl.BlockSpec(memory_space=pltpu.HBM)


def shaped(shape):
    return jax.ShapeDtypeStruct(shape, BF16)


def call(kernel, name, outs, smem, vmem, scratch=(), aliases=None):
    return pl.pallas_call(
        kernel,
        out_shape=tuple(shaped(s) if isinstance(s, tuple) else s for s in outs),
        in_specs=[SMEM] * smem + [VMEM] * vmem,
        out_specs=(VMEM,) * len(outs),
        scratch_shapes=scratch,
        input_output_aliases=aliases or {},
        compiler_params=pltpu.CompilerParams(vmem_limit_bytes=32 * 1024 * 1024),
        name=name,
    )


def lag_kernel_values(gains, lags, frame_count):
    taps = gains.shape[1]
    lag_values = jnp.arange(2 * frame_count, dtype=jnp.int32) - (frame_count - 1)
    offsets = jnp.arange(taps, dtype=jnp.int32) - (taps - 1) // 2
    hits = lag_values[None, :, None] == lags[:, None, None] * offsets[None, None, :]
    spread = jnp.where(hits, gains[:, None, :], jnp.zeros((), gains.dtype))
    return jnp.sum(spread, axis=(0, 2)).astype(BF16)


def on_device(
    movie_frames, pixel_mask, tile_owner, support, templates, row_taps, col_taps, lag_gains, dilations
):
    planes, frames, rows, cols = movie_frames.shape
    wide, plane_count = lax.axis_size("wide"), lax.axis_size("planes")
    rim = (row_taps.shape[0] - 1) // 2
    total_frames, width = frames * wide, planes * cols
    here = rows // plane_count
    share = here // wide
    edge = BLOCK * frames
    rep, plane, spot = lax.axis_index("rep"), lax.axis_index("planes"), lax.axis_index("wide")
    mib = 1 << 20

    start = jnp.where(rep == 0, rows - BLOCK, 0)
    rim_rows = exchange(lax.dynamic_slice_in_dim(movie_frames, start, BLOCK, axis=2), "rep", 1)
    cuts = 2
    depth, names = 3 * BLOCK * frames, templates.shape[0]
    smooth, col_fwd, row_fwd, code, tall_templates, flat_templates = pl.pallas_call(
        functools.partial(prepare_kernel, rim, cuts),
        out_shape=(
            shaped((frames, rows + 2 * BLOCK, width)), shaped((cols, cols)), shaped((edge, depth)),
            jax.ShapeDtypeStruct(support.shape, jnp.int32), shaped((width, names)),
            shaped((names, width)),
        ),
        in_specs=[HBM] * 6,
        out_specs=(VMEM,) * 6,
        scratch_shapes=[
            pltpu.VMEM(movie_frames.shape, BF16),
            pltpu.VMEM(pixel_mask.shape, jnp.int32),
            pltpu.VMEM(support.shape, jnp.int32),
            pltpu.VMEM((names * planes, cols), BF16),
            pltpu.VMEM((names * planes, cols), F32),
            pltpu.SMEM(col_taps.shape, F32),
            pltpu.SMEM(row_taps.shape, F32),
            pltpu.SemaphoreType.DMA((5 + planes * cuts,)),
        ],
        compiler_params=pltpu.CompilerParams(vmem_limit_bytes=32 * mib),
        name="prepare",
    )(
        *[
            pltpu.with_memory_space_constraint(x, pltpu.HBM)
            for x in (
                col_taps, row_taps, movie_frames, pixel_mask, support,
                templates.reshape(names * planes, cols),
            )
        ]
    )

    near_ks, far_ks = list(range(wide // 2)), list(range(wide // 2, wide))
    halves = {1: far_ks, 0: near_ks[::-1]}
    half_rows = here // 2
    filtered, projected = {}, {}
    flips = [(turn + 1) % plane_count for turn in range(plane_count)]
    keys = [(flip, far) for far in (1, 0) for flip in flips]
    for turn, (flip, far) in enumerate(keys):
        smooth, filtered[flip, far], mine = call(
            functools.partial(forward_kernel, flip, far, turn == 0, wide, halves[far]), "forward",
            [smooth.shape, (half_rows * frames, width), (half_rows * frames, LANES)],
            0, 6, aliases={0: 0},
            scratch=[pltpu.VMEM((half_rows * frames, LANES), BF16)],
        )(smooth, rim_rows, col_fwd, row_fwd, code, tall_templates)
        projected[flip, far] = exchange(mine, "planes", flip) if flip else mine
        if turn == 0:
            gains, lags, _ = lax.optimization_barrier((lag_gains, dilations, smooth))
            kernel_row = lag_kernel_values(gains[0], lags[0], total_frames)
            lag_rows = -(-2 * total_frames // (LANES * BLOCK)) * BLOCK
            kernel_row = jnp.pad(kernel_row, (0, lag_rows * LANES - 2 * total_frames))
            kernel_row = kernel_row.reshape(lag_rows, LANES)

    block_rows = share * frames + lag_rows
    sums, blocks = {}, {}

    def parts_of(k):
        far = int(k in far_ks)
        spots = [halves[far].index(k)] * plane_count
        return spots, [projected[flip, far] for flip in range(plane_count)]

    for k in near_ks[1:] + far_ks:
        spots, parts = parts_of(k)
        (sums[k],) = call(
            functools.partial(sum_kernel, spots), "sum", [(block_rows, LANES)],
            0, 1 + plane_count,
        )(kernel_row, *parts)
        blocks[k] = exchange(sums[k], "wide", k)

    late_col, late_row, _ = lax.optimization_barrier(
        (col_taps, row_taps, list(sums.values()))
    )
    col_adj, row_adj = call(
        functools.partial(bands_kernel, rim, frames), "bands", [(width, width), (edge, depth)],
        2, 0,
    )(late_col, late_row)
    own_spots, own_parts = parts_of(0)
    own_parts[0], col_adj, row_adj = lax.optimization_barrier((own_parts[0], col_adj, row_adj))

    cell_shape = (wide, share, frames, LANES)
    traces = call(
        functools.partial(mix_kernel, wide, own_spots), "mix", [cell_shape[1:]] * wide,
        0, 1 + wide + plane_count,
        scratch=[
            pltpu.VMEM(cell_shape, BF16), pltpu.VMEM((wide, lag_rows, LANES), F32),
            pltpu.VMEM(cell_shape, BF16),
        ],
    )(
        tile_owner.reshape(1, rows), kernel_row, *own_parts, *[blocks[k] for k in range(1, wide)],
    )
    swapped = {k: exchange(traces[k], "wide", k) for k in far_ks + near_ks[1:]}
    swapped[0] = traces[0]
    late = range(1, plane_count)
    near = jnp.concatenate([swapped[k] for k in near_ks])
    passed = {flip: exchange(near, "planes", flip) for flip in late}

    residual, edges, ordered = {}, {}, {}
    back_keys = [(flip, far) for flip in range(plane_count) for far in (0, 1)]

    def subtract(flip, far, groups, got):
        spots = [(k, n, i) for n, ks in enumerate(groups) for i, k in enumerate(ks)]
        residual[flip, far], edges[flip, far], ordered[flip, far] = call(
            functools.partial(residual_kernel, flip, far, wide, spots), "residual",
            [(half_rows * frames, width), (edge, width), (half_rows, frames, LANES)],
            0, 3 + len(got), scratch=[pltpu.VMEM((len(spots), share * frames, names), BF16)],
        )(filtered[flip, far], code, flat_templates, *got)

    subtract(0, 0, [near_ks], [near])
    distant, _ = lax.optimization_barrier(([swapped[k] for k in far_ks], edges[0, 0]))
    joined = jnp.concatenate(distant)
    subtract(0, 1, [[k] for k in far_ks], distant)
    for flip in late:
        subtract(flip, 0, [near_ks], [passed[flip]])
        subtract(flip, 1, [far_ks], [exchange(joined, "planes", flip)])

    def pick(table, part, half):
        found = table[0, 0]
        for flip, far in back_keys[1:]:
            here_it_is = ((plane ^ part) == flip) & ((spot // (wide // 2) ^ half) == far)
            found = jnp.where(here_it_is, table[flip, far], found)
        return found

    tip = pick(edges, jnp.where(rep == 0, plane_count - 1, 0), jnp.where(rep == 0, 1, 0))
    tip = exchange(tip, "rep", 1)

    foot_share = support.shape[1] // plane_count
    trace_out = pl.pallas_call(
        functools.partial(emit_kernel, back_keys, wide),
        out_shape=shaped((foot_share, frames, rows)),
        in_specs=[VMEM] * len(back_keys),
        out_specs=HBM,
        scratch_shapes=[
            pltpu.VMEM((rows * frames, LANES), F32),
            pltpu.VMEM((foot_share * frames, rows), F32),
            pltpu.VMEM((foot_share, frames, rows), BF16),
            pltpu.SemaphoreType.DMA(()),
        ],
        compiler_params=pltpu.CompilerParams(vmem_limit_bytes=32 * mib),
        name="emit",
    )(*[ordered[key] for key in back_keys])

    back_projected = pl.pallas_call(
        functools.partial(backward_kernel, back_keys, wide),
        out_shape=shaped(movie_frames.shape),
        in_specs=[VMEM] * (3 + len(back_keys)),
        out_specs=HBM,
        scratch_shapes=[
            pltpu.VMEM(((rows + 2 * BLOCK) * frames, width), BF16),
            pltpu.VMEM(movie_frames.shape, BF16),
            pltpu.SemaphoreType.DMA((rows // BLOCK,)),
        ],
        compiler_params=pltpu.CompilerParams(vmem_limit_bytes=32 * mib),
        name="backward",
    )(tip, col_adj, row_adj, *[residual[key] for key in back_keys])
    return trace_out, back_projected


def solution(mesh):
    return jax.shard_map(
        on_device,
        mesh=mesh,
        in_specs=(
            P("planes", ("groups", "wide"), "rep", None),
            P("rep", None),
            P("rep", None),
            P("rep", None),
            P(None, "planes", None),
            P(),
            P(),
            P("wide", None, None),
            P("wide", None),
        ),
        out_specs=(
            P("planes", ("groups", "wide"), "rep"),
            P("planes", ("groups", "wide"), "rep", None),
        ),
        check_vma=False,
    )
```

```python
import functools

import jax
import jax.numpy as jnp
from jax import lax
from jax.experimental import pallas as pl
from jax.experimental.pallas import tpu as pltpu
from jax.sharding import PartitionSpec as P

BLOCK = 16
LANES = 128
F32 = jnp.float32
BF16 = jnp.bfloat16
REP, PLANE, WIDE = "rep", "planes", "wide"


def exchange(cells, axis, flip):
    count = lax.axis_size(axis)
    return lax.ppermute(cells, axis, [(i, i ^ flip) for i in range(count)])


def iota(shape, dim):
    return lax.broadcasted_iota(jnp.int32, shape, dim)


def tap_row(taps_ref, place):
    lane = iota((8, LANES), 1)
    row = jnp.zeros((8, LANES), F32)
    for k in range(taps_ref.shape[0]):
        row = jnp.where(lane == place(k) % LANES, taps_ref[k], row)
    return row[:1]


def quotient(x, n):
    if n & (n - 1) == 0:
        return lax.shift_right_logical(x, n.bit_length() - 1)
    return lax.shift_right_logical(x * (65536 // n + 1), 16)


def remainder(x, n):
    return x & (n - 1) if n & (n - 1) == 0 else x - n * quotient(x, n)


def toeplitz(row, count, shift=0):
    return pltpu.roll(
        jnp.broadcast_to(row, (count, row.shape[1])), shift, 1, stride=1, stride_axis=0
    )


def column_band(taps_ref, rim, sign):
    rolled = toeplitz(tap_row(taps_ref, lambda k: sign * (k - rim)), LANES)
    gap = iota((LANES, LANES), 1) - iota((LANES, LANES), 0)
    return jnp.where(jnp.abs(gap) <= rim, rolled, 0.0).astype(BF16)


def row_band_forward(taps_ref, rim, frames):
    out_rows, depth, span = BLOCK * frames, 3 * BLOCK * frames, 3 * BLOCK
    band = toeplitz(tap_row(taps_ref, lambda k: k + BLOCK - rim), BLOCK)[:, :span].astype(BF16)
    left = (quotient(iota((out_rows, BLOCK), 0), frames) == iota((out_rows, BLOCK), 1)).astype(BF16)
    right = (remainder(iota((span, depth), 1), span) == iota((span, depth), 0)).astype(BF16)
    tall = jnp.dot(left, band, preferred_element_type=F32).astype(BF16)
    spread = jnp.dot(tall, right, preferred_element_type=F32)
    start = iota((out_rows, depth), 1) - span * remainder(iota((out_rows, depth), 0), frames)
    return jnp.where((start >= 0) & (start < span), spread, 0.0).astype(BF16)


def row_band_adjoint(taps_ref, rim, frames):
    out_rows, depth, span = BLOCK * frames, 3 * BLOCK * frames, 3 * BLOCK
    band = toeplitz(tap_row(taps_ref, lambda k: BLOCK + rim - k), BLOCK)[:, :span].astype(BF16)
    left = (remainder(iota((out_rows, BLOCK), 0), BLOCK) == iota((out_rows, BLOCK), 1)).astype(BF16)
    right = (quotient(iota((span, depth), 1), frames) == iota((span, depth), 0)).astype(BF16)
    tall = jnp.dot(left, band, preferred_element_type=F32).astype(BF16)
    spread = jnp.dot(tall, right, preferred_element_type=F32)
    same = remainder(iota((out_rows, depth), 1), frames) == quotient(iota((out_rows, depth), 0), BLOCK)
    return jnp.where(same, spread, 0.0).astype(BF16)


def aligned(start, size):
    return pl.ds(start if size % 8 else pl.multiple_of(start, size), size)


def half_of(flip, far, wide):
    return (lax.axis_index(PLANE) ^ flip) * 2 + (quotient(lax.axis_index(WIDE), wide // 2) ^ far)


def per_frame(rows, frames, copies):
    tall = jnp.broadcast_to(rows[:, None, :], (BLOCK, frames, LANES)).reshape(BLOCK * frames, LANES)
    return tall if copies == 1 else jnp.concatenate([tall] * copies, axis=1)


def prepare_kernel(
    rim, cuts, col_hbm, row_hbm, movie_hbm, mask_hbm, support_hbm, templates_hbm,
    smooth_ref, col_fwd_ref, row_fwd_ref, code_ref, templates_ref, flat_ref,
    movie_ref, mask_ref, support_ref, packed_ref, loose_ref, col_ref, row_ref, sems,
):
    planes, frames, rows, _ = movie_ref.shape
    some = frames // cuts

    def fetch(n, source, target):
        copy = pltpu.make_async_copy(source, target, sems.at[n])
        copy.start()
        return copy

    tap_copies = [fetch(0, col_hbm, col_ref), fetch(1, row_hbm, row_ref)]
    movie_copies = []
    for n in range(planes * cuts):
        piece = (n // cuts, pl.ds(n % cuts * some, some))
        movie_copies.append(fetch(5 + n, movie_hbm.at[piece], movie_ref.at[piece]))
    packed_copy = fetch(2, templates_hbm, packed_ref)
    code_copies = [fetch(3, mask_hbm, mask_ref), fetch(4, support_hbm, support_ref)]
    for copy in tap_copies:
        copy.wait()
    col_fwd = column_band(col_ref, rim, -1)
    col_fwd_ref[...] = col_fwd
    row_fwd_ref[...] = row_band_forward(row_ref, rim, frames)
    for copy in (*movie_copies, packed_copy, *code_copies):
        copy.wait()
    loose_ref[...] = packed_ref[...].astype(F32)
    code_ref[...] = support_ref[...] * 2 + mask_ref[...]
    unit = (iota((LANES, LANES), 0) == iota((LANES, LANES), 1)).astype(BF16)
    for n in range(planes * cuts):
        p, first = n // cuts, n % cuts * some
        full = jnp.dot(
            movie_ref[p, first : first + some].reshape(some * rows, LANES), col_fwd,
            preferred_element_type=F32,
        )
        smooth_ref[first : first + some, BLOCK : BLOCK + rows, p * LANES : (p + 1) * LANES] = (
            full.astype(BF16).reshape(some, rows, LANES)
        )
    for p in range(planes):
        shapes = loose_ref[pl.ds(p, templates_ref.shape[1], stride=planes), :].astype(BF16)
        flat_ref[:, p * LANES : (p + 1) * LANES] = shapes
        templates_ref[p * LANES : (p + 1) * LANES, :] = lax.dot_general(
            unit, shapes, (((1,), (1,)), ((), ())), preferred_element_type=F32
        ).astype(BF16)


def forward_kernel(
    flip, far, fill, wide, ks, smooth_in_ref, edge_ref, col_fwd_ref, row_fwd_ref, code_ref,
    templates_ref, smooth_ref, filtered_ref, out_ref, projected_ref,
):
    frames, padded_rows, width = smooth_ref.shape
    planes, rows = width // LANES, padded_rows - 2 * BLOCK
    if fill:
        for p in range(planes):
            edge = jnp.dot(
                edge_ref[p].reshape(frames * BLOCK, LANES), col_fwd_ref[...],
                preferred_element_type=F32,
            ).reshape(frames, BLOCK, LANES)
            lanes = slice(p * LANES, (p + 1) * LANES)
            above = jnp.where(lax.axis_index(REP) > 0, edge, 0.0).astype(BF16)
            below = jnp.where(lax.axis_index(REP) > 0, 0.0, edge).astype(BF16)
            smooth_ref[:, :BLOCK, lanes] = above
            smooth_ref[:, BLOCK + rows :, lanes] = below
    here = filtered_ref.shape[0] // frames
    first = half_of(flip, far, wide) * here
    tiles = templates_ref.shape[1] // LANES
    def along(b):
        near = smooth_ref[:, pl.ds(pl.multiple_of(first + b * BLOCK, BLOCK), 3 * BLOCK), :]
        near = near.reshape(frames * 3 * BLOCK, width)
        return jnp.dot(row_fwd_ref[...], near, preferred_element_type=F32)

    cells = along(0)
    for b in range(here // BLOCK):
        code = code_ref[pl.ds(pl.multiple_of(first + b * BLOCK, BLOCK), BLOCK), :]
        mask = per_frame((code & 1).astype(F32), frames, planes)
        filtered = (cells * mask).astype(BF16)
        spot = slice(b * BLOCK * frames, (b + 1) * BLOCK * frames)
        filtered_ref[spot, :] = filtered
        dense = jnp.dot(filtered, templates_ref[...], preferred_element_type=F32)
        cells = along(b + 1) if b + 1 < here // BLOCK else None
        picked = per_frame(code >> 1, frames, 1)
        lane, tile = picked & (LANES - 1), quotient(picked, LANES)
        chosen = jnp.zeros(picked.shape, F32)
        for t in range(tiles):
            found = jnp.take_along_axis(
                dense[:, t * LANES : (t + 1) * LANES], lane, axis=1, mode="promise_in_bounds"
            )
            chosen = jnp.where(tile == t, found, chosen)
        projected_ref[spot, :] = chosen.astype(BF16)
    size = out_ref.shape[0] // len(ks)
    for i, k in enumerate(ks):
        start = pl.multiple_of(((lax.axis_index(WIDE) ^ k) & (wide // 2 - 1)) * size, size)
        out_ref[i * size : (i + 1) * size, :] = projected_ref[pl.ds(start, size), :]


def add_all(parts, spots, rows):
    total = None
    for part, spot in zip(parts, spots):
        term = part[spot * rows : (spot + 1) * rows, :].astype(F32)
        total = term if total is None else total + term
    return total.astype(BF16)


def sum_kernel(spots, lag_ref, *refs):
    parts, out_ref = refs[:-1], refs[-1]
    rows = out_ref.shape[0] - lag_ref.shape[0]
    out_ref[:rows, :] = add_all(parts, spots, rows)
    out_ref[rows:, :] = lag_ref[...]


def mix_kernel(wide, spots, owner_ref, lag_ref, *refs):
    parts, refs = refs[: len(spots)], refs[len(spots) :]
    blocks, outs = refs[: wide - 1], refs[wide - 1 : 2 * wide - 1]
    cells_ref, kernels_ref, traces_ref = refs[2 * wide - 1 :]
    _, share, frames, lanes = cells_ref.shape
    total = wide * frames
    here = lax.axis_index(WIDE)
    cells_ref[here] = add_all(parts, spots, share * frames).reshape(share, frames, lanes)
    kernels_ref[here] = lag_ref[...].astype(F32)
    for k, block in enumerate(blocks, 1):
        cells_ref[here ^ k] = block[: share * frames, :].reshape(share, frames, lanes)
        kernels_ref[here ^ k] = block[share * frames :, :].astype(F32)
    first = (lax.axis_index(PLANE) * wide + here) * share
    owners = owner_ref[...]
    lane = iota(owners.shape, 1)
    for h in range(share):
        owner = jnp.sum(jnp.where(lane == first + h, owners, 0), axis=1, keepdims=True)
        owner = jnp.broadcast_to(owner, (8, lanes))
        row = []
        for i in range(0, kernels_ref.shape[1], 8):
            values = jnp.zeros((8, lanes), F32)
            for d in range(wide):
                values = jnp.where(owner == d, kernels_ref[d, i : i + 8, :], values)
            row += [values[n : n + 1, :] for n in range(8)]
        row = jnp.concatenate(row[: 2 * total // lanes], axis=1)
        lag = toeplitz(row, total, total + 1)[:, :total].astype(BF16)
        mixed = jnp.dot(lag, cells_ref[:, h].reshape(total, lanes), preferred_element_type=F32)
        traces_ref[:, h] = jnp.maximum(mixed, 0.0).astype(BF16).reshape(wide, frames, lanes)
    for k, out_ref in enumerate(outs):
        out_ref[...] = traces_ref[here ^ k]


def bands_kernel(rim, frames, col_ref, row_ref, col_adj_ref, row_adj_ref):
    band = column_band(col_ref, rim, 1)
    col_adj_ref[...] = jnp.zeros_like(col_adj_ref)
    for p in range(col_adj_ref.shape[0] // LANES):
        lanes = slice(p * LANES, (p + 1) * LANES)
        col_adj_ref[lanes, lanes] = band
    row_adj_ref[...] = row_band_adjoint(row_ref, rim, frames)


def residual_kernel(flip, far, wide, spots, filtered_ref, code_ref, templates_ref, *refs):
    traces, (out_ref, edge_ref, ordered_ref, slots_ref) = refs[:-4], refs[-4:]
    _, frames, lanes = traces[0].shape
    share = ordered_ref.shape[0] // len(spots)
    names, width = templates_ref.shape
    tile = 2 * LANES
    base = half_of(flip, far, wide) * len(spots) * share
    marks = iota((lanes, tile), 1).astype(F32).astype(BF16)
    group = min(8, share)
    for n, (k, source, offset) in enumerate(spots):
        block = (lax.axis_index(WIDE) ^ k) & (wide // 2 - 1)
        source, offset = traces[source], offset * share
        top = base + block * share
        for g in range(share // group):
            support = code_ref[aligned(top + g * group, group), :] >> 1
            support = jnp.concatenate([support] * (8 // group), axis=0)
            columns = jnp.transpose(support.astype(F32))
            for i in range(group):
                h = g * group + i
                named = jnp.broadcast_to(columns[:, i : i + 1], (lanes, lanes))
                hits = []
                for t in range(names // tile):
                    offset_name = (named - float(t * tile)).astype(BF16)
                    hits.append(
                        jnp.where(
                            marks == jnp.concatenate([offset_name] * 2, axis=1),
                            jnp.ones((), BF16), jnp.zeros((), BF16),
                        )
                    )
                hits = jnp.concatenate(hits, axis=1)
                slots_ref[n, h * frames : (h + 1) * frames, :] = jnp.dot(
                    source[offset + h], hits, preferred_element_type=F32
                ).astype(BF16)
        model = jnp.dot(slots_ref[n], templates_ref[...], preferred_element_type=F32)
        mask = (code_ref[aligned(top, share), :] & 1).astype(F32)
        mask = jnp.broadcast_to(mask[:, None, :], (share, frames, lanes)).reshape(-1, lanes)
        size = share * frames
        spot = pl.ds(pl.multiple_of(block * size, size), size)
        out_ref[spot, :] = (
            filtered_ref[spot, :].astype(F32)
            - jnp.concatenate([mask] * (width // lanes), axis=1) * model
        ).astype(BF16)
        ordered_ref[pl.ds(block * share, share)] = source[offset : offset + share]
    edge = edge_ref.shape[0]
    start = jnp.where(lax.axis_index(REP) > 0, 0, out_ref.shape[0] - edge)
    edge_ref[...] = out_ref[pl.ds(pl.multiple_of(start, edge), edge), :]


def backward_kernel(keys, wide, turned_ref, edge_ref, col_adj_ref, row_adj_ref, *refs):
    parts, (out_hbm, trace_hbm, padded_ref, out_ref, sems) = refs[: len(keys)], refs[len(keys) :]
    planes, frames, rows, _ = out_ref.shape
    edge, size = BLOCK * frames, parts[0].shape[0]
    zero = jnp.zeros_like(edge_ref)
    padded_ref[:edge, :] = jnp.where(lax.axis_index(REP) > 0, edge_ref[...], zero)
    padded_ref[edge + rows * frames :, :] = jnp.where(lax.axis_index(REP) > 0, zero, edge_ref[...])
    for (flip, far), part in zip(keys, parts):
        spot = pl.multiple_of(edge + half_of(flip, far, wide) * size, edge)
        padded_ref[pl.ds(spot, size), :] = part[...]
    def along(b):
        near = padded_ref[b * edge : (b + 3) * edge, :]
        return jnp.dot(row_adj_ref[...], near, preferred_element_type=F32).astype(BF16)

    copies = [pltpu.make_async_copy(turned_ref, trace_hbm, sems.at[rows // BLOCK])]
    copies[0].start()
    back = along(0)
    for b in range(rows // BLOCK):
        ahead = along(b + 1) if b + 1 < rows // BLOCK else None
        full = jnp.dot(back, col_adj_ref[...], preferred_element_type=F32).astype(BF16)
        for p in range(planes):
            out_ref[p, :, b * BLOCK : (b + 1) * BLOCK, :] = full[
                :, p * LANES : (p + 1) * LANES
            ].reshape(frames, BLOCK, LANES)
        piece = (slice(None), slice(None), pl.ds(b * BLOCK, BLOCK))
        copy = pltpu.make_async_copy(out_ref.at[piece], out_hbm.at[piece], sems.at[b])
        copy.start()
        copies.append(copy)
        back = ahead
    for copy in copies:
        copy.wait()


def emit_kernel(keys, wide, *refs):
    parts, (out_ref, rows_ref, turned_ref) = refs[: len(keys)], refs[len(keys) :]
    share, frames, rows = out_ref.shape
    size = rows_ref.shape[0] // len(keys)
    for (flip, far), part in zip(keys, parts):
        spot = pl.multiple_of(half_of(flip, far, wide) * size, size)
        rows_ref[pl.ds(spot, size), :] = part[...].reshape(size, LANES).astype(F32)
    first = lax.axis_index(PLANE) * share
    select = (iota((share, LANES), 1) == iota((share, LANES), 0) + first).astype(BF16)
    for f in range(frames):
        cells = rows_ref[pl.ds(f, rows, stride=frames), :].astype(BF16)
        turned_ref[pl.ds(f, share, stride=frames), :] = lax.dot_general(
            select, cells, (((1,), (1,)), ((), ())), preferred_element_type=F32
        )
    out_ref[...] = turned_ref[...].astype(BF16).reshape(share, frames, rows)


VMEM = pl.BlockSpec(memory_space=pltpu.VMEM)
SMEM = pl.BlockSpec(memory_space=pltpu.SMEM)
HBM = pl.BlockSpec(memory_space=pltpu.HBM)


def shaped(shape):
    return jax.ShapeDtypeStruct(shape, BF16)


def call(kernel, name, outs, smem, vmem, scratch=(), aliases=None):
    return pl.pallas_call(
        kernel,
        out_shape=tuple(shaped(s) if isinstance(s, tuple) else s for s in outs),
        in_specs=[SMEM] * smem + [VMEM] * vmem,
        out_specs=(VMEM,) * len(outs),
        scratch_shapes=scratch,
        input_output_aliases=aliases or {},
        compiler_params=pltpu.CompilerParams(vmem_limit_bytes=32 * 1024 * 1024),
        name=name,
    )


def lag_kernel_values(gains, lags, frame_count):
    taps = gains.shape[1]
    lag_values = jnp.arange(2 * frame_count, dtype=jnp.int32) - (frame_count - 1)
    offsets = jnp.arange(taps, dtype=jnp.int32) - (taps - 1) // 2
    hits = lag_values[None, :, None] == lags[:, None, None] * offsets[None, None, :]
    spread = jnp.where(hits, gains[:, None, :], jnp.zeros((), gains.dtype))
    return jnp.sum(spread, axis=(0, 2)).astype(BF16)


def on_device(
    movie_frames, pixel_mask, tile_owner, support, templates, row_taps, col_taps, lag_gains, dilations
):
    planes, frames, rows, cols = movie_frames.shape
    wide, plane_count = lax.axis_size("wide"), lax.axis_size("planes")
    rim = (row_taps.shape[0] - 1) // 2
    total_frames, width = frames * wide, planes * cols
    here = rows // plane_count
    share = here // wide
    edge = BLOCK * frames
    rep, plane, spot = lax.axis_index("rep"), lax.axis_index("planes"), lax.axis_index("wide")
    mib = 1 << 20

    start = jnp.where(rep == 0, rows - BLOCK, 0)
    rim_rows = exchange(lax.dynamic_slice_in_dim(movie_frames, start, BLOCK, axis=2), "rep", 1)
    cuts = 2
    depth, names = 3 * BLOCK * frames, templates.shape[0]
    smooth, col_fwd, row_fwd, code, tall_templates, flat_templates = pl.pallas_call(
        functools.partial(prepare_kernel, rim, cuts),
        out_shape=(
            shaped((frames, rows + 2 * BLOCK, width)), shaped((cols, cols)), shaped((edge, depth)),
            jax.ShapeDtypeStruct(support.shape, jnp.int32), shaped((width, names)),
            shaped((names, width)),
        ),
        in_specs=[HBM] * 6,
        out_specs=(VMEM,) * 6,
        scratch_shapes=[
            pltpu.VMEM(movie_frames.shape, BF16),
            pltpu.VMEM(pixel_mask.shape, jnp.int32),
            pltpu.VMEM(support.shape, jnp.int32),
            pltpu.VMEM((names * planes, cols), BF16),
            pltpu.VMEM((names * planes, cols), F32),
            pltpu.SMEM(col_taps.shape, F32),
            pltpu.SMEM(row_taps.shape, F32),
            pltpu.SemaphoreType.DMA((5 + planes * cuts,)),
        ],
        compiler_params=pltpu.CompilerParams(vmem_limit_bytes=32 * mib),
        name="prepare",
    )(
        *[
            pltpu.with_memory_space_constraint(x, pltpu.HBM)
            for x in (
                col_taps, row_taps, movie_frames, pixel_mask, support,
                templates.reshape(names * planes, cols),
            )
        ]
    )

    near_ks, far_ks = list(range(wide // 2)), list(range(wide // 2, wide))
    halves = {1: far_ks, 0: near_ks[::-1]}
    half_rows = here // 2
    filtered, projected = {}, {}
    flips = [(turn + 1) % plane_count for turn in range(plane_count)]
    keys = [(flip, far) for far in (1, 0) for flip in flips]
    for turn, (flip, far) in enumerate(keys):
        smooth, filtered[flip, far], mine = call(
            functools.partial(forward_kernel, flip, far, turn == 0, wide, halves[far]), "forward",
            [smooth.shape, (half_rows * frames, width), (half_rows * frames, LANES)],
            0, 6, aliases={0: 0},
            scratch=[pltpu.VMEM((half_rows * frames, LANES), BF16)],
        )(smooth, rim_rows, col_fwd, row_fwd, code, tall_templates)
        projected[flip, far] = exchange(mine, "planes", flip) if flip else mine
        if turn == 0:
            gains, lags, _ = lax.optimization_barrier((lag_gains, dilations, smooth))
            kernel_row = lag_kernel_values(gains[0], lags[0], total_frames)
            lag_rows = -(-2 * total_frames // (LANES * BLOCK)) * BLOCK
            kernel_row = jnp.pad(kernel_row, (0, lag_rows * LANES - 2 * total_frames))
            kernel_row = kernel_row.reshape(lag_rows, LANES)

    block_rows = share * frames + lag_rows
    sums, blocks = {}, {}

    def parts_of(k):
        far = int(k in far_ks)
        spots = [halves[far].index(k)] * plane_count
        return spots, [projected[flip, far] for flip in range(plane_count)]

    for k in near_ks[1:] + far_ks:
        spots, parts = parts_of(k)
        (sums[k],) = call(
            functools.partial(sum_kernel, spots), "sum", [(block_rows, LANES)],
            0, 1 + plane_count,
        )(kernel_row, *parts)
        blocks[k] = exchange(sums[k], "wide", k)

    late_col, late_row, _ = lax.optimization_barrier(
        (col_taps, row_taps, list(sums.values()))
    )
    col_adj, row_adj = call(
        functools.partial(bands_kernel, rim, frames), "bands", [(width, width), (edge, depth)],
        2, 0,
    )(late_col, late_row)
    own_spots, own_parts = parts_of(0)
    own_parts[0], col_adj, row_adj = lax.optimization_barrier((own_parts[0], col_adj, row_adj))

    cell_shape = (wide, share, frames, LANES)
    traces = call(
        functools.partial(mix_kernel, wide, own_spots), "mix", [cell_shape[1:]] * wide,
        0, 1 + wide + plane_count,
        scratch=[
            pltpu.VMEM(cell_shape, BF16), pltpu.VMEM((wide, lag_rows, LANES), F32),
            pltpu.VMEM(cell_shape, BF16),
        ],
    )(
        tile_owner.reshape(1, rows), kernel_row, *own_parts, *[blocks[k] for k in range(1, wide)],
    )
    swapped = {k: exchange(traces[k], "wide", k) for k in far_ks + near_ks[1:]}
    swapped[0] = traces[0]
    late = range(1, plane_count)
    near = jnp.concatenate([swapped[k] for k in near_ks])
    passed = {flip: exchange(near, "planes", flip) for flip in late}

    residual, edges, ordered = {}, {}, {}
    back_keys = [(flip, far) for flip in range(plane_count) for far in (0, 1)]

    def subtract(flip, far, groups, got):
        spots = [(k, n, i) for n, ks in enumerate(groups) for i, k in enumerate(ks)]
        residual[flip, far], edges[flip, far], ordered[flip, far] = call(
            functools.partial(residual_kernel, flip, far, wide, spots), "residual",
            [(half_rows * frames, width), (edge, width), (half_rows, frames, LANES)],
            0, 3 + len(got), scratch=[pltpu.VMEM((len(spots), share * frames, names), BF16)],
        )(filtered[flip, far], code, flat_templates, *got)

    subtract(0, 0, [near_ks], [near])
    distant, _ = lax.optimization_barrier(([swapped[k] for k in far_ks], edges[0, 0]))
    joined = jnp.concatenate(distant)
    subtract(0, 1, [[k] for k in far_ks], distant)
    for flip in late:
        subtract(flip, 0, [near_ks], [passed[flip]])
        got, _ = lax.optimization_barrier((exchange(joined, "planes", flip), edges[flip, 0]))
        subtract(flip, 1, [far_ks], [got])

    def pick(table, part, half):
        found = table[0, 0]
        for flip, far in back_keys[1:]:
            here_it_is = ((plane ^ part) == flip) & ((spot // (wide // 2) ^ half) == far)
            found = jnp.where(here_it_is, table[flip, far], found)
        return found

    tip = pick(edges, jnp.where(rep == 0, plane_count - 1, 0), jnp.where(rep == 0, 1, 0))
    tip = exchange(tip, "rep", 1)

    foot_share = support.shape[1] // plane_count
    turned = pl.pallas_call(
        functools.partial(emit_kernel, back_keys, wide),
        out_shape=shaped((foot_share, frames, rows)),
        in_specs=[VMEM] * len(back_keys),
        out_specs=VMEM,
        scratch_shapes=[
            pltpu.VMEM((rows * frames, LANES), F32),
            pltpu.VMEM((foot_share * frames, rows), F32),
        ],
        compiler_params=pltpu.CompilerParams(vmem_limit_bytes=32 * mib),
        name="emit",
    )(*[ordered[key] for key in back_keys])

    back_projected, trace_out = pl.pallas_call(
        functools.partial(backward_kernel, back_keys, wide),
        out_shape=(shaped(movie_frames.shape), shaped(turned.shape)),
        in_specs=[VMEM] * (4 + len(back_keys)),
        out_specs=(HBM, HBM),
        scratch_shapes=[
            pltpu.VMEM(((rows + 2 * BLOCK) * frames, width), BF16),
            pltpu.VMEM(movie_frames.shape, BF16),
            pltpu.SemaphoreType.DMA((rows // BLOCK + 1,)),
        ],
        compiler_params=pltpu.CompilerParams(vmem_limit_bytes=32 * mib),
        name="backward",
    )(turned, tip, col_adj, row_adj, *[residual[key] for key in back_keys])
    return trace_out, back_projected


def solution(mesh):
    return jax.shard_map(
        on_device,
        mesh=mesh,
        in_specs=(
            P("planes", ("groups", "wide"), "rep", None),
            P("rep", None),
            P("rep", None),
            P("rep", None),
            P(None, "planes", None),
            P(),
            P(),
            P("wide", None, None),
            P("wide", None),
        ),
        out_specs=(
            P("planes", ("groups", "wide"), "rep"),
            P("planes", ("groups", "wide"), "rep", None),
        ),
        check_vma=False,
    )
```

```python
import functools

import jax
import jax.numpy as jnp
from jax import lax
from jax.experimental import pallas as pl
from jax.experimental.pallas import tpu as pltpu
from jax.sharding import PartitionSpec as P

BLOCK = 16
LANES = 128
F32 = jnp.float32
BF16 = jnp.bfloat16
REP, PLANE, WIDE = "rep", "planes", "wide"


def exchange(cells, axis, flip):
    count = lax.axis_size(axis)
    return lax.ppermute(cells, axis, [(i, i ^ flip) for i in range(count)])


def iota(shape, dim):
    return lax.broadcasted_iota(jnp.int32, shape, dim)


def tap_row(taps_ref, place):
    lane = iota((8, LANES), 1)
    row = jnp.zeros((8, LANES), F32)
    for k in range(taps_ref.shape[0]):
        row = jnp.where(lane == place(k) % LANES, taps_ref[k], row)
    return row[:1]


def quotient(x, n):
    if n & (n - 1) == 0:
        return lax.shift_right_logical(x, n.bit_length() - 1)
    return lax.shift_right_logical(x * (65536 // n + 1), 16)


def remainder(x, n):
    return x & (n - 1) if n & (n - 1) == 0 else x - n * quotient(x, n)


def toeplitz(row, count, shift=0):
    return pltpu.roll(
        jnp.broadcast_to(row, (count, row.shape[1])), shift, 1, stride=1, stride_axis=0
    )


def column_band(taps_ref, rim, sign):
    rolled = toeplitz(tap_row(taps_ref, lambda k: sign * (k - rim)), LANES)
    gap = iota((LANES, LANES), 1) - iota((LANES, LANES), 0)
    return jnp.where(jnp.abs(gap) <= rim, rolled, 0.0).astype(BF16)


def row_band_forward(taps_ref, rim, frames):
    out_rows, depth, span = BLOCK * frames, 3 * BLOCK * frames, 3 * BLOCK
    band = toeplitz(tap_row(taps_ref, lambda k: k + BLOCK - rim), BLOCK)[:, :span].astype(BF16)
    left = (quotient(iota((out_rows, BLOCK), 0), frames) == iota((out_rows, BLOCK), 1)).astype(BF16)
    right = (remainder(iota((span, depth), 1), span) == iota((span, depth), 0)).astype(BF16)
    tall = jnp.dot(left, band, preferred_element_type=F32).astype(BF16)
    spread = jnp.dot(tall, right, preferred_element_type=F32)
    start = iota((out_rows, depth), 1) - span * remainder(iota((out_rows, depth), 0), frames)
    return jnp.where((start >= 0) & (start < span), spread, 0.0).astype(BF16)


def row_band_adjoint(taps_ref, rim, frames):
    out_rows, depth, span = BLOCK * frames, 3 * BLOCK * frames, 3 * BLOCK
    band = toeplitz(tap_row(taps_ref, lambda k: BLOCK + rim - k), BLOCK)[:, :span].astype(BF16)
    left = (remainder(iota((out_rows, BLOCK), 0), BLOCK) == iota((out_rows, BLOCK), 1)).astype(BF16)
    right = (quotient(iota((span, depth), 1), frames) == iota((span, depth), 0)).astype(BF16)
    tall = jnp.dot(left, band, preferred_element_type=F32).astype(BF16)
    spread = jnp.dot(tall, right, preferred_element_type=F32)
    same = remainder(iota((out_rows, depth), 1), frames) == quotient(iota((out_rows, depth), 0), BLOCK)
    return jnp.where(same, spread, 0.0).astype(BF16)


def aligned(start, size):
    return pl.ds(start if size % 8 else pl.multiple_of(start, size), size)


def half_of(flip, far, wide):
    return (lax.axis_index(PLANE) ^ flip) * 2 + (quotient(lax.axis_index(WIDE), wide // 2) ^ far)


def per_frame(rows, frames, copies):
    tall = jnp.broadcast_to(rows[:, None, :], (BLOCK, frames, LANES)).reshape(BLOCK * frames, LANES)
    return tall if copies == 1 else jnp.concatenate([tall] * copies, axis=1)


def prepare_kernel(
    rim, cuts, col_hbm, row_hbm, movie_hbm, mask_hbm, support_hbm, templates_hbm,
    smooth_ref, col_fwd_ref, row_fwd_ref, code_ref, templates_ref, flat_ref,
    movie_ref, mask_ref, support_ref, packed_ref, loose_ref, col_ref, row_ref, sems,
):
    planes, frames, rows, _ = movie_ref.shape
    some = frames // cuts

    def fetch(n, source, target):
        copy = pltpu.make_async_copy(source, target, sems.at[n])
        copy.start()
        return copy

    tap_copies = [fetch(0, col_hbm, col_ref), fetch(1, row_hbm, row_ref)]
    movie_copies = []
    for n in range(planes * cuts):
        piece = (n // cuts, pl.ds(n % cuts * some, some))
        movie_copies.append(fetch(5 + n, movie_hbm.at[piece], movie_ref.at[piece]))
    packed_copy = fetch(2, templates_hbm, packed_ref)
    code_copies = [fetch(3, mask_hbm, mask_ref), fetch(4, support_hbm, support_ref)]
    for copy in tap_copies:
        copy.wait()
    col_fwd = column_band(col_ref, rim, -1)
    col_fwd_ref[...] = col_fwd
    row_fwd_ref[...] = row_band_forward(row_ref, rim, frames)
    for copy in (*movie_copies, packed_copy, *code_copies):
        copy.wait()
    loose_ref[...] = packed_ref[...].astype(F32)
    code_ref[...] = support_ref[...] * 2 + mask_ref[...]
    unit = (iota((LANES, LANES), 0) == iota((LANES, LANES), 1)).astype(BF16)
    for n in range(planes * cuts):
        p, first = n // cuts, n % cuts * some
        full = jnp.dot(
            movie_ref[p, first : first + some].reshape(some * rows, LANES), col_fwd,
            preferred_element_type=F32,
        )
        smooth_ref[first : first + some, BLOCK : BLOCK + rows, p * LANES : (p + 1) * LANES] = (
            full.astype(BF16).reshape(some, rows, LANES)
        )
    for p in range(planes):
        shapes = loose_ref[pl.ds(p, templates_ref.shape[1], stride=planes), :].astype(BF16)
        flat_ref[:, p * LANES : (p + 1) * LANES] = shapes
        templates_ref[p * LANES : (p + 1) * LANES, :] = lax.dot_general(
            unit, shapes, (((1,), (1,)), ((), ())), preferred_element_type=F32
        ).astype(BF16)


def forward_kernel(
    flip, far, fill, wide, ks, smooth_in_ref, edge_ref, col_fwd_ref, row_fwd_ref, code_ref,
    templates_ref, smooth_ref, filtered_ref, out_ref, projected_ref,
):
    frames, padded_rows, width = smooth_ref.shape
    planes, rows = width // LANES, padded_rows - 2 * BLOCK
    if fill:
        for p in range(planes):
            edge = jnp.dot(
                edge_ref[p].reshape(frames * BLOCK, LANES), col_fwd_ref[...],
                preferred_element_type=F32,
            ).reshape(frames, BLOCK, LANES)
            lanes = slice(p * LANES, (p + 1) * LANES)
            above = jnp.where(lax.axis_index(REP) > 0, edge, 0.0).astype(BF16)
            below = jnp.where(lax.axis_index(REP) > 0, 0.0, edge).astype(BF16)
            smooth_ref[:, :BLOCK, lanes] = above
            smooth_ref[:, BLOCK + rows :, lanes] = below
    here = filtered_ref.shape[0] // frames
    first = half_of(flip, far, wide) * here
    tiles = templates_ref.shape[1] // LANES
    def along(b):
        near = smooth_ref[:, pl.ds(pl.multiple_of(first + b * BLOCK, BLOCK), 3 * BLOCK), :]
        near = near.reshape(frames * 3 * BLOCK, width)
        return jnp.dot(row_fwd_ref[...], near, preferred_element_type=F32)

    cells = along(0)
    for b in range(here // BLOCK):
        code = code_ref[pl.ds(pl.multiple_of(first + b * BLOCK, BLOCK), BLOCK), :]
        mask = per_frame((code & 1).astype(F32), frames, planes)
        filtered = (cells * mask).astype(BF16)
        spot = slice(b * BLOCK * frames, (b + 1) * BLOCK * frames)
        filtered_ref[spot, :] = filtered
        dense = jnp.dot(filtered, templates_ref[...], preferred_element_type=F32)
        cells = along(b + 1) if b + 1 < here // BLOCK else None
        picked = per_frame(code >> 1, frames, 1)
        lane, tile = picked & (LANES - 1), quotient(picked, LANES)
        chosen = jnp.zeros(picked.shape, F32)
        for t in range(tiles):
            found = jnp.take_along_axis(
                dense[:, t * LANES : (t + 1) * LANES], lane, axis=1, mode="promise_in_bounds"
            )
            chosen = jnp.where(tile == t, found, chosen)
        projected_ref[spot, :] = chosen.astype(BF16)
    size = out_ref.shape[0] // len(ks)
    for i, k in enumerate(ks):
        start = pl.multiple_of(((lax.axis_index(WIDE) ^ k) & (wide // 2 - 1)) * size, size)
        out_ref[i * size : (i + 1) * size, :] = projected_ref[pl.ds(start, size), :]


def add_all(parts, spots, rows):
    total = None
    for part, spot in zip(parts, spots):
        term = part[spot * rows : (spot + 1) * rows, :].astype(F32)
        total = term if total is None else total + term
    return total.astype(BF16)


def sum_kernel(spots, lag_ref, *refs):
    parts, out_ref = refs[:-1], refs[-1]
    rows = out_ref.shape[0] - lag_ref.shape[0]
    out_ref[:rows, :] = add_all(parts, spots, rows)
    out_ref[rows:, :] = lag_ref[...]


def mix_kernel(wide, spots, owner_ref, lag_ref, *refs):
    parts, refs = refs[: len(spots)], refs[len(spots) :]
    blocks, outs = refs[: wide - 1], refs[wide - 1 : 2 * wide - 1]
    cells_ref, kernels_ref, traces_ref = refs[2 * wide - 1 :]
    _, share, frames, lanes = cells_ref.shape
    total = wide * frames
    here = lax.axis_index(WIDE)
    cells_ref[here] = add_all(parts, spots, share * frames).reshape(share, frames, lanes)
    kernels_ref[here] = lag_ref[...].astype(F32)
    for k, block in enumerate(blocks, 1):
        cells_ref[here ^ k] = block[: share * frames, :].reshape(share, frames, lanes)
        kernels_ref[here ^ k] = block[share * frames :, :].astype(F32)
    first = (lax.axis_index(PLANE) * wide + here) * share
    owners = owner_ref[...]
    lane = iota(owners.shape, 1)
    for h in range(share):
        owner = jnp.sum(jnp.where(lane == first + h, owners, 0), axis=1, keepdims=True)
        owner = jnp.broadcast_to(owner, (8, lanes))
        row = []
        for i in range(0, kernels_ref.shape[1], 8):
            values = jnp.zeros((8, lanes), F32)
            for d in range(wide):
                values = jnp.where(owner == d, kernels_ref[d, i : i + 8, :], values)
            row += [values[n : n + 1, :] for n in range(8)]
        row = jnp.concatenate(row[: 2 * total // lanes], axis=1)
        lag = toeplitz(row, total, total + 1)[:, :total].astype(BF16)
        mixed = jnp.dot(lag, cells_ref[:, h].reshape(total, lanes), preferred_element_type=F32)
        traces_ref[:, h] = jnp.maximum(mixed, 0.0).astype(BF16).reshape(wide, frames, lanes)
    for k, out_ref in enumerate(outs):
        out_ref[...] = traces_ref[here ^ k]


def bands_kernel(rim, frames, col_ref, row_ref, col_adj_ref, row_adj_ref):
    band = column_band(col_ref, rim, 1)
    col_adj_ref[...] = jnp.zeros_like(col_adj_ref)
    for p in range(col_adj_ref.shape[0] // LANES):
        lanes = slice(p * LANES, (p + 1) * LANES)
        col_adj_ref[lanes, lanes] = band
    row_adj_ref[...] = row_band_adjoint(row_ref, rim, frames)


def residual_kernel(flip, far, wide, spots, filtered_ref, code_ref, templates_ref, *refs):
    traces, (out_ref, edge_ref, ordered_ref, slots_ref) = refs[:-4], refs[-4:]
    _, frames, lanes = traces[0].shape
    share = ordered_ref.shape[0] // len(spots)
    names, width = templates_ref.shape
    tile = 2 * LANES
    base = half_of(flip, far, wide) * len(spots) * share
    marks = iota((lanes, tile), 1).astype(F32).astype(BF16)
    group = min(8, share)
    for n, (k, source, offset) in enumerate(spots):
        block = (lax.axis_index(WIDE) ^ k) & (wide // 2 - 1)
        source, offset = traces[source], offset * share
        top = base + block * share
        for g in range(share // group):
            support = code_ref[aligned(top + g * group, group), :] >> 1
            support = jnp.concatenate([support] * (8 // group), axis=0)
            columns = jnp.transpose(support.astype(F32))
            for i in range(group):
                h = g * group + i
                named = jnp.broadcast_to(columns[:, i : i + 1], (lanes, lanes))
                hits = []
                for t in range(names // tile):
                    offset_name = (named - float(t * tile)).astype(BF16)
                    hits.append(
                        jnp.where(
                            marks == jnp.concatenate([offset_name] * 2, axis=1),
                            jnp.ones((), BF16), jnp.zeros((), BF16),
                        )
                    )
                hits = jnp.concatenate(hits, axis=1)
                slots_ref[n, h * frames : (h + 1) * frames, :] = jnp.dot(
                    source[offset + h], hits, preferred_element_type=F32
                ).astype(BF16)
        model = jnp.dot(slots_ref[n], templates_ref[...], preferred_element_type=F32)
        mask = (code_ref[aligned(top, share), :] & 1).astype(F32)
        mask = jnp.broadcast_to(mask[:, None, :], (share, frames, lanes)).reshape(-1, lanes)
        size = share * frames
        spot = pl.ds(pl.multiple_of(block * size, size), size)
        out_ref[spot, :] = (
            filtered_ref[spot, :].astype(F32)
            - jnp.concatenate([mask] * (width // lanes), axis=1) * model
        ).astype(BF16)
        ordered_ref[pl.ds(block * share, share)] = source[offset : offset + share]
    edge = edge_ref.shape[0]
    start = jnp.where(lax.axis_index(REP) > 0, 0, out_ref.shape[0] - edge)
    edge_ref[...] = out_ref[pl.ds(pl.multiple_of(start, edge), edge), :]


def backward_kernel(
    turned_ref, edge_ref, col_adj_ref, row_adj_ref, body_ref, out_hbm, trace_hbm, out_ref, sems
):
    planes, frames, rows, _ = out_ref.shape
    edge, last = BLOCK * frames, rows // BLOCK - 1

    def along(b):
        near = body_ref[max(b - 1, 0) * edge : min(b + 2, last + 1) * edge, :]
        if b == 0:
            near = jnp.concatenate([jnp.where(lax.axis_index(REP) > 0, edge_ref[...], 0), near])
        if b == last:
            near = jnp.concatenate([near, jnp.where(lax.axis_index(REP) > 0, 0, edge_ref[...])])
        return jnp.dot(row_adj_ref[...], near, preferred_element_type=F32).astype(BF16)

    copies = [pltpu.make_async_copy(turned_ref, trace_hbm, sems.at[rows // BLOCK])]
    copies[0].start()
    back = along(0)
    for b in range(rows // BLOCK):
        ahead = along(b + 1) if b + 1 < rows // BLOCK else None
        full = jnp.dot(back, col_adj_ref[...], preferred_element_type=F32).astype(BF16)
        for p in range(planes):
            out_ref[p, :, b * BLOCK : (b + 1) * BLOCK, :] = full[
                :, p * LANES : (p + 1) * LANES
            ].reshape(frames, BLOCK, LANES)
        piece = (slice(None), slice(None), pl.ds(b * BLOCK, BLOCK))
        copy = pltpu.make_async_copy(out_ref.at[piece], out_hbm.at[piece], sems.at[b])
        copy.start()
        copies.append(copy)
        back = ahead
    for copy in copies:
        copy.wait()


def emit_kernel(keys, wide, *refs):
    count = len(keys)
    parts, pieces = refs[:count], refs[count : 2 * count]
    out_ref, body_ref, rows_ref, turned_ref = refs[2 * count :]
    for (flip, far), piece in zip(keys, pieces):
        tall = piece.shape[0]
        body_ref[pl.ds(pl.multiple_of(half_of(flip, far, wide) * tall, tall), tall), :] = piece[...]
    share, frames, rows = out_ref.shape
    size = rows_ref.shape[0] // len(keys)
    for (flip, far), part in zip(keys, parts):
        spot = pl.multiple_of(half_of(flip, far, wide) * size, size)
        rows_ref[pl.ds(spot, size), :] = part[...].reshape(size, LANES).astype(F32)
    first = lax.axis_index(PLANE) * share
    select = (iota((share, LANES), 1) == iota((share, LANES), 0) + first).astype(BF16)
    for f in range(frames):
        cells = rows_ref[pl.ds(f, rows, stride=frames), :].astype(BF16)
        turned_ref[pl.ds(f, share, stride=frames), :] = lax.dot_general(
            select, cells, (((1,), (1,)), ((), ())), preferred_element_type=F32
        )
    out_ref[...] = turned_ref[...].astype(BF16).reshape(share, frames, rows)


VMEM = pl.BlockSpec(memory_space=pltpu.VMEM)
SMEM = pl.BlockSpec(memory_space=pltpu.SMEM)
HBM = pl.BlockSpec(memory_space=pltpu.HBM)


def shaped(shape):
    return jax.ShapeDtypeStruct(shape, BF16)


def call(kernel, name, outs, smem, vmem, scratch=(), aliases=None):
    return pl.pallas_call(
        kernel,
        out_shape=tuple(shaped(s) if isinstance(s, tuple) else s for s in outs),
        in_specs=[SMEM] * smem + [VMEM] * vmem,
        out_specs=(VMEM,) * len(outs),
        scratch_shapes=scratch,
        input_output_aliases=aliases or {},
        compiler_params=pltpu.CompilerParams(vmem_limit_bytes=32 * 1024 * 1024),
        name=name,
    )


def lag_kernel_values(gains, lags, frame_count):
    taps = gains.shape[1]
    lag_values = jnp.arange(2 * frame_count, dtype=jnp.int32) - (frame_count - 1)
    offsets = jnp.arange(taps, dtype=jnp.int32) - (taps - 1) // 2
    hits = lag_values[None, :, None] == lags[:, None, None] * offsets[None, None, :]
    spread = jnp.where(hits, gains[:, None, :], jnp.zeros((), gains.dtype))
    return jnp.sum(spread, axis=(0, 2)).astype(BF16)


def on_device(
    movie_frames, pixel_mask, tile_owner, support, templates, row_taps, col_taps, lag_gains, dilations
):
    planes, frames, rows, cols = movie_frames.shape
    wide, plane_count = lax.axis_size("wide"), lax.axis_size("planes")
    rim = (row_taps.shape[0] - 1) // 2
    total_frames, width = frames * wide, planes * cols
    here = rows // plane_count
    share = here // wide
    edge = BLOCK * frames
    rep, plane, spot = lax.axis_index("rep"), lax.axis_index("planes"), lax.axis_index("wide")
    mib = 1 << 20

    start = jnp.where(rep == 0, rows - BLOCK, 0)
    rim_rows = exchange(lax.dynamic_slice_in_dim(movie_frames, start, BLOCK, axis=2), "rep", 1)
    cuts = 2
    depth, names = 3 * BLOCK * frames, templates.shape[0]
    smooth, col_fwd, row_fwd, code, tall_templates, flat_templates = pl.pallas_call(
        functools.partial(prepare_kernel, rim, cuts),
        out_shape=(
            shaped((frames, rows + 2 * BLOCK, width)), shaped((cols, cols)), shaped((edge, depth)),
            jax.ShapeDtypeStruct(support.shape, jnp.int32), shaped((width, names)),
            shaped((names, width)),
        ),
        in_specs=[HBM] * 6,
        out_specs=(VMEM,) * 6,
        scratch_shapes=[
            pltpu.VMEM(movie_frames.shape, BF16),
            pltpu.VMEM(pixel_mask.shape, jnp.int32),
            pltpu.VMEM(support.shape, jnp.int32),
            pltpu.VMEM((names * planes, cols), BF16),
            pltpu.VMEM((names * planes, cols), F32),
            pltpu.SMEM(col_taps.shape, F32),
            pltpu.SMEM(row_taps.shape, F32),
            pltpu.SemaphoreType.DMA((5 + planes * cuts,)),
        ],
        compiler_params=pltpu.CompilerParams(vmem_limit_bytes=32 * mib),
        name="prepare",
    )(
        *[
            pltpu.with_memory_space_constraint(x, pltpu.HBM)
            for x in (
                col_taps, row_taps, movie_frames, pixel_mask, support,
                templates.reshape(names * planes, cols),
            )
        ]
    )

    near_ks, far_ks = list(range(wide // 2)), list(range(wide // 2, wide))
    halves = {1: far_ks, 0: near_ks[::-1]}
    half_rows = here // 2
    filtered, projected = {}, {}
    flips = [(turn + 1) % plane_count for turn in range(plane_count)]
    keys = [(flip, far) for far in (1, 0) for flip in flips]
    for turn, (flip, far) in enumerate(keys):
        smooth, filtered[flip, far], mine = call(
            functools.partial(forward_kernel, flip, far, turn == 0, wide, halves[far]), "forward",
            [smooth.shape, (half_rows * frames, width), (half_rows * frames, LANES)],
            0, 6, aliases={0: 0},
            scratch=[pltpu.VMEM((half_rows * frames, LANES), BF16)],
        )(smooth, rim_rows, col_fwd, row_fwd, code, tall_templates)
        projected[flip, far] = exchange(mine, "planes", flip) if flip else mine
        if turn == 0:
            gains, lags, _ = lax.optimization_barrier((lag_gains, dilations, smooth))
            kernel_row = lag_kernel_values(gains[0], lags[0], total_frames)
            lag_rows = -(-2 * total_frames // (LANES * BLOCK)) * BLOCK
            kernel_row = jnp.pad(kernel_row, (0, lag_rows * LANES - 2 * total_frames))
            kernel_row = kernel_row.reshape(lag_rows, LANES)

    block_rows = share * frames + lag_rows
    sums, blocks = {}, {}

    def parts_of(k):
        far = int(k in far_ks)
        spots = [halves[far].index(k)] * plane_count
        return spots, [projected[flip, far] for flip in range(plane_count)]

    for k in near_ks[1:] + far_ks:
        spots, parts = parts_of(k)
        (sums[k],) = call(
            functools.partial(sum_kernel, spots), "sum", [(block_rows, LANES)],
            0, 1 + plane_count,
        )(kernel_row, *parts)
        blocks[k] = exchange(sums[k], "wide", k)

    late_col, late_row, _ = lax.optimization_barrier(
        (col_taps, row_taps, list(sums.values()))
    )
    col_adj, row_adj = call(
        functools.partial(bands_kernel, rim, frames), "bands", [(width, width), (edge, depth)],
        2, 0,
    )(late_col, late_row)
    own_spots, own_parts = parts_of(0)
    own_parts[0], col_adj, row_adj = lax.optimization_barrier((own_parts[0], col_adj, row_adj))

    cell_shape = (wide, share, frames, LANES)
    traces = call(
        functools.partial(mix_kernel, wide, own_spots), "mix", [cell_shape[1:]] * wide,
        0, 1 + wide + plane_count,
        scratch=[
            pltpu.VMEM(cell_shape, BF16), pltpu.VMEM((wide, lag_rows, LANES), F32),
            pltpu.VMEM(cell_shape, BF16),
        ],
    )(
        tile_owner.reshape(1, rows), kernel_row, *own_parts, *[blocks[k] for k in range(1, wide)],
    )
    swapped = {k: exchange(traces[k], "wide", k) for k in far_ks + near_ks[1:]}
    swapped[0] = traces[0]
    late = range(1, plane_count)
    near = jnp.concatenate([swapped[k] for k in near_ks])
    passed = {flip: exchange(near, "planes", flip) for flip in late}

    residual, edges, ordered = {}, {}, {}
    back_keys = [(flip, far) for flip in range(plane_count) for far in (0, 1)]

    def subtract(flip, far, groups, got):
        spots = [(k, n, i) for n, ks in enumerate(groups) for i, k in enumerate(ks)]
        residual[flip, far], edges[flip, far], ordered[flip, far] = call(
            functools.partial(residual_kernel, flip, far, wide, spots), "residual",
            [(half_rows * frames, width), (edge, width), (half_rows, frames, LANES)],
            0, 3 + len(got), scratch=[pltpu.VMEM((len(spots), share * frames, names), BF16)],
        )(filtered[flip, far], code, flat_templates, *got)

    subtract(0, 0, [near_ks], [near])
    distant, _ = lax.optimization_barrier(([swapped[k] for k in far_ks], edges[0, 0]))
    joined = jnp.concatenate(distant)
    subtract(0, 1, [[k] for k in far_ks], distant)
    for flip in late:
        subtract(flip, 0, [near_ks], [passed[flip]])
        got, _ = lax.optimization_barrier((exchange(joined, "planes", flip), edges[flip, 0]))
        subtract(flip, 1, [far_ks], [got])

    def pick(table, part, half):
        found = table[0, 0]
        for flip, far in back_keys[1:]:
            here_it_is = ((plane ^ part) == flip) & ((spot // (wide // 2) ^ half) == far)
            found = jnp.where(here_it_is, table[flip, far], found)
        return found

    tip = pick(edges, jnp.where(rep == 0, plane_count - 1, 0), jnp.where(rep == 0, 1, 0))
    tip = exchange(tip, "rep", 1)

    foot_share = support.shape[1] // plane_count
    turned, body = pl.pallas_call(
        functools.partial(emit_kernel, back_keys, wide),
        out_shape=(shaped((foot_share, frames, rows)), shaped((rows * frames, width))),
        in_specs=[VMEM] * (2 * len(back_keys)),
        out_specs=(VMEM, VMEM),
        scratch_shapes=[
            pltpu.VMEM((rows * frames, LANES), F32),
            pltpu.VMEM((foot_share * frames, rows), F32),
        ],
        compiler_params=pltpu.CompilerParams(vmem_limit_bytes=32 * mib),
        name="emit",
    )(*[ordered[key] for key in back_keys], *[residual[key] for key in back_keys])

    back_projected, trace_out = pl.pallas_call(
        backward_kernel,
        out_shape=(shaped(movie_frames.shape), shaped(turned.shape)),
        in_specs=[VMEM] * 5,
        out_specs=(HBM, HBM),
        scratch_shapes=[
            pltpu.VMEM(movie_frames.shape, BF16),
            pltpu.SemaphoreType.DMA((rows // BLOCK + 1,)),
        ],
        compiler_params=pltpu.CompilerParams(vmem_limit_bytes=32 * mib),
        name="backward",
    )(turned, tip, col_adj, row_adj, body)
    return trace_out, back_projected


def solution(mesh):
    return jax.shard_map(
        on_device,
        mesh=mesh,
        in_specs=(
            P("planes", ("groups", "wide"), "rep", None),
            P("rep", None),
            P("rep", None),
            P("rep", None),
            P(None, "planes", None),
            P(),
            P(),
            P("wide", None, None),
            P("wide", None),
        ),
        out_specs=(
            P("planes", ("groups", "wide"), "rep"),
            P("planes", ("groups", "wide"), "rep", None),
        ),
        check_vma=False,
    )
```
